32 devices in a mesh: gx: 4 (over y, x), gy: 2 (over core), ga: 4 (over z).
Axes of the slice: x: 2, y: 2, z: 4, core: 2. Of those that a mesh axis runs over, the one named last changes fastest.
Arguments:
- mixture_fields_initial: float32 [16, 64, 64, 128], P(None, 'gx', ('gy', 'ga')), may hold values from 0 to 1
- flow_speed_vector: float32 [3, 64, 64, 128], P(None, 'gx', ('gy', 'ga')), may hold values from -2 to 2
- thermal_field: float32 [64, 64, 128], P('gx', ('gy', 'ga')), may hold values from 1 to 3
- mass_diffusivity: float32 [16], replicated, may hold values from 0.05 to 0.3
- arrhenius_constant: float32 [16], replicated, may hold values from 0.3 to 3
- arrhenius_energy_temp: float32 [16], replicated, may hold values from 0.5 to 4
- production_coefficients: float32 [16, 16], replicated, may hold values from -1.5 to 1.5
- tucker_factor_east: float32 [64, 64], P('gx'), may hold values from -1 to 1, as said below
- tucker_factor_north: float32 [64, 64], P(('gy', 'ga')), may hold values from -1 to 1, as said below
- tucker_factor_vertical: float32 [128, 32], replicated, may hold values from -1 to 1, as said below
- tucker_factor_component: float32 [16, 8], replicated, may hold values from -1 to 1, as said below
Outputs:
- mixture_fields_final: float32 [16, 64, 64, 128], P(None, 'gx', ('gy', 'ga'))
- residual: float32 [16, 64, 64, 128], P(None, 'gx', ('gy', 'ga'))
- tucker_core: float32 [8, 64, 64, 32], P(None, 'gx', ('gy', 'ga'))
The draws below stay inside these ranges and needn't reach their ends.
Inputs may be any that keep to these rules, and one draw needn't show every extreme that they name: tucker_factor_east has orthonormal columns. tucker_factor_north has orthonormal columns. tucker_factor_vertical has orthonormal columns. tucker_factor_component has orthonormal columns.
All inputs are finite; a program needn't handle non-finite values.
Results may differ from the reference program's by a relative error of at most 0.0001.
Values sent between devices are 32-bit elements; how exact they have to be, the bound alone decides.
No kernel may reach another device: no remote copies, remote signals or barrier semaphores. Data moves between devices by JAX's collectives and lax.ppermute only.
A program may use at most 64 MiB of HBM per device.

```python
import math
import jax
import jax.numpy as jnp
from jax import lax

S = 16
RS = 8
RX = 64
RY = 64
RZ = 32
GRID_LENGTH_UP = 128
SUB = 2
GRID_LENGTH_EAST = 64
GRID_LENGTH_NORTH = 64


def orthonormal(key, rows, columns):
    matrix = jax.random.normal(key, (rows, columns), jnp.float32)
    return jnp.linalg.qr(matrix)[0]


def draw_tucker_factor_east(key, part):
    return orthonormal(jax.random.fold_in(key, 11), GRID_LENGTH_EAST, RX)


def draw_tucker_factor_north(key, part):
    return orthonormal(jax.random.fold_in(key, 12), GRID_LENGTH_NORTH, RY)


def draw_tucker_factor_vertical(key, part):
    return orthonormal(jax.random.fold_in(key, 13), GRID_LENGTH_UP, RZ)


def draw_tucker_factor_component(key, part):
    return orthonormal(jax.random.fold_in(key, 14), S, RS)


def level_of(rng, shape, shards, low, top_value):
    loudness, own = 1.0, jax.random.fold_in(rng, 6)
    for axis_at, shards_of in shards:
        heights = jnp.exp(jax.random.uniform(jax.random.fold_in(own, axis_at), (shards_of,), jnp.float32, low / len(shards), top_value / len(shards)))
        loudness = loudness * jnp.repeat(heights, shape[axis_at] // shards_of).reshape([-1 if axis == axis_at else 1 for axis in range(len(shape))])
    return loudness


def centred(key, extent, spread, most, shards=(), kind=jnp.bfloat16):
    gain = level_of(key, extent, shards, -0.22, 0.18) if shards else 1.0
    entries = jax.random.normal(key, extent, jnp.float32) * spread * gain
    return jnp.minimum(jnp.maximum(entries, -most), most).astype(kind)


def setup_inputs(seed: int = 0) -> dict:
    splits = jax.random.split(jax.random.key(seed), 12)
    mixture_fields_initial = jnp.clip(1.0 * jax.random.uniform(splits[0], (S, GRID_LENGTH_EAST, GRID_LENGTH_NORTH, GRID_LENGTH_UP), jnp.float32) ** level_of(splits[0], (S, GRID_LENGTH_EAST, GRID_LENGTH_NORTH, GRID_LENGTH_UP), ((1, 4), (2, 8)), -0.2, 0.2), 0.0, 1.0)
    flow_speed_vector = centred(splits[1], (3, GRID_LENGTH_EAST, GRID_LENGTH_NORTH, GRID_LENGTH_UP), 0.5, 2.0, ((1, 4), (2, 8)), jnp.float32)
    thermal_field = jnp.clip(1.0 + 2.0 * jax.random.uniform(splits[2], (GRID_LENGTH_EAST, GRID_LENGTH_NORTH, GRID_LENGTH_UP), jnp.float32) ** level_of(splits[2], (GRID_LENGTH_EAST, GRID_LENGTH_NORTH, GRID_LENGTH_UP), ((0, 4), (1, 8)), -0.2, 0.2), 1.0, 3.0)
    mass_diffusivity = jnp.clip(jnp.exp(jax.random.uniform(splits[3], (S,), jnp.float32, math.log(0.05), math.log(0.3))), 0.05, 0.3)
    arrhenius_constant = jnp.clip(jnp.exp(jax.random.uniform(splits[4], (S,), jnp.float32, math.log(0.3), math.log(3.0))), 0.3, 3.0)
    arrhenius_energy_temp = jnp.clip(jnp.exp(jax.random.uniform(splits[5], (S,), jnp.float32, math.log(0.5), math.log(4.0))), 0.5, 4.0)
    production_coefficients = centred(splits[6], (S, S), S ** -0.5, 1.5, (), jnp.float32)
    tucker_factor_east = draw_tucker_factor_east(jax.random.fold_in(splits[11], 71), 0)
    tucker_factor_north = draw_tucker_factor_north(jax.random.fold_in(splits[11], 71), 0)
    tucker_factor_vertical = draw_tucker_factor_vertical(jax.random.fold_in(splits[11], 71), 0)
    tucker_factor_component = draw_tucker_factor_component(jax.random.fold_in(splits[11], 71), 0)
    return dict(mixture_fields_initial=mixture_fields_initial, flow_speed_vector=flow_speed_vector, thermal_field=thermal_field, mass_diffusivity=mass_diffusivity, arrhenius_constant=arrhenius_constant, arrhenius_energy_temp=arrhenius_energy_temp, production_coefficients=production_coefficients, tucker_factor_east=tucker_factor_east, tucker_factor_north=tucker_factor_north, tucker_factor_vertical=tucker_factor_vertical, tucker_factor_component=tucker_factor_component)


time_step = 0.5

def advance_solution(tensor_elements, flow_speed_vector, thermal_field, mass_diffusivity, arrhenius_constant, arrhenius_energy_temp, production_coefficients):
    padded = jnp.pad(tensor_elements, ((0, 0), (1, 1), (1, 1), (0, 0)))
    x_plus = padded[:, 2:, 1:-1, :]
    x_minus = padded[:, :-2, 1:-1, :]
    y_plus = padded[:, 1:-1, 2:, :]
    y_minus = padded[:, 1:-1, :-2, :]
    zero_layer = jnp.zeros_like(tensor_elements[..., :1])
    z_plus = jnp.concatenate([tensor_elements[..., 1:], zero_layer], axis=3)
    z_minus = jnp.concatenate([zero_layer, tensor_elements[..., :-1]], axis=3)
    laplace = x_plus + x_minus + y_plus + y_minus + z_plus + z_minus - 6.0 * tensor_elements
    advect = 0.5 * (flow_speed_vector[0] * (x_plus - x_minus) + flow_speed_vector[1] * (y_plus - y_minus) + flow_speed_vector[2] * (z_plus - z_minus))
    swap_neighbour_halo = jnp.concatenate([tensor_elements[1:], tensor_elements[:1]], axis=0)
    reaction_source_terms = arrhenius_constant[:, None, None, None] * jnp.exp(-arrhenius_energy_temp[:, None, None, None] / thermal_field) * tensor_elements * swap_neighbour_halo
    produced = jnp.einsum('sk,kxyz->sxyz', production_coefficients, reaction_source_terms, precision=lax.Precision.HIGHEST)
    return tensor_elements + time_step * (mass_diffusivity[:, None, None, None] * laplace - advect + produced)

def reference(mixture_fields_initial, flow_speed_vector, thermal_field, mass_diffusivity, arrhenius_constant, arrhenius_energy_temp, production_coefficients, tucker_factor_east, tucker_factor_north, tucker_factor_vertical, tucker_factor_component):
    highest = lax.Precision.HIGHEST
    mixture_snapshot_record = mixture_fields_initial
    for substep in range(SUB):
        mixture_snapshot_record = advance_solution(mixture_snapshot_record, flow_speed_vector, thermal_field, mass_diffusivity, arrhenius_constant, arrhenius_energy_temp, production_coefficients)
    projected = jnp.einsum('sxyz,sa->axyz', mixture_snapshot_record, tucker_factor_component, precision=highest)
    projected = jnp.einsum('axyz,zd->axyd', projected, tucker_factor_vertical, precision=highest)
    projected = jnp.einsum('axyd,yc->axcd', projected, tucker_factor_north, precision=highest)
    tucker_core = jnp.einsum('axcd,xb->abcd', projected, tucker_factor_east, precision=highest)
    expanded = jnp.einsum('abcd,xb->axcd', tucker_core, tucker_factor_east, precision=highest)
    expanded = jnp.einsum('axcd,yc->axyd', expanded, tucker_factor_north, precision=highest)
    expanded = jnp.einsum('axyd,zd->axyz', expanded, tucker_factor_vertical, precision=highest)
    expanded = jnp.einsum('axyz,sa->sxyz', expanded, tucker_factor_component, precision=highest)
    residual = mixture_snapshot_record - expanded
    mixture_fields_final = mixture_snapshot_record
    for substep in range(SUB):
        mixture_fields_final = advance_solution(mixture_fields_final, flow_speed_vector, thermal_field, mass_diffusivity, arrhenius_constant, arrhenius_energy_temp, production_coefficients)
    return (mixture_fields_final, residual, tucker_core)
```

```python
import jax
import jax.numpy as jnp
from jax import lax
from jax.sharding import PartitionSpec as P

SUB = 2


time_step = 0.5

ROW = "gx"
COLUMN = ("gy", "ga")
EVERY = ("gx", "gy", "ga")


def faces_beside(low_face, high_face, axes):
    count = lax.axis_size(axes)
    even = lax.axis_index(axes) % 2 == 0

    def swapped(face, first):
        couples = [(i, i + 1) for i in range(first, count - 1, 2)]
        return lax.ppermute(face, axes, couples + [(b, a) for a, b in couples])

    one = swapped(jnp.where(even, high_face, low_face), 0)
    other = swapped(jnp.where(even, low_face, high_face), 1)
    return jnp.where(even, other, one), jnp.where(even, one, other)


def advance_solution(
    tensor_elements,
    flow_speed_vector,
    thermal_field,
    mass_diffusivity,
    arrhenius_constant,
    arrhenius_energy_temp,
    production_coefficients,
):
    y_before, y_after = faces_beside(
        tensor_elements[:, :, :1], tensor_elements[:, :, -1:], COLUMN
    )
    x_before, x_after = faces_beside(tensor_elements[:, :1], tensor_elements[:, -1:], ROW)
    x_plus = jnp.concatenate([tensor_elements[:, 1:], x_after], axis=1)
    x_minus = jnp.concatenate([x_before, tensor_elements[:, :-1]], axis=1)
    y_plus = jnp.concatenate([tensor_elements[:, :, 1:], y_after], axis=2)
    y_minus = jnp.concatenate([y_before, tensor_elements[:, :, :-1]], axis=2)
    zero_layer = jnp.zeros_like(tensor_elements[..., :1])
    z_plus = jnp.concatenate([tensor_elements[..., 1:], zero_layer], axis=3)
    z_minus = jnp.concatenate([zero_layer, tensor_elements[..., :-1]], axis=3)
    laplace = x_plus + x_minus + y_plus + y_minus + z_plus + z_minus - 6.0 * tensor_elements
    advect = 0.5 * (
        flow_speed_vector[0] * (x_plus - x_minus)
        + flow_speed_vector[1] * (y_plus - y_minus)
        + flow_speed_vector[2] * (z_plus - z_minus)
    )
    swap_neighbour_halo = jnp.concatenate([tensor_elements[1:], tensor_elements[:1]], axis=0)
    reaction_source_terms = (
        arrhenius_constant[:, None, None, None]
        * jnp.exp(-arrhenius_energy_temp[:, None, None, None] / thermal_field)
        * tensor_elements
        * swap_neighbour_halo
    )
    produced = jnp.einsum(
        "sk,kxyz->sxyz",
        production_coefficients,
        reaction_source_terms,
        precision=lax.Precision.HIGHEST,
    )
    return tensor_elements + time_step * (
        mass_diffusivity[:, None, None, None] * laplace - advect + produced
    )


def whole_factors(tucker_factor_east, tucker_factor_north):
    rows, columns = lax.axis_size(ROW), lax.axis_size(COLUMN)

    def shares(factor, holders, axes):
        count = -(-factor.shape[0] // holders)
        padded = jnp.pad(factor, ((0, count * holders - factor.shape[0]), (0, 0)))
        return lax.dynamic_slice_in_dim(padded, lax.axis_index(axes) * count, count, 0)

    east = shares(tucker_factor_east, columns, COLUMN)
    north = shares(tucker_factor_north, rows, ROW)
    sent = jnp.concatenate([east.reshape(-1), north.reshape(-1)])
    sent = jnp.pad(sent, (0, -sent.size % 128)).reshape(1, -1, 128)
    sent = jnp.broadcast_to(sent, (rows * columns,) + sent.shape[1:])
    got = lax.all_to_all(sent, EVERY, 0, 0, tiled=True).reshape(rows, columns, -1)
    whole_east = got[:, :, : east.size].reshape(rows, -1, east.shape[1])
    whole_east = whole_east[:, : tucker_factor_east.shape[0]].reshape(-1, east.shape[1])
    whole_north = got[:, :, east.size : east.size + north.size]
    whole_north = whole_north.reshape(rows, columns, *north.shape).transpose(1, 0, 2, 3)
    whole_north = whole_north.reshape(columns, -1, north.shape[1])
    whole_north = whole_north[:, : tucker_factor_north.shape[0]].reshape(-1, north.shape[1])
    return whole_east, whole_north


def compress_and_expand(
    snapshot,
    east,
    north,
    tucker_factor_vertical,
    tucker_factor_component,
):
    highest = lax.Precision.HIGHEST
    rows, columns = lax.axis_size(ROW), lax.axis_size(COLUMN)
    devices = rows * columns
    (_, wide, deep, _), (_, ranks_a) = snapshot.shape, tucker_factor_component.shape
    ranks_d = tucker_factor_vertical.shape[1]
    ranks_b, ranks_c = east.shape[1], north.shape[1]
    projected = jnp.einsum("sxyz,sa->axyz", snapshot, tucker_factor_component, precision=highest)
    projected = jnp.einsum("axyz,zd->dyxa", projected, tucker_factor_vertical, precision=highest)
    pairs = ranks_a * ranks_d
    share = -(-pairs // devices)
    flat = jnp.transpose(projected, (0, 3, 1, 2)).reshape(pairs, deep, wide)
    flat = jnp.pad(flat, ((0, share * devices - pairs), (0, 0), (0, 0)))
    flat = flat.reshape(devices, share, deep, wide).transpose(0, 2, 3, 1)
    flat = lax.all_to_all(
        flat.reshape(devices, deep, wide * share), EVERY, 0, 0, tiled=True
    )
    whole = flat.reshape(rows, columns * deep, wide, share)
    part = jnp.einsum("gyxp,yc->cgxp", whole, north, precision=highest)
    part = part.reshape(ranks_c, rows * wide, share)
    core = jnp.einsum("cxp,xb->cbp", part, east, precision=highest)
    part = jnp.einsum("cbp,xb->cxp", core, east, precision=highest)
    whole = jnp.einsum("cxp,yc->yxp", part, north, precision=highest)
    own_b, own_c = ranks_b // rows, ranks_c // columns

    def pieces(array, tall, broad):
        array = array.reshape(columns, tall, rows, broad, share)
        return array.transpose(2, 0, 1, 3, 4).reshape(devices, tall * broad * share)

    sent = jnp.concatenate([pieces(core, own_c, own_b), pieces(whole, deep, wide)], axis=1)
    sent = jnp.pad(sent, ((0, 0), (0, -sent.shape[1] % 1024)))
    got = lax.all_to_all(
        sent.reshape(devices, -1, 128), EVERY, 0, 0, tiled=True
    ).reshape(devices, -1)

    def ranks_together(array, tall, broad):
        array = array.reshape(devices, tall, broad, share).transpose(0, 3, 2, 1)
        array = array.reshape(devices * share, broad, tall)[:pairs]
        return array.reshape(ranks_d, ranks_a, broad, tall)

    core_size = own_c * own_b * share
    core = ranks_together(got[:, :core_size], own_c, own_b).transpose(1, 2, 3, 0)
    expanded = ranks_together(got[:, core_size : core_size + deep * wide * share], deep, wide)
    expanded = jnp.einsum("daxy,zd->axyz", expanded, tucker_factor_vertical, precision=highest)
    expanded = jnp.einsum("axyz,sa->sxyz", expanded, tucker_factor_component, precision=highest)
    return core, snapshot - expanded


def body(
    mixture_fields_initial,
    flow_speed_vector,
    thermal_field,
    mass_diffusivity,
    arrhenius_constant,
    arrhenius_energy_temp,
    production_coefficients,
    tucker_factor_east,
    tucker_factor_north,
    tucker_factor_vertical,
    tucker_factor_component,
):
    chemistry = (
        flow_speed_vector,
        thermal_field,
        mass_diffusivity,
        arrhenius_constant,
        arrhenius_energy_temp,
        production_coefficients,
    )
    east, north = whole_factors(tucker_factor_east, tucker_factor_north)
    snapshot = mixture_fields_initial
    for substep in range(SUB):
        snapshot = advance_solution(snapshot, *chemistry)
    tucker_core, residual = compress_and_expand(
        snapshot,
        east,
        north,
        tucker_factor_vertical,
        tucker_factor_component,
    )
    mixture_fields_final = snapshot
    for substep in range(SUB):
        mixture_fields_final = advance_solution(mixture_fields_final, *chemistry)
    return (mixture_fields_final, residual, tucker_core)


def solution(mesh):
    in_specs = (
        P(None, "gx", ("gy", "ga"), None),
        P(None, "gx", ("gy", "ga"), None),
        P("gx", ("gy", "ga"), None),
        P(),
        P(),
        P(),
        P(),
        P("gx", None),
        P(("gy", "ga"), None),
        P(),
        P(),
    )
    out_specs = (
        P(None, "gx", ("gy", "ga"), None),
        P(None, "gx", ("gy", "ga"), None),
        P(None, "gx", ("gy", "ga"), None),
    )
    return jax.shard_map(body, mesh=mesh, in_specs=in_specs, out_specs=out_specs, check_vma=False)
```

```python
import functools

import jax
import jax.numpy as jnp
from jax import lax
from jax.experimental import pallas as pl
from jax.experimental.pallas import tpu as pltpu
from jax.sharding import PartitionSpec as P

SUB = 2


time_step = 0.5

ROW = "gx"
COLUMN = ("gy", "ga")
EVERY = ("gx", "gy", "ga")
HIGHEST = lax.Precision.HIGHEST
HIGH = lax.Precision.HIGH
VMEM_LIMIT = 8 * 1024 * 1024


def vmem_call(kernel, outs, in_smem, n_in, flops=0, moved=0, exps=0, scratch=()):
    vmem = pl.BlockSpec(memory_space=pltpu.VMEM)
    smem = pl.BlockSpec(memory_space=pltpu.SMEM)
    return pl.pallas_call(
        kernel,
        in_specs=[smem] * in_smem + [vmem] * (n_in - in_smem),
        out_specs=[vmem] * len(outs),
        out_shape=[jax.ShapeDtypeStruct(shape, jnp.float32) for shape in outs],
        scratch_shapes=[pltpu.VMEM(shape, jnp.float32) for shape in scratch],
        compiler_params=pltpu.CompilerParams(vmem_limit_bytes=VMEM_LIMIT),
        cost_estimate=pl.CostEstimate(flops=flops, bytes_accessed=moved, transcendentals=exps),
    )


def planes_of_species(ref, species, plane, at):
    return jnp.concatenate(
        [ref[pl.ds(first * plane + at, 8, stride=plane), :] for first in range(0, species, 8)], axis=0
    )


def store_planes_of_species(ref, species, plane, at, value):
    for first in range(0, species, 8):
        ref[pl.ds(first * plane + at, 8, stride=plane), :] = value[first : first + 8]


def faces_kernel(shape, even_ref, rows_ref, x_one, x_other, y_one, y_other):
    wide, deep, species, _ = shape
    even_x, even_y = even_ref[0] == 1, even_ref[1] == 1
    plane = wide * deep
    for y in range(deep):
        low = planes_of_species(rows_ref, species, plane, y)
        high = planes_of_species(rows_ref, species, plane, (wide - 1) * deep + y)
        x_one[y] = jnp.where(even_x, high, low)
        x_other[y] = jnp.where(even_x, low, high)
    for x in range(wide):
        low = planes_of_species(rows_ref, species, plane, x * deep)
        high = planes_of_species(rows_ref, species, plane, x * deep + deep - 1)
        y_one[x] = jnp.where(even_y, high, low)
        y_other[x] = jnp.where(even_y, low, high)


def prepare_kernel(shape, given, thermal_ref, constant_ref, energy_ref, field, rates):
    wide, deep, species, up = shape
    constant = jnp.broadcast_to(constant_ref[...], (species, up))
    energy = jnp.broadcast_to(energy_ref[...], (species, up))
    for x in range(wide):
        inverse = -1.0 / thermal_ref[x]
        field[x] = jnp.swapaxes(given[:, x], 0, 1)
        for y in range(deep):
            rates[x, y] = constant * jnp.exp(energy * inverse[y : y + 1])


def blocks_on_diagonal(matrix, count):
    high, wide = matrix.shape
    tall, broad = count * high, count * wide

    def picks(rows, size):
        row = lax.broadcasted_iota(jnp.int32, (rows, size), 0) % size
        return (row == lax.broadcasted_iota(jnp.int32, (rows, size), 1)).astype(jnp.float32)

    full = jnp.dot(picks(tall, high), matrix, precision=HIGHEST, preferred_element_type=jnp.float32)
    full = lax.dot_general(
        full, picks(broad, wide), (((1,), (1,)), ((), ())), precision=HIGHEST,
        preferred_element_type=jnp.float32,
    )
    row = lax.broadcasted_iota(jnp.int32, (tall, broad), 0) // high
    column = lax.broadcasted_iota(jnp.int32, (tall, broad), 1) // wide
    return jnp.where(row == column, full, 0.0)


def matrices_kernel(
    together, wide, own_ref, production, component, component_turned, east, north,
    mix, squeeze, widen, factor_rows,
):
    mix[...] = blocks_on_diagonal(time_step * production[...], together)
    squeeze[...] = blocks_on_diagonal(component_turned[...], wide)
    widen[...] = blocks_on_diagonal(component[...], wide)

    def two_rows(ref, at):
        return jnp.concatenate([ref[pl.ds(2 * at + row, 1), :] for row in range(2)], axis=1)

    if factor_rows is not None:
        factor_rows[0:1] = two_rows(east, own_ref[3])
        factor_rows[1:2] = two_rows(north, own_ref[2])


def _without_rows(kernel, *refs):
    kernel(*refs, None)


def step(shape, refs, emit):
    wide, deep, species, up = shape
    even_ref, field, x_one, x_other, y_one, y_other, rates, flow, diffusivity_ref, mix_ref = refs
    even_x, even_y = even_ref[0] == 1, even_ref[1] == 1
    diffusivity = jnp.broadcast_to(diffusivity_ref[...] * time_step, (species, up))
    mix = mix_ref[...]
    lane = lax.broadcasted_iota(jnp.int32, (deep, species, up), 2)
    first, last = lane == 0, lane == up - 1
    together = 4 if wide % 4 == 0 else 1
    half = max(together // 2, 1)
    x_before = jnp.where(even_x, x_other[...], x_one[...])
    x_after = jnp.where(even_x, x_one[...], x_other[...])
    for x0 in range(0, wide, together):
        made = []
        for x in range(x0, x0 + together):
            here = field[x]
            ahead = pltpu.roll(here.reshape(deep, species, up), species - 1, 1)
            made.append((rates[x] * here * ahead).reshape(deep * species, up))
        if together == 4:
            right = jnp.concatenate(
                [jnp.concatenate(made[:2], axis=0), jnp.concatenate(made[2:], axis=0)], axis=1
            )
        else:
            right = made[0]
        produced = jnp.dot(mix, right, precision=HIGH, preferred_element_type=jnp.float32)
        for x in range(x0, x0 + together):
            here = field[x]
            x_minus = field[x - 1] if x > 0 else x_before
            x_plus = field[x + 1] if x < wide - 1 else x_after
            before = jnp.where(even_y, y_other[x], y_one[x])
            after = jnp.where(even_y, y_one[x], y_other[x])
            y_minus = jnp.concatenate([before[None], here[:-1]], axis=0)
            y_plus = jnp.concatenate([here[1:], after[None]], axis=0)
            z_minus = jnp.where(first, 0.0, pltpu.roll(here, 1, 2))
            z_plus = jnp.where(last, 0.0, pltpu.roll(here, up - 1, 2))

            def speed(d):
                return jnp.stack(
                    [jnp.broadcast_to(flow[d, x, pl.ds(y, 1), :], (species, up)) for y in range(deep)]
                )

            laplace = (x_plus + x_minus) + (y_plus + y_minus) + (z_plus + z_minus) - 6.0 * here
            advect = (
                speed(0) * (x_plus - x_minus)
                + speed(1) * (y_plus - y_minus)
                + speed(2) * (z_plus - z_minus)
            )
            part = (x - x0) % half if together == 4 else 0
            group = (x - x0) // half if together == 4 else 0
            size = deep * species
            reacted = produced[part * size : (part + 1) * size, group * up : (group + 1) * up]
            emit(
                x,
                here
                + diffusivity[None] * laplace
                - (0.5 * time_step) * advect
                + reacted.reshape(deep, species, up),
            )


def emit_faces(shape, even_ref, x, plane, x_one, x_other, y_one, y_other):
    wide, deep, _, _ = shape
    even_x, even_y = even_ref[0] == 1, even_ref[1] == 1
    low, high = plane[0], plane[deep - 1]
    y_one[x] = jnp.where(even_y, high, low)
    y_other[x] = jnp.where(even_y, low, high)
    if x == 0:
        @pl.when(even_x)
        def _():
            x_other[...] = plane

        @pl.when(jnp.logical_not(even_x))
        def _():
            x_one[...] = plane
    if x == wide - 1:
        @pl.when(even_x)
        def _():
            x_one[...] = plane

        @pl.when(jnp.logical_not(even_x))
        def _():
            x_other[...] = plane


def advance_kernel(shape, *refs):
    even_ref, (out, x_one, x_other, y_one, y_other) = refs[0], refs[10:]

    def emit(x, plane):
        out[x] = plane
        emit_faces(shape, even_ref, x, plane, x_one, x_other, y_one, y_other)

    step(shape, refs[:10], emit)


def final_kernel(shape, *refs):
    out = refs[10]

    def emit(x, plane):
        out[:, x] = jnp.swapaxes(plane, 0, 1)

    step(shape, refs[:10], emit)


def project_kernel(shape, ranks, field, component, vertical, factor_rows, out):
    wide, deep, species, up = shape
    ranks_a, ranks_d = ranks
    each = deep + 2
    for y in range(deep):
        rows = field[:, y].reshape(wide * species, up)
        on_a = jnp.dot(component[...], rows, precision=HIGHEST, preferred_element_type=jnp.float32)
        on_d = lax.dot_general(
            vertical[...], on_a, (((1,), (1,)), ((), ())), precision=HIGHEST,
            preferred_element_type=jnp.float32,
        )
        out[pl.ds(y, ranks_d, stride=each), :] = on_d
    for row in range(2):
        out[pl.ds(deep + row, ranks_d, stride=each), :] = jnp.broadcast_to(
            factor_rows[row : row + 1], (ranks_d, 128)
        )


def core_kernel(counts, got, out):
    rows, columns, ranks_a, tall, deep = counts
    devices, each = rows * columns, deep + 2
    whole = jnp.concatenate(
        [
            jnp.concatenate(
                [got[pl.ds((row * columns + column) * each, deep), :] for column in range(columns)],
                axis=0,
            )
            for row in range(rows)
        ],
        axis=1,
    )

    def halves(at):
        both = got[pl.ds(at, devices, stride=each), :]
        return jnp.concatenate([both[:, :64], both[:, 64:]], axis=0)

    def is_at(shape, row_place, column_place):
        row = lax.broadcasted_iota(jnp.int32, shape, 0)
        column = lax.broadcasted_iota(jnp.int32, shape, 1)
        return row_place(row) == column_place(column)

    def dot(a, b, contract, precision=HIGH):
        return lax.dot_general(
            a, b, ((contract[:1], contract[1:]), ((), ())), precision=precision,
            preferred_element_type=jnp.float32,
        )

    high = 2 * devices
    broad = high * ranks_a
    own = 128 // ranks_a

    def of_east(at):
        x = at // ranks_a
        return (x % 2) * devices + x // 2

    def column_b(at):
        return at // 128 * own + at % own

    def column_a(at):
        return at // own % ranks_a

    def same(at):
        return at

    pick = is_at((broad, high), of_east, same).astype(jnp.float32)
    east = dot(pick, halves(deep), (1, 0))
    widen = is_at((high, broad), same, column_b).astype(jnp.float32)
    east = dot(east, widen, (1, 0))
    east = jnp.where(is_at((broad, broad), lambda at: at % ranks_a, column_a), east, 0.0)

    def of_north(at):
        column, row = at // deep, at % deep // 2
        return (at % 2) * devices + row * columns + column

    pick = is_at((high, high), of_north, same).astype(jnp.float32)
    north = dot(pick, halves(deep + 1), (1, 0), HIGHEST)

    half = dot(north, whole, (0, 0))
    core = dot(half, east, (1, 0))
    half = dot(core, east, (1, 1))
    whole = dot(north, half, (1, 0))
    for row in range(rows):
        for column in range(columns):
            at = row * columns + column
            out[at, 0:tall] = core[column * tall : (column + 1) * tall, row * 128 : (row + 1) * 128]
            out[at, tall : tall + deep] = whole[
                column * deep : (column + 1) * deep, row * 128 : (row + 1) * 128
            ]


def expand_kernel(shape, ranks, tall, got, field, component, vertical, residual, core, full):
    wide, deep, species, up = shape
    ranks_a, ranks_d = ranks
    each = tall + deep
    for y in range(deep):
        on_d = got[pl.ds(tall + y, ranks_d, stride=each), :]
        on_a = lax.dot_general(
            on_d, vertical[...], (((0,), (0,)), ((), ())), precision=HIGH,
            preferred_element_type=jnp.float32,
        )
        full[y] = jnp.dot(component[...], on_a, precision=HIGH, preferred_element_type=jnp.float32)
    for x in range(wide):
        residual[:, x] = jnp.swapaxes(
            field[x] - full[:, x * species : (x + 1) * species, :], 0, 1
        )
    turned = [got[pl.ds(c, ranks_d, stride=each), :].T for c in range(tall)]
    core[...] = jnp.swapaxes(jnp.stack(turned), 0, 1)


def faces_beside(faces):
    def swapped(face, axes, first):
        couples = [(i, i + 1) for i in range(first, lax.axis_size(axes) - 1, 2)]
        return lax.ppermute(face, axes, couples + [(b, a) for a, b in couples])

    x_one, x_other, y_one, y_other = faces
    y_one, y_other = swapped(y_one, COLUMN, 0), swapped(y_other, COLUMN, 1)
    x_one, x_other = swapped(x_one, ROW, 0), swapped(x_other, ROW, 1)
    return x_one, x_other, y_one, y_other


def whole_factors(tucker_factor_east, tucker_factor_north):
    rows, columns = lax.axis_size(ROW), lax.axis_size(COLUMN)

    def shares(factor, holders, axes):
        count = -(-factor.shape[0] // holders)
        padded = jnp.pad(factor, ((0, count * holders - factor.shape[0]), (0, 0)))
        return lax.dynamic_slice_in_dim(padded, lax.axis_index(axes) * count, count, 0)

    east = shares(tucker_factor_east, columns, COLUMN)
    north = shares(tucker_factor_north, rows, ROW)
    sent = jnp.concatenate([east.reshape(-1), north.reshape(-1)])
    sent = jnp.pad(sent, (0, -sent.size % 128)).reshape(1, -1, 128)
    sent = jnp.broadcast_to(sent, (rows * columns,) + sent.shape[1:])
    got = lax.all_to_all(sent, EVERY, 0, 0, tiled=True).reshape(rows, columns, -1)
    whole_east = got[:, :, : east.size].reshape(rows, -1, east.shape[1])
    whole_east = whole_east[:, : tucker_factor_east.shape[0]].reshape(-1, east.shape[1])
    whole_north = got[:, :, east.size : east.size + north.size]
    whole_north = whole_north.reshape(rows, columns, *north.shape).transpose(1, 0, 2, 3)
    whole_north = whole_north.reshape(columns, -1, north.shape[1])
    whole_north = whole_north[:, : tucker_factor_north.shape[0]].reshape(-1, north.shape[1])
    return whole_east, whole_north


def compress_and_expand(snapshot, east, north, vertical, component):
    rows, columns = lax.axis_size(ROW), lax.axis_size(COLUMN)
    devices = rows * columns
    (wide, deep, _, _), (_, ranks_a) = snapshot.shape, component.shape
    ranks_d = vertical.shape[1]
    ranks_b, ranks_c = east.shape[1], north.shape[1]
    projected = jnp.einsum("xysz,sa->xyaz", snapshot, component, precision=HIGHEST)
    projected = jnp.einsum("xyaz,zd->dyxa", projected, vertical, precision=HIGHEST)
    pairs = ranks_a * ranks_d
    share = -(-pairs // devices)
    flat = jnp.transpose(projected, (0, 3, 1, 2)).reshape(pairs, deep, wide)
    flat = jnp.pad(flat, ((0, share * devices - pairs), (0, 0), (0, 0)))
    flat = flat.reshape(devices, share, deep, wide).transpose(0, 2, 3, 1)
    flat = lax.all_to_all(
        flat.reshape(devices, deep, wide * share), EVERY, 0, 0, tiled=True
    )
    whole = flat.reshape(rows, columns * deep, wide, share)
    part = jnp.einsum("gyxp,yc->cgxp", whole, north, precision=HIGHEST)
    part = part.reshape(ranks_c, rows * wide, share)
    core = jnp.einsum("cxp,xb->cbp", part, east, precision=HIGHEST)
    part = jnp.einsum("cbp,xb->cxp", core, east, precision=HIGHEST)
    whole = jnp.einsum("cxp,yc->yxp", part, north, precision=HIGHEST)
    own_b, own_c = ranks_b // rows, ranks_c // columns

    def pieces(array, tall, broad):
        array = array.reshape(columns, tall, rows, broad, share)
        return array.transpose(2, 0, 1, 3, 4).reshape(devices, tall * broad * share)

    sent = jnp.concatenate([pieces(core, own_c, own_b), pieces(whole, deep, wide)], axis=1)
    sent = jnp.pad(sent, ((0, 0), (0, -sent.shape[1] % 1024)))
    got = lax.all_to_all(
        sent.reshape(devices, -1, 128), EVERY, 0, 0, tiled=True
    ).reshape(devices, -1)

    def ranks_together(array, tall, broad):
        array = array.reshape(devices, tall, broad, share).transpose(0, 3, 2, 1)
        array = array.reshape(devices * share, broad, tall)[:pairs]
        return array.reshape(ranks_d, ranks_a, broad, tall)

    core_size = own_c * own_b * share
    core = ranks_together(got[:, :core_size], own_c, own_b).transpose(1, 2, 3, 0)
    expanded = ranks_together(got[:, core_size : core_size + deep * wide * share], deep, wide)
    expanded = jnp.einsum("daxy,zd->axyz", expanded, vertical, precision=HIGHEST)
    expanded = jnp.einsum("axyz,sa->sxyz", expanded, component, precision=HIGHEST)
    return core, snapshot.transpose(2, 0, 1, 3) - expanded


def body(
    mixture_fields_initial,
    flow_speed_vector,
    thermal_field,
    mass_diffusivity,
    arrhenius_constant,
    arrhenius_energy_temp,
    production_coefficients,
    tucker_factor_east,
    tucker_factor_north,
    tucker_factor_vertical,
    tucker_factor_component,
):
    species, wide, deep, up = mixture_fields_initial.shape
    shape = (wide, deep, species, up)
    cells = wide * deep * species * up
    rows, columns = lax.axis_size(ROW), lax.axis_size(COLUMN)
    devices = rows * columns
    ranks_a, ranks_d = tucker_factor_component.shape[1], tucker_factor_vertical.shape[1]
    ranks_b, ranks_c = tucker_factor_east.shape[1], tucker_factor_north.shape[1]
    own_b, own_c = ranks_b // rows, ranks_c // columns
    kernels_fit = (
        ranks_d == devices
        and wide * ranks_a == 128
        and own_b * ranks_a == 128
        and deep == own_c == 8
        and ranks_b == ranks_c == 64
        and wide == 2 * columns
        and deep == 2 * rows
    )

    row, column = lax.axis_index(ROW), lax.axis_index(COLUMN)
    own = jnp.stack([1 - row % 2, 1 - column % 2, row, column]).astype(jnp.int32)
    face_shapes = [(deep, species, up)] * 2 + [(wide, species, up)] * 2
    field_rows = mixture_fields_initial.reshape(species * wide * deep, up)
    faces = vmem_call(functools.partial(faces_kernel, shape), face_shapes, 1, 2)(own, field_rows)
    faces = faces_beside(faces)
    field, rates = vmem_call(
        functools.partial(prepare_kernel, shape), [shape, shape], 0, 4,
        flops=4 * cells, moved=12 * cells, exps=cells,
    )(
        mixture_fields_initial,
        thermal_field,
        arrhenius_constant[:, None],
        arrhenius_energy_temp[:, None],
    )
    together = 2 if wide % 4 == 0 else 1
    both = together * deep
    matrices = functools.partial(matrices_kernel, both, wide)
    matrix_shapes = [
        (both * species,) * 2, (wide * ranks_a, wide * species), (wide * species, wide * ranks_a)
    ]
    if kernels_fit:
        matrix_shapes.append((2, 128))
    else:
        matrices = functools.partial(_without_rows, matrices)
    mix, squeeze, widen, *factor_rows = vmem_call(
        matrices, matrix_shapes, 1, 6, flops=cells, moved=cells,
    )(
        own,
        production_coefficients,
        tucker_factor_component,
        tucker_factor_component.T,
        tucker_factor_east,
        tucker_factor_north,
    )
    fixed = (rates, flow_speed_vector, mass_diffusivity[:, None], mix)
    advance = vmem_call(
        functools.partial(advance_kernel, shape), [shape] + face_shapes, 1, 10,
        flops=60 * cells, moved=8 * cells,
    )
    final = vmem_call(
        functools.partial(final_kernel, shape), [mixture_fields_initial.shape], 1, 10,
        flops=60 * cells, moved=8 * cells,
    )
    for substep in range(SUB):
        if substep:
            faces = faces_beside(faces)
        field, *faces = advance(own, field, *faces, *fixed)
    snapshot = field

    if kernels_fit:
        (sent,) = vmem_call(
            functools.partial(project_kernel, shape, (ranks_a, ranks_d)),
            [(devices * (deep + 2), 128)], 0, 4, flops=60 * cells, moved=4 * cells,
        )(snapshot, squeeze, tucker_factor_vertical.T, *factor_rows)
        got = lax.all_to_all(
            sent.reshape(devices, (deep + 2) // 2, 2, 128), EVERY, 0, 0, tiled=True
        )
        for substep in range(SUB - 1):
            faces = faces_beside(faces)
            field, *faces = advance(own, field, *faces, *fixed)
        got, field = lax.optimization_barrier((got, field))
        (sent,) = vmem_call(
            functools.partial(core_kernel, (rows, columns, ranks_a, own_c, deep)),
            [(devices, own_c + deep, 128)], 0, 1, flops=60 * cells, moved=4 * cells,
        )(got.reshape(devices * (deep + 2), 128))
        got = lax.all_to_all(sent, EVERY, 0, 0, tiled=True)
    else:
        east, north = whole_factors(tucker_factor_east, tucker_factor_north)
        tucker_core, residual = compress_and_expand(
            snapshot, east, north, tucker_factor_vertical, tucker_factor_component
        )
        for substep in range(SUB - 1):
            faces = faces_beside(faces)
            field, *faces = advance(own, field, *faces, *fixed)
    faces = faces_beside(faces)
    (mixture_fields_final,) = final(own, field, *faces, *fixed)
    if kernels_fit:
        residual, tucker_core = vmem_call(
            functools.partial(expand_kernel, shape, (ranks_a, ranks_d), own_c),
            [mixture_fields_initial.shape, (ranks_a * own_b, own_c, ranks_d)], 0, 4,
            flops=60 * cells, moved=8 * cells, scratch=[(deep, wide * species, up)],
        )(
            got.reshape(devices * (own_c + deep), 128),
            snapshot,
            widen,
            tucker_factor_vertical.T,
        )
        tucker_core = tucker_core.reshape(ranks_a, own_b, own_c, ranks_d)
    return (mixture_fields_final, residual, tucker_core)


def solution(mesh):
    in_specs = (
        P(None, "gx", ("gy", "ga"), None),
        P(None, "gx", ("gy", "ga"), None),
        P("gx", ("gy", "ga"), None),
        P(),
        P(),
        P(),
        P(),
        P("gx", None),
        P(("gy", "ga"), None),
        P(),
        P(),
    )
    out_specs = (
        P(None, "gx", ("gy", "ga"), None),
        P(None, "gx", ("gy", "ga"), None),
        P(None, "gx", ("gy", "ga"), None),
    )
    return jax.shard_map(body, mesh=mesh, in_specs=in_specs, out_specs=out_specs, check_vma=False)
```

```python
import functools

import jax
import jax.numpy as jnp
from jax import lax
from jax.experimental import pallas as pl
from jax.experimental.pallas import tpu as pltpu
from jax.sharding import PartitionSpec as P

SUB = 2


time_step = 0.5

ROW = "gx"
COLUMN = ("gy", "ga")
EVERY = ("gx", "gy", "ga")
HIGHEST = lax.Precision.HIGHEST
HIGH = lax.Precision.HIGH
VMEM_LIMIT = 8 * 1024 * 1024


def vmem_call(kernel, outs, in_smem, n_in, flops=0, moved=0, exps=0, scratch=()):
    vmem = pl.BlockSpec(memory_space=pltpu.VMEM)
    smem = pl.BlockSpec(memory_space=pltpu.SMEM)
    return pl.pallas_call(
        kernel,
        in_specs=[smem] * in_smem + [vmem] * (n_in - in_smem),
        out_specs=[vmem] * len(outs),
        out_shape=[jax.ShapeDtypeStruct(shape, jnp.float32) for shape in outs],
        scratch_shapes=[pltpu.VMEM(shape, jnp.float32) for shape in scratch],
        compiler_params=pltpu.CompilerParams(vmem_limit_bytes=VMEM_LIMIT),
        cost_estimate=pl.CostEstimate(flops=flops, bytes_accessed=moved, transcendentals=exps),
    )


def planes_of_species(ref, species, plane, at):
    return jnp.concatenate(
        [ref[pl.ds(first * plane + at, 8, stride=plane), :] for first in range(0, species, 8)], axis=0
    )


def store_planes_of_species(ref, species, plane, at, value):
    for first in range(0, species, 8):
        ref[pl.ds(first * plane + at, 8, stride=plane), :] = value[first : first + 8]


def faces_kernel(shape, even_ref, rows_ref, x_one, x_other, y_one, y_other):
    wide, deep, species, _ = shape
    even_x, even_y = even_ref[0] == 1, even_ref[1] == 1
    plane = wide * deep
    for y in range(deep):
        low = planes_of_species(rows_ref, species, plane, y)
        high = planes_of_species(rows_ref, species, plane, (wide - 1) * deep + y)
        x_one[y] = jnp.where(even_x, high, low)
        x_other[y] = jnp.where(even_x, low, high)
    for x in range(wide):
        low = planes_of_species(rows_ref, species, plane, x * deep)
        high = planes_of_species(rows_ref, species, plane, x * deep + deep - 1)
        y_one[x] = jnp.where(even_y, high, low)
        y_other[x] = jnp.where(even_y, low, high)


def tiled(matrix, count):
    size = matrix.shape[1]
    column = lax.broadcasted_iota(jnp.int32, (size, size * count), 1) % size
    pick = (column == lax.broadcasted_iota(jnp.int32, (size, size * count), 0)).astype(jnp.float32)
    return jnp.dot(matrix, pick, precision=HIGHEST, preferred_element_type=jnp.float32)


def where_equal(matrix, of_row, of_column):
    row = lax.broadcasted_iota(jnp.int32, matrix.shape, 0)
    column = lax.broadcasted_iota(jnp.int32, matrix.shape, 1)
    return jnp.where(of_row(row) == of_column(column), matrix, 0.0)


def prepare_kernel(shape, ranks, own_ref, given, *refs):
    wide, deep, species, up = shape
    ranks_a, _ = ranks
    held, semaphores, refs = refs[-11:-1], refs[-1], refs[:-11]
    copies = [
        pltpu.make_async_copy(source, target, semaphores.at[at])
        for at, (source, target) in enumerate(zip(refs[:10], held))
    ]
    for copy in copies:
        copy.start()
    (flow, thermal, diffusivity, constant, energy, production, turned, vertical, east,
     north) = held
    (field, rates, speeds, coefficients, mix, squeeze, wide_rows, upright,
     *factor_rows) = refs[10:]
    for x in range(wide):
        field[x] = jnp.swapaxes(given[:, x], 0, 1)
    for copy in copies:
        copy.wait()
    eye = (
        lax.broadcasted_iota(jnp.int32, (species, species), 0)
        == lax.broadcasted_iota(jnp.int32, (species, species), 1)
    )
    for at, ref in enumerate((diffusivity, constant, energy)):
        column = jnp.sum(jnp.where(eye, ref[...], 0.0), axis=1, keepdims=True)
        coefficients[at] = jnp.broadcast_to(time_step * column if at == 0 else column, (species, up))
    for x in range(wide):
        speeds[3, x] = thermal[x]
        inverse = -1.0 / thermal[x]
        for d in range(3):
            speeds[d, x] = (0.5 * time_step) * flow[d, x]
        for y in range(deep):
            rates[x, y] = coefficients[1] * jnp.exp(coefficients[2] * inverse[y : y + 1])
    count = mix.shape[0] // species
    full = jnp.concatenate([tiled(time_step * production[...], count)] * count, axis=0)
    mix[...] = where_equal(full, lambda at: at // species, lambda at: at // species)
    full = tiled(turned[...], wide)
    full = [jnp.broadcast_to(full[a : a + 1], (wide, full.shape[1])) for a in range(ranks_a)]
    full = jnp.concatenate(full, axis=0)
    squeeze[...] = where_equal(full, lambda at: at % wide, lambda at: at // species)
    pick = lax.broadcasted_iota(jnp.int32, (ranks_a, ranks_a * wide), 1) // wide
    pick = pick == lax.broadcasted_iota(jnp.int32, pick.shape, 0)
    wide_rows[...] = lax.dot_general(
        turned[...], pick.astype(jnp.float32), (((0,), (0,)), ((), ())), precision=HIGHEST,
        preferred_element_type=jnp.float32,
    )
    upright[...] = vertical[...]
    if factor_rows:
        def two_rows(ref, at):
            return jnp.concatenate([ref[pl.ds(2 * at + row, 1), :] for row in range(2)], axis=1)

        factor_rows[0][0:1] = two_rows(east, own_ref[3])
        factor_rows[0][1:2] = two_rows(north, own_ref[2])


def reacted(cells, mix):
    species = cells[0].shape[0]
    group = mix.shape[0] // species
    made = []
    for first in range(0, len(cells), 2 * group):
        some = cells[first : first + 2 * group]
        some = some + [jnp.zeros_like(some[0])] * (-len(some) % group)
        right = [
            jnp.concatenate(some[at : at + group], axis=0) for at in range(0, len(some), group)
        ]
        up = right[0].shape[1]
        produced = jnp.dot(
            mix, jnp.concatenate(right, axis=1), precision=HIGH, preferred_element_type=jnp.float32
        )
        for at in range(len(right)):
            for cell in range(group):
                made.append(
                    produced[cell * species : (cell + 1) * species, at * up : (at + 1) * up]
                )
    return made[: len(cells)]


def sources(here, rates):
    made = rates * here * pltpu.roll(here, here.shape[1] - 1, 1)
    return [made[cell] for cell in range(here.shape[0])]


def advanced(here, x_minus, x_plus, y_minus, y_plus, speeds, diffusivity, produced):
    up = here.shape[2]
    lane = lax.broadcasted_iota(jnp.int32, here.shape, 2)
    z_minus = jnp.where(lane == 0, 0.0, pltpu.roll(here, 1, 2))
    z_plus = jnp.where(lane == up - 1, 0.0, pltpu.roll(here, up - 1, 2))
    laplace = (x_plus + x_minus) + (y_plus + y_minus) + (z_plus + z_minus) - 6.0 * here
    advect = (
        speeds[0] * (x_plus - x_minus)
        + speeds[1] * (y_plus - y_minus)
        + speeds[2] * (z_plus - z_minus)
    )
    return here + diffusivity * laplace - advect + jnp.stack(produced)


def rows_for_species(rows, species):
    return jnp.stack([jnp.broadcast_to(row, (species, row.shape[1])) for row in rows])


def own_speeds(flow, x, deep):
    return [[flow[d, x, pl.ds(y, 1), :] for y in range(deep)] for d in range(3)]


def planes_advanced(planes, here, x_beside, y_beside, rates, speeds, diffusivity, mix, emit, together=4):
    for at in range(0, len(planes), together):
        some = planes[at : at + together]
        cells, counts = [], []
        for x in some:
            made = sources(here(x), rates(x))
            counts.append((len(cells), len(cells) + len(made)))
            cells += made
        produced = reacted(cells, mix)
        for x, (start, end) in zip(some, counts):
            emit(
                x,
                advanced(
                    here(x), x_beside(x, 0), x_beside(x, 1), y_beside(x, 0), y_beside(x, 1),
                    speeds(x), diffusivity, produced[start:end],
                ),
            )


def block_kernel(shape, field, rates, flow, coefficients, mix_ref, out):
    wide, deep, species, up = shape

    def x_beside(x, side):
        at = x + 2 * side - 1
        return field[at] if 0 <= at < wide else jnp.zeros((deep, species, up), jnp.float32)

    def y_beside(x, side):
        here, none = field[x], jnp.zeros((1, species, up), jnp.float32)
        return jnp.concatenate([here[1:], none] if side else [none, here[:-1]], axis=0)

    def emit(x, plane):
        out[x] = plane

    planes_advanced(
        range(wide), lambda x: field[x], x_beside, y_beside, lambda x: rates[x],
        lambda x: [rows_for_species(speed, species) for speed in own_speeds(flow, x, deep)],
        coefficients[0][None], mix_ref[...], emit,
    )


def from_beyond(value, side, speed, diffusivity):
    across = speed * value
    return diffusivity * value - across if side else diffusivity * value + across


def finish(shape, refs, emit):
    wide, deep, species, up = shape
    own_ref, block, x_one, x_other, y_one, y_other, flow, coefficients = refs
    even_x, even_y = own_ref[0] == 1, own_ref[1] == 1
    diffusivity = coefficients[0][None]

    def row(d, x, y):
        return jnp.broadcast_to(flow[d, x, pl.ds(y, 1), :], (species, up))

    for x in range(wide):
        plane = block[x]
        before = jnp.where(even_y, y_other[x], y_one[x])
        after = jnp.where(even_y, y_one[x], y_other[x])
        before = from_beyond(before, 0, row(1, x, 0), diffusivity[0])
        after = from_beyond(after, 1, row(1, x, deep - 1), diffusivity[0])
        plane = jnp.concatenate(
            [(plane[0] + before)[None], plane[1:-1], (plane[-1] + after)[None]], axis=0
        )
        for side in range(2):
            if x == (wide - 1 if side else 0):
                one, other = (x_one, x_other) if side else (x_other, x_one)
                value = jnp.where(even_x, one[...], other[...])
                speed = rows_for_species(own_speeds(flow, x, deep)[0], species)
                plane = plane + from_beyond(value, side, speed, diffusivity)
        emit(x, plane)


def to_one_or_other(even, one, other, high, value):
    first = even if high else jnp.logical_not(even)

    @pl.when(first)
    def _():
        one[...] = value

    @pl.when(jnp.logical_not(first))
    def _():
        other[...] = value


def advance_kernel(shape, *refs):
    wide, deep, _, _ = shape
    own_ref, (out, x_one, x_other, y_one, y_other) = refs[0], refs[8:]
    even_x, even_y = own_ref[0] == 1, own_ref[1] == 1

    def emit(x, plane):
        out[x] = plane
        low, high = plane[0], plane[deep - 1]
        y_one[x] = jnp.where(even_y, high, low)
        y_other[x] = jnp.where(even_y, low, high)
        if x == 0:
            to_one_or_other(even_x, x_one, x_other, False, plane)
        if x == wide - 1:
            to_one_or_other(even_x, x_one, x_other, True, plane)

    finish(shape, refs[:8], emit)


def snapshot_kernel(shape, *refs):
    _, deep, species, _ = shape
    own_ref, flow, (out, y_one, y_other) = refs[0], refs[6], refs[8:]
    even_y = own_ref[1] == 1

    def emit(x, plane):
        out[x] = plane

        def others(y):
            rows = [flow[d, x, pl.ds(y, 1), :] for d in range(4)]
            return jnp.concatenate(rows * 2, axis=0)

        low = jnp.concatenate([plane[0], plane[1], others(0)], axis=0)
        high = jnp.concatenate([plane[deep - 1], plane[deep - 2], others(deep - 1)], axis=0)
        y_one[x] = jnp.where(even_y, high, low)
        y_other[x] = jnp.where(even_y, low, high)

    finish(shape, refs[:8], emit)


def wide_faces_kernel(shape, own_ref, field, y_one, y_other, flow, x_one, x_other):
    wide, deep, species, _ = shape
    even_x, even_y = own_ref[0] == 1, own_ref[1] == 1
    first, second = slice(0, species), slice(species, 2 * species)
    rest = slice(2 * species, 2 * species + 8)

    def face(outer, inner, out):
        for y in range(deep):
            out[y, first] = field[outer, y]
            out[y, second] = field[inner, y]
            rows = [flow[d, outer, y : y + 1, :] for d in range(4)]
            out[y, rest] = jnp.concatenate(rows * 2, axis=0)
        out[deep, first] = jnp.where(even_y, y_other[outer, first], y_one[outer, first])
        out[deep, second] = jnp.where(even_y, y_one[outer, first], y_other[outer, first])
        out[deep, rest] = jnp.zeros_like(out[deep, rest])

    @pl.when(even_x)
    def _():
        face(wide - 1, wide - 2, x_one)
        face(0, 1, x_other)

    @pl.when(jnp.logical_not(even_x))
    def _():
        face(0, 1, x_one)
        face(wide - 1, wide - 2, x_other)


def choose(even, one, other, side, at):
    first, second = (one, other) if side else (other, one)
    return jnp.where(even, first[at], second[at])


def rate_of(temperature, coefficients):
    return coefficients[1] * jnp.exp(coefficients[2] * (-1.0 / temperature))


def third_step_kernel(
    shape, counts, own_ref, block, field, y_one, y_other, rates, flow, coefficients, mix_ref,
    inner, middle,
):
    wide, deep, species, up = shape
    _, columns = counts
    even_y, column = own_ref[1] == 1, own_ref[3]
    inside = (column > 0, column < columns - 1)
    diffusivity, mix = coefficients[0][None], mix_ref[...]
    first, second = slice(0, species), slice(species, 2 * species)
    rest = slice(2 * species, 2 * species + 8)

    def beside(side, x, at):
        return choose(even_y, y_one, y_other, side, (x, at))

    def here(x):
        return jnp.stack([beside(0, x, first), beside(1, x, first)])

    def x_beside(x, side):
        at = x + 2 * side - 1
        return here(at) if 0 <= at < wide else jnp.zeros((2, species, up), jnp.float32)

    def y_beside(x, side):
        outer = beside(side, x, second)
        return jnp.stack([field[x, 0], outer] if side else [outer, field[x, deep - 1]])

    def other_rows(x):
        return [beside(side, x, rest) for side in range(2)]

    def emit(x, plane):
        inner[x, 0] = jnp.where(inside[0], plane[0], 0.0)
        inner[x, deep + 1] = jnp.where(inside[1], plane[1], 0.0)

    planes_advanced(
        range(wide), here, x_beside, y_beside,
        lambda x: jnp.stack(
            [rate_of(rows[3:4], coefficients) for rows in other_rows(x)]
        ),
        lambda x: [
            rows_for_species([rows[d : d + 1] for rows in other_rows(x)], species) for d in range(3)
        ],
        diffusivity, mix, emit, 16,
    )

    def row(x, y):
        return jnp.broadcast_to(flow[1, x, pl.ds(y, 1), :], (species, up))

    for x in range(wide):
        low = from_beyond(beside(0, x, first), 0, row(x, 0), diffusivity[0])
        high = from_beyond(beside(1, x, first), 1, row(x, deep - 1), diffusivity[0])
        inner[x, 1] = block[x, 0] + low
        inner[x, 2:deep] = block[x, 1 : deep - 1]
        inner[x, deep] = block[x, deep - 1] + high

    def emit_last(x, plane):
        middle[:, x - 2] = jnp.swapaxes(plane, 0, 1)

    planes_advanced(
        range(2, wide - 2),
        lambda x: inner[x, 1 : deep + 1],
        lambda x, side: inner[x + 2 * side - 1, 1 : deep + 1],
        lambda x, side: inner[x, 2 * side : 2 * side + deep],
        lambda x: rates[x],
        lambda x: [rows_for_species(speed, species) for speed in own_speeds(flow, x, deep)],
        diffusivity, mix, emit_last,
    )


def fourth_step_kernel(
    shape, counts, own_ref, inner, middle, field, x_one, x_other, y_one, y_other, rates, flow,
    coefficients, mix_ref, out, edge, x_sides,
):
    wide, deep, species, up = shape
    rows, _ = counts
    even_x, even_y, row = own_ref[0] == 1, own_ref[1] == 1, own_ref[2]
    inside = (row > 0, row < rows - 1)
    diffusivity, mix = coefficients[0][None], mix_ref[...]
    first, second = slice(0, species), slice(species, 2 * species)
    rest = slice(2 * species, 2 * species + 8)
    cells = slice(0, deep)

    out[:, 2 : wide - 2] = middle[...]

    def beside(side, at, of=cells):
        return choose(even_x, x_one, x_other, side, (of, at))

    def corners(side):
        return [beside(side, at, deep) for at in (first, second)]

    def last(side):
        return wide - 1 if side else 0

    def y_beside(side, to):
        here, corner = beside(side, first), corners(side)[to][None]
        return jnp.concatenate([here[1:], corner] if to else [corner, here[:-1]], axis=0)

    def other_rows(side):
        others = beside(side, rest)
        return [others[y] for y in range(deep)]

    def emit(side, plane):
        x_sides[side] = jnp.where(inside[side], plane, 0.0)

    planes_advanced(
        range(2), lambda side: beside(side, first),
        lambda side, to: beside(side, second) if side == to else field[last(side)],
        y_beside,
        lambda side: jnp.stack(
            [rate_of(rows[3:4], coefficients) for rows in other_rows(side)]
        ),
        lambda side: [
            rows_for_species([rows[d : d + 1] for rows in other_rows(side)], species)
            for d in range(3)
        ],
        diffusivity, mix, emit,
    )
    for side in range(2):
        x = last(side)
        low, high = corners(side)
        value = jnp.concatenate([low[None], beside(side, first), high[None]], axis=0)
        ends = [choose(even_y, y_one, y_other, to, (x, rest))[0:1] for to in range(2)]
        speed = rows_for_species([ends[0]] + own_speeds(flow, x, deep)[0] + [ends[1]], species)
        edge[side] = inner[x] + from_beyond(value, side, speed, diffusivity)

    def plane_of(x):
        if x < 0 or x >= wide:
            return x_sides[0 if x < 0 else 1]
        if x == 0 or x == wide - 1:
            return edge[0 if x == 0 else 1, 1 : deep + 1]
        return inner[x, 1 : deep + 1]

    def y_of(x, side):
        at = slice(2 * side, 2 * side + deep)
        return edge[0 if x == 0 else 1, at] if x in (0, wide - 1) else inner[x, at]

    def emit_last(x, plane):
        out[:, x] = jnp.swapaxes(plane, 0, 1)

    planes_advanced(
        [0, 1, wide - 2, wide - 1], plane_of, lambda x, side: plane_of(x + 2 * side - 1), y_of,
        lambda x: rates[x],
        lambda x: [rows_for_species(speed, species) for speed in own_speeds(flow, x, deep)],
        diffusivity, mix, emit_last,
    )


def project_kernel(shape, ranks, field, component, vertical, factor_rows, out):
    wide, deep, species, up = shape
    ranks_a, ranks_d = ranks
    each = deep + 2
    for y in range(deep):
        rows = field[:, y].reshape(wide * species, up)
        on_a = jnp.dot(component[...], rows, precision=HIGHEST, preferred_element_type=jnp.float32)
        on_d = lax.dot_general(
            vertical[...], on_a, (((1,), (1,)), ((), ())), precision=HIGHEST,
            preferred_element_type=jnp.float32,
        )
        out[pl.ds(y, ranks_d, stride=each), :] = on_d
    for row in range(2):
        out[pl.ds(deep + row, ranks_d, stride=each), :] = jnp.broadcast_to(
            factor_rows[row : row + 1], (ranks_d, 128)
        )


def core_kernel(counts, got, out):
    rows, columns, ranks_a, tall, deep = counts
    devices, each = rows * columns, deep + 2
    own = 128 // ranks_a

    def dot(a, b, contract, precision=HIGHEST):
        return lax.dot_general(
            a, b, ((contract[:1], contract[1:]), ((), ())), precision=precision,
            preferred_element_type=jnp.float32,
        )

    whole = jnp.concatenate(
        [
            jnp.concatenate(
                [got[pl.ds((row * columns + column) * each, deep), :] for column in range(columns)],
                axis=0,
            )
            for row in range(rows)
        ],
        axis=1,
    )

    def in_order(at, of_row):
        both = got[pl.ds(at, devices, stride=each), :]
        halves = jnp.concatenate([both[:, :64], both[:, 64:]], axis=0)
        pick = jnp.full((2 * devices, 2 * devices), 1.0, jnp.float32)
        return dot(where_equal(pick, of_row, lambda at: at), halves, (1, 0))

    east = in_order(deep, lambda at: at % 2 * devices + at // 2)
    north = in_order(
        deep + 1, lambda at: at % 2 * devices + at % deep // 2 * columns + at // deep
    )

    def by_rank(array):
        return jnp.concatenate(
            [
                jnp.concatenate(
                    [
                        array[(row * ranks_a + a) * own : (row * ranks_a + a + 1) * own]
                        for row in range(rows)
                    ],
                    axis=0,
                )
                for a in range(ranks_a)
            ],
            axis=1,
        )

    def by_row(parts):
        return jnp.concatenate(
            [
                parts[a][row * own : (row + 1) * own]
                for row in range(rows)
                for a in range(ranks_a)
            ],
            axis=0,
        ).T

    half = by_rank(dot(whole, north, (0, 0)))
    core = dot(east, half, (0, 0))
    half = dot(east, core, (1, 0))
    ranks_c = north.shape[1]
    split = [slice(a * ranks_c, (a + 1) * ranks_c) for a in range(ranks_a)]
    core = by_row([core[:, at] for at in split])
    whole = by_row([dot(half[:, at], north, (1, 1)) for at in split])
    for row in range(rows):
        for column in range(columns):
            at = row * columns + column
            out[at, 0:tall] = core[column * tall : (column + 1) * tall, row * 128 : (row + 1) * 128]
            out[at, tall : tall + deep] = whole[
                column * deep : (column + 1) * deep, row * 128 : (row + 1) * 128
            ]


def expand_kernel(shape, ranks, tall, got, field, wide_rows, vertical, residual, core, full):
    wide, deep, species, up = shape
    ranks_a, ranks_d = ranks
    each = tall + deep
    component = where_equal(
        jnp.concatenate([wide_rows[...]] * wide, axis=0),
        lambda at: at // species,
        lambda at: at % wide,
    )
    for y in range(deep):
        on_d = got[pl.ds(tall + y, ranks_d, stride=each), :]
        on_a = lax.dot_general(
            on_d, vertical[...], (((0,), (0,)), ((), ())), precision=HIGH,
            preferred_element_type=jnp.float32,
        )
        full[y] = jnp.dot(component, on_a, precision=HIGH, preferred_element_type=jnp.float32)
    for x in range(wide):
        residual[:, x] = jnp.swapaxes(
            field[x] - full[:, x * species : (x + 1) * species, :], 0, 1
        )
    turned = [got[pl.ds(c, ranks_d, stride=each), :].T for c in range(tall)]
    core[...] = jnp.swapaxes(jnp.stack(turned), 0, 1)


def swapped(one, other, axes):
    got = []
    for first, face in enumerate((one, other)):
        couples = [(i, i + 1) for i in range(first, lax.axis_size(axes) - 1, 2)]
        got.append(lax.ppermute(face, axes, couples + [(b, a) for a, b in couples]))
    return got


def faces_beside(faces):
    x_one, x_other, y_one, y_other = faces
    y_one, y_other = swapped(y_one, y_other, COLUMN)
    x_one, x_other = swapped(x_one, x_other, ROW)
    return x_one, x_other, y_one, y_other


def whole_factors(tucker_factor_east, tucker_factor_north):
    rows, columns = lax.axis_size(ROW), lax.axis_size(COLUMN)

    def shares(factor, holders, axes):
        count = -(-factor.shape[0] // holders)
        padded = jnp.pad(factor, ((0, count * holders - factor.shape[0]), (0, 0)))
        return lax.dynamic_slice_in_dim(padded, lax.axis_index(axes) * count, count, 0)

    east = shares(tucker_factor_east, columns, COLUMN)
    north = shares(tucker_factor_north, rows, ROW)
    sent = jnp.concatenate([east.reshape(-1), north.reshape(-1)])
    sent = jnp.pad(sent, (0, -sent.size % 128)).reshape(1, -1, 128)
    sent = jnp.broadcast_to(sent, (rows * columns,) + sent.shape[1:])
    got = lax.all_to_all(sent, EVERY, 0, 0, tiled=True).reshape(rows, columns, -1)
    whole_east = got[:, :, : east.size].reshape(rows, -1, east.shape[1])
    whole_east = whole_east[:, : tucker_factor_east.shape[0]].reshape(-1, east.shape[1])
    whole_north = got[:, :, east.size : east.size + north.size]
    whole_north = whole_north.reshape(rows, columns, *north.shape).transpose(1, 0, 2, 3)
    whole_north = whole_north.reshape(columns, -1, north.shape[1])
    whole_north = whole_north[:, : tucker_factor_north.shape[0]].reshape(-1, north.shape[1])
    return whole_east, whole_north


def compress_and_expand(snapshot, east, north, vertical, component):
    rows, columns = lax.axis_size(ROW), lax.axis_size(COLUMN)
    devices = rows * columns
    (wide, deep, _, _), (_, ranks_a) = snapshot.shape, component.shape
    ranks_d = vertical.shape[1]
    ranks_b, ranks_c = east.shape[1], north.shape[1]
    projected = jnp.einsum("xysz,sa->xyaz", snapshot, component, precision=HIGHEST)
    projected = jnp.einsum("xyaz,zd->dyxa", projected, vertical, precision=HIGHEST)
    pairs = ranks_a * ranks_d
    share = -(-pairs // devices)
    flat = jnp.transpose(projected, (0, 3, 1, 2)).reshape(pairs, deep, wide)
    flat = jnp.pad(flat, ((0, share * devices - pairs), (0, 0), (0, 0)))
    flat = flat.reshape(devices, share, deep, wide).transpose(0, 2, 3, 1)
    flat = lax.all_to_all(
        flat.reshape(devices, deep, wide * share), EVERY, 0, 0, tiled=True
    )
    whole = flat.reshape(rows, columns * deep, wide, share)
    part = jnp.einsum("gyxp,yc->cgxp", whole, north, precision=HIGHEST)
    part = part.reshape(ranks_c, rows * wide, share)
    core = jnp.einsum("cxp,xb->cbp", part, east, precision=HIGHEST)
    part = jnp.einsum("cbp,xb->cxp", core, east, precision=HIGHEST)
    whole = jnp.einsum("cxp,yc->yxp", part, north, precision=HIGHEST)
    own_b, own_c = ranks_b // rows, ranks_c // columns

    def pieces(array, tall, broad):
        array = array.reshape(columns, tall, rows, broad, share)
        return array.transpose(2, 0, 1, 3, 4).reshape(devices, tall * broad * share)

    sent = jnp.concatenate([pieces(core, own_c, own_b), pieces(whole, deep, wide)], axis=1)
    sent = jnp.pad(sent, ((0, 0), (0, -sent.shape[1] % 1024)))
    got = lax.all_to_all(
        sent.reshape(devices, -1, 128), EVERY, 0, 0, tiled=True
    ).reshape(devices, -1)

    def ranks_together(array, tall, broad):
        array = array.reshape(devices, tall, broad, share).transpose(0, 3, 2, 1)
        array = array.reshape(devices * share, broad, tall)[:pairs]
        return array.reshape(ranks_d, ranks_a, broad, tall)

    core_size = own_c * own_b * share
    core = ranks_together(got[:, :core_size], own_c, own_b).transpose(1, 2, 3, 0)
    expanded = ranks_together(got[:, core_size : core_size + deep * wide * share], deep, wide)
    expanded = jnp.einsum("daxy,zd->axyz", expanded, vertical, precision=HIGHEST)
    expanded = jnp.einsum("axyz,sa->sxyz", expanded, component, precision=HIGHEST)
    return core, snapshot.transpose(2, 0, 1, 3) - expanded


def body(
    mixture_fields_initial,
    flow_speed_vector,
    thermal_field,
    mass_diffusivity,
    arrhenius_constant,
    arrhenius_energy_temp,
    production_coefficients,
    tucker_factor_east,
    tucker_factor_north,
    tucker_factor_vertical,
    tucker_factor_component,
):
    species, wide, deep, up = mixture_fields_initial.shape
    shape = (wide, deep, species, up)
    cells = wide * deep * species * up
    rows, columns = lax.axis_size(ROW), lax.axis_size(COLUMN)
    devices = rows * columns
    ranks_a, ranks_d = tucker_factor_component.shape[1], tucker_factor_vertical.shape[1]
    ranks_b, ranks_c = tucker_factor_east.shape[1], tucker_factor_north.shape[1]
    own_b, own_c = ranks_b // rows, ranks_c // columns
    kernels_fit = (
        ranks_d == devices
        and wide * ranks_a == 128
        and own_b * ranks_a == 128
        and deep == own_c == 8
        and ranks_b == ranks_c == 64
        and wide == 2 * columns
        and deep == 2 * rows
    )

    row, column = lax.axis_index(ROW), lax.axis_index(COLUMN)
    own = jnp.stack([1 - row % 2, 1 - column % 2, row, column]).astype(jnp.int32)
    face_shapes = [(deep, species, up)] * 2 + [(wide, species, up)] * 2
    field_rows = mixture_fields_initial.reshape(species * wide * deep, up)
    faces = vmem_call(functools.partial(faces_kernel, shape), face_shapes, 1, 2)(own, field_rows)
    faces = faces_beside(faces)
    both = 16
    out_shapes = [
        shape, shape, (4, wide, deep, up), (3, species, up), (both * species,) * 2,
        (wide * ranks_a, wide * species), (species, wide * ranks_a), (ranks_d, up),
    ] + [(2, 128)] * kernels_fit
    small = (
        flow_speed_vector, thermal_field, mass_diffusivity[None], arrhenius_constant[None],
        arrhenius_energy_temp[None], production_coefficients,
        tucker_factor_component.T, tucker_factor_vertical.T, tucker_factor_east,
        tucker_factor_north,
    )
    vmem, smem = (pl.BlockSpec(memory_space=space) for space in (pltpu.VMEM, pltpu.SMEM))
    (field, rates, speeds, coefficients, mix, squeeze, wide_rows, upright,
     *factor_rows) = pl.pallas_call(
        functools.partial(prepare_kernel, shape, (ranks_a, ranks_d)),
        in_specs=[smem, vmem] + [pl.BlockSpec(memory_space=pltpu.HBM)] * len(small),
        out_specs=[vmem] * len(out_shapes),
        out_shape=[jax.ShapeDtypeStruct(out, jnp.float32) for out in out_shapes],
        scratch_shapes=[pltpu.VMEM(array.shape, jnp.float32) for array in small]
        + [pltpu.SemaphoreType.DMA((len(small),))],
        compiler_params=pltpu.CompilerParams(vmem_limit_bytes=VMEM_LIMIT),
        cost_estimate=pl.CostEstimate(
            flops=4 * cells, bytes_accessed=12 * cells, transcendentals=cells
        ),
    )(
        own, mixture_fields_initial,
        *(pltpu.with_memory_space_constraint(array, pltpu.HBM) for array in small),
    )
    block = vmem_call(
        functools.partial(block_kernel, shape), [shape], 0, 5, flops=60 * cells, moved=8 * cells
    )
    advance = vmem_call(
        functools.partial(advance_kernel, shape), [shape] + face_shapes, 1, 8,
        flops=4 * cells, moved=8 * cells,
    )
    fixed = (rates, speeds, coefficients, mix)
    for substep in range(SUB - 1):
        field, *faces = advance(
            own, *block(field, *fixed), *faces, speeds, coefficients
        )
        faces = faces_beside(faces)
    high = 2 * species + 8
    snapshot, *y_faces = vmem_call(
        functools.partial(snapshot_kernel, shape), [shape] + [(wide, high, up)] * 2, 1, 8,
        flops=4 * cells, moved=8 * cells,
    )(own, *block(field, *fixed), *faces, speeds, coefficients)
    y_faces = swapped(*y_faces, COLUMN)
    x_faces = vmem_call(
        functools.partial(wide_faces_kernel, shape), [(deep + 1, high, up)] * 2, 1, 5,
        flops=cells, moved=cells,
    )(own, snapshot, *y_faces, speeds)
    x_faces = swapped(*x_faces, ROW)
    inner, middle = vmem_call(
        functools.partial(third_step_kernel, shape, (rows, columns)),
        [(wide, deep + 2, species, up), (species, wide - 4, deep, up)], 1, 9,
        flops=120 * cells, moved=16 * cells,
    )(own, *block(snapshot, *fixed), snapshot, *y_faces, *fixed)
    if kernels_fit:
        (sent,) = vmem_call(
            functools.partial(project_kernel, shape, (ranks_a, ranks_d)),
            [(devices * (deep + 2), 128)], 0, 4, flops=60 * cells, moved=4 * cells,
        )(snapshot, squeeze, upright, *factor_rows)
        got = lax.all_to_all(
            sent.reshape(devices, (deep + 2) // 2, 2, 128), EVERY, 0, 0, tiled=True
        )
        (sent,) = vmem_call(
            functools.partial(core_kernel, (rows, columns, ranks_a, own_c, deep)),
            [(devices, own_c + deep, 128)], 0, 1, flops=60 * cells, moved=4 * cells,
        )(got.reshape(devices * (deep + 2), 128))
        got = lax.all_to_all(sent, EVERY, 0, 0, tiled=True)
        residual, tucker_core = vmem_call(
            functools.partial(expand_kernel, shape, (ranks_a, ranks_d), own_c),
            [mixture_fields_initial.shape, (ranks_a * own_b, own_c, ranks_d)], 0, 4,
            flops=60 * cells, moved=8 * cells, scratch=[(deep, wide * species, up)],
        )(
            got.reshape(devices * (own_c + deep), 128),
            snapshot,
            wide_rows,
            upright,
        )
        tucker_core = tucker_core.reshape(ranks_a, own_b, own_c, ranks_d)
    else:
        east, north = whole_factors(tucker_factor_east, tucker_factor_north)
        tucker_core, residual = compress_and_expand(
            snapshot, east, north, tucker_factor_vertical, tucker_factor_component
        )
    own_last, _ = lax.optimization_barrier((own, tucker_core))
    (mixture_fields_final,) = vmem_call(
        functools.partial(fourth_step_kernel, shape, (rows, columns)),
        [mixture_fields_initial.shape], 1, 12,
        flops=60 * cells, moved=8 * cells,
        scratch=[(2, deep + 2, species, up), (2, deep, species, up)],
    )(own_last, inner, middle, snapshot, *x_faces, *y_faces, *fixed)
    return (mixture_fields_final, residual, tucker_core)


def solution(mesh):
    in_specs = (
        P(None, "gx", ("gy", "ga"), None),
        P(None, "gx", ("gy", "ga"), None),
        P("gx", ("gy", "ga"), None),
        P(),
        P(),
        P(),
        P(),
        P("gx", None),
        P(("gy", "ga"), None),
        P(),
        P(),
    )
    out_specs = (
        P(None, "gx", ("gy", "ga"), None),
        P(None, "gx", ("gy", "ga"), None),
        P(None, "gx", ("gy", "ga"), None),
    )
    return jax.shard_map(body, mesh=mesh, in_specs=in_specs, out_specs=out_specs, check_vma=False)
```

```python
import functools

import jax
import jax.numpy as jnp
from jax import lax
from jax.experimental import pallas as pl
from jax.experimental.pallas import tpu as pltpu
from jax.sharding import PartitionSpec as P

SUB = 2


time_step = 0.5

ROW = "gx"
COLUMN = ("gy", "ga")
EVERY = ("gx", "gy", "ga")
HIGHEST = lax.Precision.HIGHEST
VMEM_LIMIT = 4 * 1024 * 1024


def vmem_call(
    kernel, outs, in_smem, n_in, flops=0, moved=0, exps=0, scratch=(), placed=(), copies=0, aliases={}
):
    vmem = pl.BlockSpec(memory_space=pltpu.VMEM)
    smem = pl.BlockSpec(memory_space=pltpu.SMEM)
    anywhere = pl.BlockSpec(memory_space=pl.ANY)
    ins = [smem] * in_smem + [vmem] * (n_in - in_smem)
    specs = [anywhere if at in placed else spec for at, spec in enumerate(ins + [vmem] * len(outs))]
    return pl.pallas_call(
        kernel,
        in_specs=specs[:n_in],
        out_specs=specs[n_in:],
        out_shape=[jax.ShapeDtypeStruct(shape, jnp.float32) for shape in outs],
        scratch_shapes=[pltpu.VMEM(shape, jnp.float32) for shape in scratch]
        + [pltpu.SemaphoreType.DMA((copies,))] * (copies > 0),
        input_output_aliases=aliases,
        compiler_params=pltpu.CompilerParams(vmem_limit_bytes=VMEM_LIMIT),
        cost_estimate=pl.CostEstimate(flops=flops, bytes_accessed=moved, transcendentals=exps),
    )


def planes_of_species(ref, species, plane, at):
    return jnp.concatenate(
        [ref[pl.ds(first * plane + at, 8, stride=plane), :] for first in range(0, species, 8)], axis=0
    )


def store_planes_of_species(ref, species, plane, at, value):
    for first in range(0, species, 8):
        ref[pl.ds(first * plane + at, 8, stride=plane), :] = value[first : first + 8]


def faces_kernel(shape, even_ref, rows_ref, x_one, x_other, y_one, y_other):
    wide, deep, species, _ = shape
    even_x, even_y = even_ref[0] == 1, even_ref[1] == 1
    plane = wide * deep
    for y in range(deep):
        low = planes_of_species(rows_ref, species, plane, y)
        high = planes_of_species(rows_ref, species, plane, (wide - 1) * deep + y)
        x_one[y] = jnp.where(even_x, high, low)
        x_other[y] = jnp.where(even_x, low, high)
    for x in range(wide):
        low = planes_of_species(rows_ref, species, plane, x * deep)
        high = planes_of_species(rows_ref, species, plane, x * deep + deep - 1)
        y_one[x] = jnp.where(even_y, high, low)
        y_other[x] = jnp.where(even_y, low, high)


def tiled(matrix, count):
    size = matrix.shape[1]
    column = lax.broadcasted_iota(jnp.int32, (size, size * count), 1) % size
    pick = (column == lax.broadcasted_iota(jnp.int32, (size, size * count), 0)).astype(jnp.float32)
    return jnp.dot(matrix, pick, precision=HIGHEST, preferred_element_type=jnp.float32)


def where_equal(matrix, of_row, of_column):
    row = lax.broadcasted_iota(jnp.int32, matrix.shape, 0)
    column = lax.broadcasted_iota(jnp.int32, matrix.shape, 1)
    return jnp.where(of_row(row) == of_column(column), matrix, 0.0)


def prepare_kernel(shape, ranks, own_ref, given, *refs):
    wide, deep, species, up = shape
    ranks_a, _ = ranks
    held, semaphores, refs = refs[-11:-1], refs[-1], refs[:-11]
    copies = [
        pltpu.make_async_copy(source, target, semaphores.at[at])
        for at, (source, target) in enumerate(zip(refs[:10], held))
    ]
    for copy in copies:
        copy.start()
    (flow, thermal, diffusivity, constant, energy, production, turned, vertical, east,
     north) = held
    (field, rates, speeds, coefficients, mix, squeeze, wide_rows, upright,
     *factor_rows) = refs[10:]
    for x in range(wide):
        field[x] = jnp.swapaxes(given[:, x], 0, 1)
    for copy in copies:
        copy.wait()
    eye = (
        lax.broadcasted_iota(jnp.int32, (species, species), 0)
        == lax.broadcasted_iota(jnp.int32, (species, species), 1)
    )
    for at, ref in enumerate((diffusivity, constant, energy)):
        column = jnp.sum(jnp.where(eye, ref[...], 0.0), axis=1, keepdims=True)
        coefficients[at] = jnp.broadcast_to(time_step * column if at == 0 else column, (species, up))
    for x in range(wide):
        speeds[3, x] = thermal[x]
        inverse = -1.0 / thermal[x]
        for d in range(3):
            speeds[d, x] = (0.5 * time_step) * flow[d, x]
        for y in range(deep):
            rates[x, y] = coefficients[1] * jnp.exp(coefficients[2] * inverse[y : y + 1])
    mix[...] = tiled(time_step * production[...], mix.shape[1] // species)
    full = tiled(turned[...], wide)
    full = [jnp.broadcast_to(full[a : a + 1], (wide, full.shape[1])) for a in range(ranks_a)]
    full = jnp.concatenate(full, axis=0)
    squeeze[...] = where_equal(full, lambda at: at % wide, lambda at: at // species)
    pick = lax.broadcasted_iota(jnp.int32, (ranks_a, ranks_a * wide), 1) // wide
    pick = pick == lax.broadcasted_iota(jnp.int32, pick.shape, 0)
    wide_rows[...] = lax.dot_general(
        turned[...], pick.astype(jnp.float32), (((0,), (0,)), ((), ())), precision=HIGHEST,
        preferred_element_type=jnp.float32,
    )
    upright[...] = vertical[...]
    if factor_rows:
        def two_rows(ref, at):
            return jnp.concatenate([ref[pl.ds(2 * at + row, 1), :] for row in range(2)], axis=1)

        factor_rows[0][0:1] = two_rows(east, own_ref[3])
        factor_rows[0][1:2] = two_rows(north, own_ref[2])


def halves_of(value):
    high = value.astype(jnp.bfloat16)
    return high, (value - high.astype(jnp.float32)).astype(jnp.bfloat16)


def product(a, b, contract):
    def dot(left, right):
        return lax.dot_general(
            left, right, ((contract[:1], contract[1:]), ((), ())),
            preferred_element_type=jnp.float32,
        )

    (a_high, a_low), (b_high, b_low) = halves_of(a), halves_of(b)
    return dot(a_high, b_high) + (dot(a_high, b_low) + dot(a_low, b_high))


def mixing(rows):
    species, size = rows.shape
    full = jnp.concatenate([rows] * (size // species), axis=0)
    high, low = halves_of(
        where_equal(full, lambda at: at // species, lambda at: at // species)
    )
    return jnp.concatenate(
        [jnp.concatenate([high, high], axis=1), jnp.concatenate([low, low], axis=1)], axis=0
    )


def reacted(cells, mix):
    species, up = cells[0].shape
    size = mix.shape[0] // 2
    group = size // species
    cells = cells + [jnp.zeros_like(cells[0])] * (-len(cells) % group)
    right = []
    for at in range(0, len(cells), group):
        high, low = halves_of(jnp.concatenate(cells[at : at + group], axis=0))
        right.append(jnp.concatenate([high, low], axis=0))
    produced = jnp.dot(mix, jnp.concatenate(right, axis=1), preferred_element_type=jnp.float32)
    produced = produced[:size] + produced[size:]
    return [
        produced[cell * species : (cell + 1) * species, at * up : (at + 1) * up]
        for at in range(len(right))
        for cell in range(group)
    ]


def sources(here, rates):
    made = rates * here * pltpu.roll(here, here.shape[1] - 1, 1)
    return [made[cell] for cell in range(here.shape[0])]


def advanced(here, x_minus, x_plus, y_minus, y_plus, speeds, diffusivity, produced):
    up = here.shape[2]
    lane = lax.broadcasted_iota(jnp.int32, here.shape, 2)
    z_minus = jnp.where(lane == 0, 0.0, pltpu.roll(here, 1, 2))
    z_plus = jnp.where(lane == up - 1, 0.0, pltpu.roll(here, up - 1, 2))
    laplace = (x_plus + x_minus) + (y_plus + y_minus) + (z_plus + z_minus) - 6.0 * here
    advect = (
        speeds[0] * (x_plus - x_minus)
        + speeds[1] * (y_plus - y_minus)
        + speeds[2] * (z_plus - z_minus)
    )
    return here + diffusivity * laplace - advect + jnp.stack(produced)


def rows_for_species(rows, species):
    return jnp.stack([jnp.broadcast_to(row, (species, row.shape[1])) for row in rows])


def own_speeds(flow, x, deep):
    return [[flow[d, x, pl.ds(y, 1), :] for y in range(deep)] for d in range(3)]


def planes_advanced(planes, here, x_beside, y_beside, rates, speeds, diffusivity, mix, emit, together=4):
    for at in range(0, len(planes), together):
        some = planes[at : at + together]
        cells, counts = [], []
        for x in some:
            made = sources(here(x), rates(x))
            counts.append((len(cells), len(cells) + len(made)))
            cells += made
        produced = reacted(cells, mix)
        for x, (start, end) in zip(some, counts):
            emit(
                x,
                advanced(
                    here(x), x_beside(x, 0), x_beside(x, 1), y_beside(x, 0), y_beside(x, 1),
                    speeds(x), diffusivity, produced[start:end],
                ),
            )


def rate_of(temperature, coefficients):
    return coefficients[1] * jnp.exp(coefficients[2] * (-1.0 / temperature))


def own_rates(flow, coefficients, x, deep):
    inverse = -1.0 / flow[3, x]
    return jnp.stack(
        [coefficients[1] * jnp.exp(coefficients[2] * inverse[y : y + 1]) for y in range(deep)]
    )


def block_kernel(shape, field, rates, flow, coefficients, mix_ref, out):
    wide, deep, species, up = shape

    def x_beside(x, side):
        at = x + 2 * side - 1
        return field[at] if 0 <= at < wide else jnp.zeros((deep, species, up), jnp.float32)

    def y_beside(x, side):
        here, none = field[x], jnp.zeros((1, species, up), jnp.float32)
        return jnp.concatenate([here[1:], none] if side else [none, here[:-1]], axis=0)

    def emit(x, plane):
        out[x] = plane

    planes_advanced(
        range(wide), lambda x: field[x], x_beside, y_beside,
        lambda x: rates[x],
        lambda x: [rows_for_species(speed, species) for speed in own_speeds(flow, x, deep)],
        coefficients[0][None], mixing(mix_ref[...]), emit,
    )


def from_beyond(value, side, speed, diffusivity):
    across = speed * value
    return diffusivity * value - across if side else diffusivity * value + across


def finish(shape, refs, emit):
    wide, deep, species, up = shape
    own_ref, block, x_one, x_other, y_one, y_other, flow, coefficients = refs
    even_x, even_y = own_ref[0] == 1, own_ref[1] == 1
    diffusivity = coefficients[0][None]

    def row(d, x, y):
        return jnp.broadcast_to(flow[d, x, pl.ds(y, 1), :], (species, up))

    for x in range(wide):
        plane = block[x]
        before = jnp.where(even_y, y_other[x], y_one[x])
        after = jnp.where(even_y, y_one[x], y_other[x])
        before = from_beyond(before, 0, row(1, x, 0), diffusivity[0])
        after = from_beyond(after, 1, row(1, x, deep - 1), diffusivity[0])
        plane = jnp.concatenate(
            [(plane[0] + before)[None], plane[1:-1], (plane[-1] + after)[None]], axis=0
        )
        for side in range(2):
            if x == (wide - 1 if side else 0):
                one, other = (x_one, x_other) if side else (x_other, x_one)
                value = jnp.where(even_x, one[...], other[...])
                speed = rows_for_species(own_speeds(flow, x, deep)[0], species)
                plane = plane + from_beyond(value, side, speed, diffusivity)
        emit(x, plane)


def to_one_or_other(even, one, other, high, value):
    first = even if high else jnp.logical_not(even)

    @pl.when(first)
    def _():
        one[...] = value

    @pl.when(jnp.logical_not(first))
    def _():
        other[...] = value


def advance_kernel(shape, *refs):
    wide, deep, _, _ = shape
    own_ref, (out, x_one, x_other, y_one, y_other) = refs[0], refs[8:]
    even_x, even_y = own_ref[0] == 1, own_ref[1] == 1

    def emit(x, plane):
        out[x] = plane
        low, high = plane[0], plane[deep - 1]
        y_one[x] = jnp.where(even_y, high, low)
        y_other[x] = jnp.where(even_y, low, high)
        if x == 0:
            to_one_or_other(even_x, x_one, x_other, False, plane)
        if x == wide - 1:
            to_one_or_other(even_x, x_one, x_other, True, plane)

    finish(shape, refs[:8], emit)


def outer_of(cell, species):
    return slice(2 * cell * species, (2 * cell + 1) * species)


def inner_of(cell, species):
    return slice((2 * cell + 1) * species, (2 * cell + 2) * species)


def flow_of(cell, count, species):
    return slice(2 * count * species + 4 * cell, 2 * count * species + 4 * cell + 4)


def snapshot_kernel(shape, *refs):
    wide, deep, species, _ = shape
    own_ref, flow, (out, y_one, y_other) = refs[0], refs[6], refs[8:]
    even_y = own_ref[1] == 1

    def emit(x, plane):
        out[x] = plane

        def put(low, high, at):
            y_one[at] = jnp.where(even_y, high, low)
            y_other[at] = jnp.where(even_y, low, high)

        def others(y):
            return jnp.concatenate([flow[d, x, pl.ds(y, 1), :] for d in range(4)], axis=0)

        put(plane[0], plane[deep - 1], outer_of(x, species))
        put(plane[1], plane[deep - 2], inner_of(x, species))
        put(others(0), others(deep - 1), flow_of(x, wide, species))

    finish(shape, refs[:8], emit)


def wide_faces_kernel(shape, own_ref, field, y_one, y_other, flow, x_one, x_other):
    wide, deep, species, _ = shape
    even_x, even_y = own_ref[0] == 1, own_ref[1] == 1

    def face(outer, inner, out):
        for y in range(deep):
            out[outer_of(y, species)] = field[outer, y]
            out[inner_of(y, species)] = field[inner, y]
            out[flow_of(y, deep + 1, species)] = jnp.concatenate(
                [flow[d, outer, y : y + 1, :] for d in range(4)], axis=0
            )
        at = outer_of(outer, species)
        out[outer_of(deep, species)] = choose(even_y, y_one, y_other, 0, at)
        out[inner_of(deep, species)] = choose(even_y, y_one, y_other, 1, at)

    @pl.when(even_x)
    def _():
        face(wide - 1, wide - 2, x_one)
        face(0, 1, x_other)

    @pl.when(jnp.logical_not(even_x))
    def _():
        face(0, 1, x_one)
        face(wide - 1, wide - 2, x_other)


def planes_copied(groups, ready, out, semaphores):
    copies, at = {}, 0
    for group in groups:
        copies[group[-1]] = pltpu.make_async_copy(
            ready.at[:, pl.ds(at, len(group))],
            out.at[:, pl.ds(group[0], len(group))],
            semaphores.at[len(copies)],
        )
        at += len(group)
    return copies


def choose(even, one, other, side, at):
    first, second = (one, other) if side else (other, one)
    return jnp.where(even, first[at], second[at])


def third_step_kernel(
    shape, counts, own_ref, field, y_one, y_other, flow, coefficients, mix_ref, edges, ends, out,
    inner, ready, semaphores,
):
    wide, deep, species, up = shape
    _, columns = counts
    even_y, column = own_ref[1] == 1, own_ref[3]
    inside = (column > 0, column < columns - 1)
    diffusivity, mix = coefficients[0][None], mixing(mix_ref[...])

    def beside(side, x, rows):
        return choose(even_y, y_one, y_other, side, rows)

    def here(x):
        at = outer_of(x, species)
        return jnp.concatenate(
            [beside(0, x, at)[None], field[x], beside(1, x, at)[None]], axis=0
        )

    def x_beside(x, side):
        at = x + 2 * side - 1
        return here(at) if 0 <= at < wide else jnp.zeros((deep + 2, species, up), jnp.float32)

    def y_beside(x, side):
        plane, beyond = here(x), beside(side, x, inner_of(x, species))[None]
        return jnp.concatenate([plane[1:], beyond] if side else [beyond, plane[:-1]], axis=0)

    def others(side, x):
        return beside(side, x, flow_of(x, wide, species))

    def rates(x):
        sides = [rate_of(others(side, x)[3:4], coefficients)[None] for side in range(2)]
        return jnp.concatenate([sides[0], own_rates(flow, coefficients, x, deep), sides[1]], axis=0)

    def speeds(x):
        ends, own = [others(side, x) for side in range(2)], own_speeds(flow, x, deep)
        return [
            rows_for_species([ends[0][d : d + 1]] + own[d] + [ends[1][d : d + 1]], species)
            for d in range(3)
        ]

    def emit(x, plane):
        inner[x, 0] = jnp.where(inside[0], plane[0], 0.0)
        inner[x, 1 : deep + 1] = plane[1 : deep + 1]
        inner[x, deep + 1] = jnp.where(inside[1], plane[deep + 1], 0.0)
        if x < 3 or x >= wide - 3:
            edges[x if x < 3 else x - wide + 6] = inner[x]
        if x in (0, wide - 1):
            for side in range(2):
                ends[0 if x == 0 else 1, side, 0:4] = others(side, x)

    planes_advanced(range(wide), here, x_beside, y_beside, rates, speeds, diffusivity, mix, emit)

    inmost = range(2, wide - 2)
    copies = planes_copied(
        [inmost[at : at + 4] for at in range(0, len(inmost), 4)], ready, out, semaphores
    )

    def emit_last(x, plane):
        ready[:, x - 2] = jnp.swapaxes(plane, 0, 1)
        if x in copies:
            copies[x].start()

    planes_advanced(
        inmost,
        lambda x: inner[x, 1 : deep + 1],
        lambda x, side: inner[x + 2 * side - 1, 1 : deep + 1],
        lambda x, side: inner[x, 2 * side : 2 * side + deep],
        lambda x: own_rates(flow, coefficients, x, deep),
        lambda x: [rows_for_species(speed, species) for speed in own_speeds(flow, x, deep)],
        diffusivity, mix, emit_last,
    )
    for copy in copies.values():
        copy.wait()


def fourth_step_kernel(
    shape, counts, own_ref, edges, ends, _, field, x_one, x_other, flow, coefficients, mix_ref,
    out, edge, x_sides, ready, semaphores,
):
    wide, deep, species, up = shape
    rows, _ = counts
    even_x, row = own_ref[0] == 1, own_ref[2]
    inside = (row > 0, row < rows - 1)
    diffusivity, mix = coefficients[0][None], mixing(mix_ref[...])
    def beside(side, rows_of, cells=range(deep)):
        return jnp.stack(
            [choose(even_x, x_one, x_other, side, rows_of(cell, species)) for cell in cells]
        )

    def corners(side):
        return [beside(side, rows_of, [deep])[0] for rows_of in (outer_of, inner_of)]

    def last(side):
        return wide - 1 if side else 0

    def y_beside(side, to):
        here, corner = beside(side, outer_of), corners(side)[to][None]
        return jnp.concatenate([here[1:], corner] if to else [corner, here[:-1]], axis=0)

    def other_rows(side):
        return [
            choose(even_x, x_one, x_other, side, flow_of(y, deep + 1, species)) for y in range(deep)
        ]

    def emit(side, plane):
        x_sides[side] = jnp.where(inside[side], plane, 0.0)

    planes_advanced(
        range(2), lambda side: beside(side, outer_of),
        lambda side, to: beside(side, inner_of) if side == to else field[last(side)],
        y_beside,
        lambda side: jnp.stack(
            [rate_of(rows[3:4], coefficients) for rows in other_rows(side)]
        ),
        lambda side: [
            rows_for_species([rows[d : d + 1] for rows in other_rows(side)], species)
            for d in range(3)
        ],
        diffusivity, mix, emit,
    )
    for side in range(2):
        x = last(side)
        low, high = corners(side)
        value = jnp.concatenate([low[None], beside(side, outer_of), high[None]], axis=0)
        speed = rows_for_species(
            [ends[side, 0, 0:1]] + own_speeds(flow, x, deep)[0] + [ends[side, 1, 0:1]], species
        )
        edge[side] = edges[5 * side] + from_beyond(value, side, speed, diffusivity)

    def plane_of(x):
        if x < 0 or x >= wide:
            return x_sides[0 if x < 0 else 1]
        if x == 0 or x == wide - 1:
            return edge[0 if x == 0 else 1, 1 : deep + 1]
        return edges[x if x < 3 else x - wide + 6, 1 : deep + 1]

    def y_of(x, side):
        at = slice(2 * side, 2 * side + deep)
        if x in (0, wide - 1):
            return edge[0 if x == 0 else 1, at]
        return edges[x if x < 3 else x - wide + 6, at]

    outermost = [0, 1, wide - 2, wide - 1]
    copies = planes_copied([outermost[:2], outermost[2:]], ready, out, semaphores)

    def emit_last(x, plane):
        ready[:, outermost.index(x)] = jnp.swapaxes(plane, 0, 1)
        if x in copies:
            copies[x].start()

    planes_advanced(
        outermost, plane_of, lambda x, side: plane_of(x + 2 * side - 1), y_of,
        lambda x: own_rates(flow, coefficients, x, deep),
        lambda x: [rows_for_species(speed, species) for speed in own_speeds(flow, x, deep)],
        diffusivity, mix, emit_last,
    )
    for copy in copies.values():
        copy.wait()


def project_kernel(shape, ranks, field, component, vertical, factor_rows, out):
    wide, deep, species, up = shape
    ranks_a, ranks_d = ranks
    each = deep + 2
    cells = [field[x, y] for y in range(deep) for x in range(wide)]
    high, low = halves_of(jnp.concatenate(cells, axis=0))
    both = jnp.concatenate([high, low], axis=1)
    high, low = halves_of(vertical[...])
    left = jnp.concatenate(
        [jnp.concatenate([high, high], axis=1), jnp.concatenate([low, low], axis=1)], axis=0
    )
    on_d = lax.dot_general(
        left, both, (((1,), (1,)), ((), ())), preferred_element_type=jnp.float32
    )
    on_d = on_d[:ranks_d] + on_d[ranks_d:]
    size = wide * species
    on_d = jnp.concatenate([on_d[:, y * size : (y + 1) * size] for y in range(deep)], axis=0)
    on_both = product(on_d, component[...], (1, 1))
    for y in range(deep):
        out[pl.ds(y, ranks_d, stride=each), :] = on_both[y * ranks_d : (y + 1) * ranks_d]
    for row in range(2):
        out[pl.ds(deep + row, ranks_d, stride=each), :] = jnp.broadcast_to(
            factor_rows[row : row + 1], (ranks_d, 128)
        )


def core_kernel(counts, got, out):
    rows, columns, ranks_a, tall, deep = counts
    devices, each = rows * columns, deep + 2
    own = 128 // ranks_a

    whole = jnp.concatenate(
        [
            jnp.concatenate(
                [got[pl.ds((row * columns + column) * each, deep), :] for column in range(columns)],
                axis=0,
            )
            for row in range(rows)
        ],
        axis=1,
    )

    def in_order(at, of_row):
        both = got[pl.ds(at, devices, stride=each), :]
        halves = jnp.concatenate([both[:, :64], both[:, 64:]], axis=0)
        pick = jnp.full((2 * devices, 2 * devices), 1.0, jnp.float32)
        return product(where_equal(pick, of_row, lambda at: at), halves, (1, 0))

    east = in_order(deep, lambda at: at % 2 * devices + at // 2)
    north = in_order(
        deep + 1, lambda at: at % 2 * devices + at % deep // 2 * columns + at // deep
    )

    def by_rank(array):
        return jnp.concatenate(
            [
                jnp.concatenate(
                    [
                        array[(row * ranks_a + a) * own : (row * ranks_a + a + 1) * own]
                        for row in range(rows)
                    ],
                    axis=0,
                )
                for a in range(ranks_a)
            ],
            axis=1,
        )

    def by_row(parts):
        return jnp.concatenate(
            [
                parts[a][row * own : (row + 1) * own]
                for row in range(rows)
                for a in range(ranks_a)
            ],
            axis=0,
        ).T

    half = by_rank(product(whole, north, (0, 0)))
    core = product(east, half, (0, 0))
    half = product(east, core, (1, 0))
    ranks_c = north.shape[1]
    split = [slice(a * ranks_c, (a + 1) * ranks_c) for a in range(ranks_a)]
    core = by_row([core[:, at] for at in split])
    whole = by_row([product(half[:, at], north, (1, 1)) for at in split])
    for row in range(rows):
        for column in range(columns):
            at = row * columns + column
            out[at, 0:tall] = core[column * tall : (column + 1) * tall, row * 128 : (row + 1) * 128]
            out[at, tall : tall + deep] = whole[
                column * deep : (column + 1) * deep, row * 128 : (row + 1) * 128
            ]


def expand_kernel(shape, ranks, tall, got, field, wide_rows, vertical, residual, core, full):
    wide, deep, species, up = shape
    ranks_a, ranks_d = ranks
    each = tall + deep
    component = where_equal(
        jnp.concatenate([wide_rows[...]] * wide, axis=0),
        lambda at: at // species,
        lambda at: at % wide,
    )
    for y in range(deep):
        on_d = got[pl.ds(tall + y, ranks_d, stride=each), :]
        on_a = product(on_d, vertical[...], (0, 0))
        full[y] = product(component, on_a, (1, 0))
    for x in range(wide):
        residual[:, x] = jnp.swapaxes(
            field[x] - full[:, x * species : (x + 1) * species, :], 0, 1
        )
    turned = [got[pl.ds(c, ranks_d, stride=each), :].T for c in range(tall)]
    core[...] = jnp.swapaxes(jnp.stack(turned), 0, 1)


def swapped(one, other, axes):
    got = []
    for first, face in enumerate((one, other)):
        couples = [(i, i + 1) for i in range(first, lax.axis_size(axes) - 1, 2)]
        got.append(lax.ppermute(face, axes, couples + [(b, a) for a, b in couples]))
    return got


def faces_beside(faces):
    x_one, x_other, y_one, y_other = faces
    y_one, y_other = swapped(y_one, y_other, COLUMN)
    x_one, x_other = swapped(x_one, x_other, ROW)
    return x_one, x_other, y_one, y_other


def whole_factors(tucker_factor_east, tucker_factor_north):
    rows, columns = lax.axis_size(ROW), lax.axis_size(COLUMN)

    def shares(factor, holders, axes):
        count = -(-factor.shape[0] // holders)
        padded = jnp.pad(factor, ((0, count * holders - factor.shape[0]), (0, 0)))
        return lax.dynamic_slice_in_dim(padded, lax.axis_index(axes) * count, count, 0)

    east = shares(tucker_factor_east, columns, COLUMN)
    north = shares(tucker_factor_north, rows, ROW)
    sent = jnp.concatenate([east.reshape(-1), north.reshape(-1)])
    sent = jnp.pad(sent, (0, -sent.size % 128)).reshape(1, -1, 128)
    sent = jnp.broadcast_to(sent, (rows * columns,) + sent.shape[1:])
    got = lax.all_to_all(sent, EVERY, 0, 0, tiled=True).reshape(rows, columns, -1)
    whole_east = got[:, :, : east.size].reshape(rows, -1, east.shape[1])
    whole_east = whole_east[:, : tucker_factor_east.shape[0]].reshape(-1, east.shape[1])
    whole_north = got[:, :, east.size : east.size + north.size]
    whole_north = whole_north.reshape(rows, columns, *north.shape).transpose(1, 0, 2, 3)
    whole_north = whole_north.reshape(columns, -1, north.shape[1])
    whole_north = whole_north[:, : tucker_factor_north.shape[0]].reshape(-1, north.shape[1])
    return whole_east, whole_north


def compress_and_expand(snapshot, east, north, vertical, component):
    rows, columns = lax.axis_size(ROW), lax.axis_size(COLUMN)
    devices = rows * columns
    (wide, deep, _, _), (_, ranks_a) = snapshot.shape, component.shape
    ranks_d = vertical.shape[1]
    ranks_b, ranks_c = east.shape[1], north.shape[1]
    projected = jnp.einsum("xysz,sa->xyaz", snapshot, component, precision=HIGHEST)
    projected = jnp.einsum("xyaz,zd->dyxa", projected, vertical, precision=HIGHEST)
    pairs = ranks_a * ranks_d
    share = -(-pairs // devices)
    flat = jnp.transpose(projected, (0, 3, 1, 2)).reshape(pairs, deep, wide)
    flat = jnp.pad(flat, ((0, share * devices - pairs), (0, 0), (0, 0)))
    flat = flat.reshape(devices, share, deep, wide).transpose(0, 2, 3, 1)
    flat = lax.all_to_all(
        flat.reshape(devices, deep, wide * share), EVERY, 0, 0, tiled=True
    )
    whole = flat.reshape(rows, columns * deep, wide, share)
    part = jnp.einsum("gyxp,yc->cgxp", whole, north, precision=HIGHEST)
    part = part.reshape(ranks_c, rows * wide, share)
    core = jnp.einsum("cxp,xb->cbp", part, east, precision=HIGHEST)
    part = jnp.einsum("cbp,xb->cxp", core, east, precision=HIGHEST)
    whole = jnp.einsum("cxp,yc->yxp", part, north, precision=HIGHEST)
    own_b, own_c = ranks_b // rows, ranks_c // columns

    def pieces(array, tall, broad):
        array = array.reshape(columns, tall, rows, broad, share)
        return array.transpose(2, 0, 1, 3, 4).reshape(devices, tall * broad * share)

    sent = jnp.concatenate([pieces(core, own_c, own_b), pieces(whole, deep, wide)], axis=1)
    sent = jnp.pad(sent, ((0, 0), (0, -sent.shape[1] % 1024)))
    got = lax.all_to_all(
        sent.reshape(devices, -1, 128), EVERY, 0, 0, tiled=True
    ).reshape(devices, -1)

    def ranks_together(array, tall, broad):
        array = array.reshape(devices, tall, broad, share).transpose(0, 3, 2, 1)
        array = array.reshape(devices * share, broad, tall)[:pairs]
        return array.reshape(ranks_d, ranks_a, broad, tall)

    core_size = own_c * own_b * share
    core = ranks_together(got[:, :core_size], own_c, own_b).transpose(1, 2, 3, 0)
    expanded = ranks_together(got[:, core_size : core_size + deep * wide * share], deep, wide)
    expanded = jnp.einsum("daxy,zd->axyz", expanded, vertical, precision=HIGHEST)
    expanded = jnp.einsum("axyz,sa->sxyz", expanded, component, precision=HIGHEST)
    return core, snapshot.transpose(2, 0, 1, 3) - expanded


def body(
    mixture_fields_initial,
    flow_speed_vector,
    thermal_field,
    mass_diffusivity,
    arrhenius_constant,
    arrhenius_energy_temp,
    production_coefficients,
    tucker_factor_east,
    tucker_factor_north,
    tucker_factor_vertical,
    tucker_factor_component,
):
    species, wide, deep, up = mixture_fields_initial.shape
    shape = (wide, deep, species, up)
    cells = wide * deep * species * up
    rows, columns = lax.axis_size(ROW), lax.axis_size(COLUMN)
    devices = rows * columns
    ranks_a, ranks_d = tucker_factor_component.shape[1], tucker_factor_vertical.shape[1]
    ranks_b, ranks_c = tucker_factor_east.shape[1], tucker_factor_north.shape[1]
    own_b, own_c = ranks_b // rows, ranks_c // columns
    kernels_fit = (
        ranks_d == devices
        and wide * ranks_a == 128
        and own_b * ranks_a == 128
        and deep == own_c == 8
        and ranks_b == ranks_c == 64
        and wide == 2 * columns
        and deep == 2 * rows
    )

    row, column = lax.axis_index(ROW), lax.axis_index(COLUMN)
    own = jnp.stack([1 - row % 2, 1 - column % 2, row, column]).astype(jnp.int32)
    face_shapes = [(deep, species, up)] * 2 + [(wide, species, up)] * 2
    field_rows = mixture_fields_initial.reshape(species * wide * deep, up)
    faces = vmem_call(functools.partial(faces_kernel, shape), face_shapes, 1, 2)(own, field_rows)
    faces = faces_beside(faces)
    out_shapes = [
        shape, shape, (4, wide, deep, up), (3, species, up), (species, 128),
        (wide * ranks_a, wide * species), (species, wide * ranks_a), (ranks_d, up),
    ] + [(2, 128)] * kernels_fit
    small = (
        flow_speed_vector, thermal_field, mass_diffusivity[None], arrhenius_constant[None],
        arrhenius_energy_temp[None], production_coefficients,
        tucker_factor_component.T, tucker_factor_vertical.T, tucker_factor_east,
        tucker_factor_north,
    )
    vmem, smem = (pl.BlockSpec(memory_space=space) for space in (pltpu.VMEM, pltpu.SMEM))
    (field, rates, speeds, coefficients, mix, squeeze, wide_rows, upright,
     *factor_rows) = pl.pallas_call(
        functools.partial(prepare_kernel, shape, (ranks_a, ranks_d)),
        in_specs=[smem, vmem] + [pl.BlockSpec(memory_space=pltpu.HBM)] * len(small),
        out_specs=[vmem] * len(out_shapes),
        out_shape=[jax.ShapeDtypeStruct(out, jnp.float32) for out in out_shapes],
        scratch_shapes=[pltpu.VMEM(array.shape, jnp.float32) for array in small]
        + [pltpu.SemaphoreType.DMA((len(small),))],
        compiler_params=pltpu.CompilerParams(vmem_limit_bytes=VMEM_LIMIT),
        cost_estimate=pl.CostEstimate(
            flops=4 * cells, bytes_accessed=12 * cells, transcendentals=cells
        ),
    )(
        own, mixture_fields_initial,
        *(pltpu.with_memory_space_constraint(array, pltpu.HBM) for array in small),
    )
    block = vmem_call(
        functools.partial(block_kernel, shape), [shape], 0, 5, flops=60 * cells, moved=8 * cells
    )
    advance = vmem_call(
        functools.partial(advance_kernel, shape), [shape] + face_shapes, 1, 8,
        flops=4 * cells, moved=8 * cells,
    )
    fixed = (rates, speeds, coefficients, mix)
    for substep in range(SUB - 1):
        field, *faces = advance(
            own, *block(field, *fixed), *faces, speeds, coefficients
        )
        faces = faces_beside(faces)
    high = 2 * species + 4
    snapshot, *y_faces = vmem_call(
        functools.partial(snapshot_kernel, shape), [shape] + [(wide * high + 64, up)] * 2, 1, 8,
        flops=4 * cells, moved=8 * cells,
    )(own, *block(field, *fixed), *faces, speeds, coefficients)
    y_faces = swapped(*y_faces, COLUMN)
    x_faces = vmem_call(
        functools.partial(wide_faces_kernel, shape), [((deep + 1) * high + 36, up)] * 2, 1, 5,
        flops=cells, moved=cells,
    )(own, snapshot, *y_faces, speeds)
    x_faces = swapped(*x_faces, ROW)
    if kernels_fit:
        (sent,) = vmem_call(
            functools.partial(project_kernel, shape, (ranks_a, ranks_d)),
            [(devices * (deep + 2), 128)], 0, 4, flops=60 * cells, moved=4 * cells,
        )(snapshot, squeeze, upright, *factor_rows)
        got = lax.all_to_all(
            sent.reshape(devices, (deep + 2) // 2, 2, 128), EVERY, 0, 0, tiled=True
        )
        (sent,) = vmem_call(
            functools.partial(core_kernel, (rows, columns, ranks_a, own_c, deep)),
            [(devices, own_c + deep, 128)], 0, 1, flops=60 * cells, moved=4 * cells,
        )(got.reshape(devices * (deep + 2), 128))
        got = lax.all_to_all(sent, EVERY, 0, 0, tiled=True)
        residual, tucker_core = vmem_call(
            functools.partial(expand_kernel, shape, (ranks_a, ranks_d), own_c),
            [mixture_fields_initial.shape, (ranks_a * own_b, own_c, ranks_d)], 0, 4,
            flops=60 * cells, moved=8 * cells,
            scratch=[(deep, wide * species, up)],
        )(
            got.reshape(devices * (own_c + deep), 128),
            snapshot,
            wide_rows,
            upright,
        )
        tucker_core = tucker_core.reshape(ranks_a, own_b, own_c, ranks_d)
    else:
        east, north = whole_factors(tucker_factor_east, tucker_factor_north)
        tucker_core, residual = compress_and_expand(
            snapshot, east, north, tucker_factor_vertical, tucker_factor_component
        )
    fixed = fixed[1:]
    edges, ends, inmost = vmem_call(
        functools.partial(third_step_kernel, shape, (rows, columns)),
        [(6, deep + 2, species, up), (2, 2, 8, up), mixture_fields_initial.shape], 1, 7,
        flops=120 * cells, moved=16 * cells,
        scratch=[(wide, deep + 2, species, up), (species, wide - 4, deep, up)], placed=[9],
        copies=-(-(wide - 4) // 4),
    )(own, snapshot, *y_faces, *fixed)
    own, _ = lax.optimization_barrier((own, tucker_core))
    (mixture_fields_final,) = vmem_call(
        functools.partial(fourth_step_kernel, shape, (rows, columns)),
        [mixture_fields_initial.shape], 1, 10,
        flops=60 * cells, moved=8 * cells,
        scratch=[(2, deep + 2, species, up), (2, deep, species, up), (species, 4, deep, up)],
        placed=[3, 10], copies=2, aliases={3: 0},
    )(own, edges, ends, inmost, snapshot, *x_faces, *fixed)
    return (mixture_fields_final, residual, tucker_core)


def solution(mesh):
    in_specs = (
        P(None, "gx", ("gy", "ga"), None),
        P(None, "gx", ("gy", "ga"), None),
        P("gx", ("gy", "ga"), None),
        P(),
        P(),
        P(),
        P(),
        P("gx", None),
        P(("gy", "ga"), None),
        P(),
        P(),
    )
    out_specs = (
        P(None, "gx", ("gy", "ga"), None),
        P(None, "gx", ("gy", "ga"), None),
        P(None, "gx", ("gy", "ga"), None),
    )
    return jax.shard_map(body, mesh=mesh, in_specs=in_specs, out_specs=out_specs, check_vma=False)
```

```python
import functools

import jax
import jax.numpy as jnp
from jax import lax
from jax.experimental import pallas as pl
from jax.experimental.pallas import tpu as pltpu
from jax.sharding import PartitionSpec as P

SUB = 2


time_step = 0.5

ROW = "gx"
COLUMN = ("gy", "ga")
EVERY = ("gx", "gy", "ga")
HIGHEST = lax.Precision.HIGHEST
VMEM_LIMIT = 4 * 1024 * 1024
FACE_COPIES = 4

SPARE_Y, SPARE_X = 24, 160


def vmem_call(
    kernel, outs, in_smem, n_in, flops=0, moved=0, exps=0, scratch=(), placed=(), copies=0, aliases={}
):
    vmem = pl.BlockSpec(memory_space=pltpu.VMEM)
    smem = pl.BlockSpec(memory_space=pltpu.SMEM)
    anywhere = pl.BlockSpec(memory_space=pl.ANY)
    ins = [smem] * in_smem + [vmem] * (n_in - in_smem)
    specs = [anywhere if at in placed else spec for at, spec in enumerate(ins + [vmem] * len(outs))]
    return pl.pallas_call(
        kernel,
        in_specs=specs[:n_in],
        out_specs=specs[n_in:],
        out_shape=[jax.ShapeDtypeStruct(shape, jnp.float32) for shape in outs],
        scratch_shapes=[pltpu.VMEM(shape, jnp.float32) for shape in scratch]
        + [pltpu.SemaphoreType.DMA((copies,))] * (copies > 0),
        input_output_aliases=aliases,
        compiler_params=pltpu.CompilerParams(vmem_limit_bytes=VMEM_LIMIT),
        cost_estimate=pl.CostEstimate(flops=flops, bytes_accessed=moved, transcendentals=exps),
    )


def planes_of_species(ref, species, plane, at):
    return jnp.concatenate(
        [ref[pl.ds(first * plane + at, 8, stride=plane), :] for first in range(0, species, 8)], axis=0
    )


def store_planes_of_species(ref, species, plane, at, value):
    for first in range(0, species, 8):
        ref[pl.ds(first * plane + at, 8, stride=plane), :] = value[first : first + 8]


def faces_kernel(shape, own_ref, given, x_one, x_other, y_one, y_other, held, semaphores):
    wide, deep, species, up = shape
    even_x, even_y = own_ref[0] == 1, own_ref[1] == 1
    plane, together = wide * deep, -(-wide // FACE_COPIES)
    copies = {}
    for x in range(0, wide, together):
        some = pl.ds(x, min(together, wide - x))
        copies[x] = pltpu.make_async_copy(
            given.at[:, some], held.at[:, some], semaphores.at[x // together]
        )
        copies[x].start()
    rows = held.reshape(species * plane, up)
    for x in range(wide):
        if x in copies:
            copies[x].wait()
        low = planes_of_species(rows, species, plane, x * deep)
        high = planes_of_species(rows, species, plane, x * deep + deep - 1)
        y_one[x] = jnp.where(even_y, high, low)
        y_other[x] = jnp.where(even_y, low, high)
        if x in (0, wide - 1):
            face = jnp.swapaxes(held[:, x], 0, 1)
            to_one_or_other(even_x, x_one, x_other, x > 0, face)


def tiled(matrix, count):
    size = matrix.shape[1]
    column = lax.broadcasted_iota(jnp.int32, (size, size * count), 1) % size
    pick = (column == lax.broadcasted_iota(jnp.int32, (size, size * count), 0)).astype(jnp.float32)
    return jnp.dot(matrix, pick, precision=HIGHEST, preferred_element_type=jnp.float32)


def where_equal(matrix, of_row, of_column):
    row = lax.broadcasted_iota(jnp.int32, matrix.shape, 0)
    column = lax.broadcasted_iota(jnp.int32, matrix.shape, 1)
    return jnp.where(of_row(row) == of_column(column), matrix, 0.0)


def fetched(sources, held, semaphores):
    copies = [
        pltpu.make_async_copy(source, target, semaphores.at[at])
        for at, (source, target) in enumerate(zip(sources, held))
    ]
    for copy in copies:
        copy.start()
    return copies


def prepare_kernel(shape, given, *refs):
    wide, deep, species, up = shape
    held, semaphores = refs[-7:-1], refs[-1]
    copies = fetched(refs[:6], held, semaphores)
    flow, thermal, diffusivity, constant, energy, production = held
    field, rates, speeds, coefficients, mix = refs[6:-7]
    for x in range(wide):
        field[x] = jnp.swapaxes(given[:, x], 0, 1)
    for copy in copies:
        copy.wait()
    eye = (
        lax.broadcasted_iota(jnp.int32, (species, species), 0)
        == lax.broadcasted_iota(jnp.int32, (species, species), 1)
    )
    for at, ref in enumerate((diffusivity, constant, energy)):
        column = jnp.sum(jnp.where(eye, ref[...], 0.0), axis=1, keepdims=True)
        coefficients[at] = jnp.broadcast_to(time_step * column if at == 0 else column, (species, up))
    for x in range(wide):
        speeds[3, x] = thermal[x]
        inverse = -1.0 / thermal[x]
        for d in range(3):
            speeds[d, x] = (0.5 * time_step) * flow[d, x]
        for y in range(deep):
            rates[x, y] = coefficients[1] * jnp.exp(coefficients[2] * inverse[y : y + 1])
    mix[...] = tiled(time_step * production[...], mix.shape[1] // species)


def matrices_kernel(shape, own_ref, *refs):
    wide, _, species, _ = shape
    held, semaphores = refs[-5:-1], refs[-1]
    copies = fetched(refs[:4], held, semaphores)
    turned, vertical, east, north = held
    squeeze, wide_rows, upright, factor_rows = refs[4:-5]
    for copy in copies:
        copy.wait()
    ranks_a = turned.shape[0]
    full = tiled(turned[...], wide)
    full = [jnp.broadcast_to(full[a : a + 1], (wide, full.shape[1])) for a in range(ranks_a)]
    full = jnp.concatenate(full, axis=0)
    squeeze[...] = where_equal(full, lambda at: at % wide, lambda at: at // species)
    pick = lax.broadcasted_iota(jnp.int32, (ranks_a, ranks_a * wide), 1) // wide
    pick = pick == lax.broadcasted_iota(jnp.int32, pick.shape, 0)
    wide_rows[...] = lax.dot_general(
        turned[...], pick.astype(jnp.float32), (((0,), (0,)), ((), ())), precision=HIGHEST,
        preferred_element_type=jnp.float32,
    )
    upright[...] = vertical[...]

    def two_rows(ref, at):
        return jnp.concatenate([ref[pl.ds(2 * at + row, 1), :] for row in range(2)], axis=1)

    factor_rows[0:1] = two_rows(east, own_ref[3])
    factor_rows[1:2] = two_rows(north, own_ref[2])


def halves_of(value):
    high = value.astype(jnp.bfloat16)
    return high, (value - high.astype(jnp.float32)).astype(jnp.bfloat16)


def product(a, b, contract):
    def dot(left, right):
        return lax.dot_general(
            left, right, ((contract[:1], contract[1:]), ((), ())),
            preferred_element_type=jnp.float32,
        )

    (a_high, a_low), (b_high, b_low) = halves_of(a), halves_of(b)
    return dot(a_high, b_high) + (dot(a_high, b_low) + dot(a_low, b_high))


def mixing(rows):
    species, size = rows.shape
    full = jnp.concatenate([rows] * (size // species), axis=0)
    high, low = halves_of(
        where_equal(full, lambda at: at // species, lambda at: at // species)
    )
    return jnp.concatenate(
        [jnp.concatenate([high, high], axis=1), jnp.concatenate([low, low], axis=1)], axis=0
    )


def reacted(cells, mix):
    species, up = cells[0].shape
    size = mix.shape[0] // 2
    group = size // species
    cells = cells + [jnp.zeros_like(cells[0])] * (-len(cells) % group)
    right = []
    for at in range(0, len(cells), group):
        high, low = halves_of(jnp.concatenate(cells[at : at + group], axis=0))
        right.append(jnp.concatenate([high, low], axis=0))
    produced = jnp.dot(mix, jnp.concatenate(right, axis=1), preferred_element_type=jnp.float32)
    produced = produced[:size] + produced[size:]
    return [
        produced[cell * species : (cell + 1) * species, at * up : (at + 1) * up]
        for at in range(len(right))
        for cell in range(group)
    ]


def sources(here, rates):
    made = rates * here * pltpu.roll(here, here.shape[1] - 1, 1)
    return [made[cell] for cell in range(here.shape[0])]


def advanced(here, x_minus, x_plus, y_minus, y_plus, speeds, diffusivity, produced):
    up = here.shape[2]
    lane = lax.broadcasted_iota(jnp.int32, here.shape, 2)
    z_minus = jnp.where(lane == 0, 0.0, pltpu.roll(here, 1, 2))
    z_plus = jnp.where(lane == up - 1, 0.0, pltpu.roll(here, up - 1, 2))
    laplace = (x_plus + x_minus) + (y_plus + y_minus) + (z_plus + z_minus) - 6.0 * here
    advect = (
        speeds[0] * (x_plus - x_minus)
        + speeds[1] * (y_plus - y_minus)
        + speeds[2] * (z_plus - z_minus)
    )
    return here + diffusivity * laplace - advect + jnp.stack(produced)


def rows_for_species(rows, species):
    return jnp.stack([jnp.broadcast_to(row, (species, row.shape[1])) for row in rows])


def own_speeds(flow, x, deep):
    return [[flow[d, x, pl.ds(y, 1), :] for y in range(deep)] for d in range(3)]


def planes_advanced(planes, here, x_beside, y_beside, rates, speeds, diffusivity, mix, emit, together=4):
    for at in range(0, len(planes), together):
        some = planes[at : at + together]
        cells, counts = [], []
        for x in some:
            made = sources(here(x), rates(x))
            counts.append((len(cells), len(cells) + len(made)))
            cells += made
        produced = reacted(cells, mix)
        for x, (start, end) in zip(some, counts):
            emit(
                x,
                advanced(
                    here(x), x_beside(x, 0), x_beside(x, 1), y_beside(x, 0), y_beside(x, 1),
                    speeds(x), diffusivity, produced[start:end],
                ),
            )


def rate_of(temperature, coefficients):
    return coefficients[1] * jnp.exp(coefficients[2] * (-1.0 / temperature))


def own_rates(flow, coefficients, x, deep):
    inverse = -1.0 / flow[3, x]
    return jnp.stack(
        [coefficients[1] * jnp.exp(coefficients[2] * inverse[y : y + 1]) for y in range(deep)]
    )


def block_kernel(shape, held, field, *refs):
    wide, deep, species, up = shape
    rates, (flow, coefficients, mix_ref, out) = refs[0] if held else None, refs[held:]

    def x_beside(x, side):
        at = x + 2 * side - 1
        return field[at] if 0 <= at < wide else jnp.zeros((deep, species, up), jnp.float32)

    def y_beside(x, side):
        here, none = field[x], jnp.zeros((1, species, up), jnp.float32)
        return jnp.concatenate([here[1:], none] if side else [none, here[:-1]], axis=0)

    def emit(x, plane):
        out[x] = plane

    planes_advanced(
        range(wide), lambda x: field[x], x_beside, y_beside,
        lambda x: rates[x] if held else own_rates(flow, coefficients, x, deep),
        lambda x: [rows_for_species(speed, species) for speed in own_speeds(flow, x, deep)],
        coefficients[0][None], mixing(mix_ref[...]), emit,
    )


def from_beyond(value, side, speed, diffusivity):
    across = speed * value
    return diffusivity * value - across if side else diffusivity * value + across


def finish(shape, refs, emit):
    wide, deep, species, up = shape
    own_ref, block, x_one, x_other, y_one, y_other, flow, coefficients = refs
    even_x, even_y = own_ref[0] == 1, own_ref[1] == 1
    diffusivity = coefficients[0][None]

    def row(d, x, y):
        return jnp.broadcast_to(flow[d, x, pl.ds(y, 1), :], (species, up))

    for x in range(wide):
        plane = block[x]
        before = jnp.where(even_y, y_other[x], y_one[x])
        after = jnp.where(even_y, y_one[x], y_other[x])
        before = from_beyond(before, 0, row(1, x, 0), diffusivity[0])
        after = from_beyond(after, 1, row(1, x, deep - 1), diffusivity[0])
        plane = jnp.concatenate(
            [(plane[0] + before)[None], plane[1:-1], (plane[-1] + after)[None]], axis=0
        )
        for side in range(2):
            if x == (wide - 1 if side else 0):
                one, other = (x_one, x_other) if side else (x_other, x_one)
                value = jnp.where(even_x, one[...], other[...])
                speed = rows_for_species(own_speeds(flow, x, deep)[0], species)
                plane = plane + from_beyond(value, side, speed, diffusivity)
        emit(x, plane)


def to_one_or_other(even, one, other, high, value):
    first = even if high else jnp.logical_not(even)

    @pl.when(first)
    def _():
        one[...] = value

    @pl.when(jnp.logical_not(first))
    def _():
        other[...] = value


def advance_kernel(shape, *refs):
    wide, deep, _, _ = shape
    own_ref, (out, x_one, x_other, y_one, y_other) = refs[0], refs[8:]
    even_x, even_y = own_ref[0] == 1, own_ref[1] == 1

    def emit(x, plane):
        out[x] = plane
        low, high = plane[0], plane[deep - 1]
        y_one[x] = jnp.where(even_y, high, low)
        y_other[x] = jnp.where(even_y, low, high)
        if x == 0:
            to_one_or_other(even_x, x_one, x_other, False, plane)
        if x == wide - 1:
            to_one_or_other(even_x, x_one, x_other, True, plane)

    finish(shape, refs[:8], emit)


def outer_of(cell, species):
    return slice(2 * cell * species, (2 * cell + 1) * species)


def inner_of(cell, species):
    return slice((2 * cell + 1) * species, (2 * cell + 2) * species)


def flow_of(cell, count, species):
    return slice(2 * count * species + 4 * cell, 2 * count * species + 4 * cell + 4)


def snapshot_kernel(shape, *refs):
    wide, deep, species, _ = shape
    own_ref, flow, (out, y_one, y_other) = refs[0], refs[6], refs[8:]
    even_y = own_ref[1] == 1

    def emit(x, plane):
        out[x] = plane

        def put(low, high, at):
            y_one[at] = jnp.where(even_y, high, low)
            y_other[at] = jnp.where(even_y, low, high)

        def others(y):
            return jnp.concatenate([flow[d, x, pl.ds(y, 1), :] for d in range(4)], axis=0)

        put(plane[0], plane[deep - 1], outer_of(x, species))
        put(plane[1], plane[deep - 2], inner_of(x, species))
        put(others(0), others(deep - 1), flow_of(x, wide, species))

    finish(shape, refs[:8], emit)


def wide_faces_kernel(shape, own_ref, field, y_one, y_other, flow, x_one, x_other):
    wide, deep, species, _ = shape
    even_x, even_y = own_ref[0] == 1, own_ref[1] == 1

    def face(outer, inner, out):
        for y in range(deep):
            out[outer_of(y, species)] = field[outer, y]
            out[inner_of(y, species)] = field[inner, y]
            out[flow_of(y, deep + 1, species)] = jnp.concatenate(
                [flow[d, outer, y : y + 1, :] for d in range(4)], axis=0
            )
        at = outer_of(outer, species)
        out[outer_of(deep, species)] = choose(even_y, y_one, y_other, 0, at)
        out[inner_of(deep, species)] = choose(even_y, y_one, y_other, 1, at)

    @pl.when(even_x)
    def _():
        face(wide - 1, wide - 2, x_one)
        face(0, 1, x_other)

    @pl.when(jnp.logical_not(even_x))
    def _():
        face(0, 1, x_one)
        face(wide - 1, wide - 2, x_other)


def planes_copied(groups, ready, out, semaphores):
    copies, at = {}, 0
    for group in groups:
        copies[group[-1]] = pltpu.make_async_copy(
            ready.at[:, pl.ds(at, len(group))],
            out.at[:, pl.ds(group[0], len(group))],
            semaphores.at[len(copies)],
        )
        at += len(group)
    return copies


def choose(even, one, other, side, at):
    first, second = (one, other) if side else (other, one)
    return jnp.where(even, first[at], second[at])


def third_step_kernel(
    shape, counts, own_ref, block, field, y_one, y_other, flow, coefficients, mix_ref, edges, ends,
    out, inner, ready, semaphores,
):
    wide, deep, species, up = shape
    _, columns = counts
    even_y, column = own_ref[1] == 1, own_ref[3]
    inside = (column > 0, column < columns - 1)
    diffusivity, mix = coefficients[0][None], mixing(mix_ref[...])

    def outer(side, x):
        return choose(even_y, y_one, y_other, side, outer_of(x, species))

    def others(side, x):
        return choose(even_y, y_one, y_other, side, flow_of(x, wide, species))

    def here(x):
        return jnp.stack([outer(0, x), outer(1, x)])

    def x_beside(x, side):
        at = x + 2 * side - 1
        return here(at) if 0 <= at < wide else jnp.zeros((2, species, up), jnp.float32)

    def y_beside(x, side):
        beyond = choose(even_y, y_one, y_other, side, inner_of(x, species))
        return jnp.stack([field[x, 0], beyond] if side else [beyond, field[x, deep - 1]])

    def emit(x, plane):
        for side in range(2):
            inner[x, side * (deep + 1)] = jnp.where(inside[side], plane[side], 0.0)

    planes_advanced(
        range(wide), here, x_beside, y_beside,
        lambda x: jnp.stack([rate_of(others(side, x)[3:4], coefficients) for side in range(2)]),
        lambda x: [
            rows_for_species([others(side, x)[d : d + 1] for side in range(2)], species)
            for d in range(3)
        ],
        diffusivity, mix, emit, 16,
    )

    def row(x, y):
        return jnp.broadcast_to(flow[1, x, pl.ds(y, 1), :], (species, up))

    for x in range(wide):
        inner[x, 1] = block[x, 0] + from_beyond(outer(0, x), 0, row(x, 0), diffusivity[0])
        inner[x, 2:deep] = block[x, 1 : deep - 1]
        inner[x, deep] = block[x, deep - 1] + from_beyond(
            outer(1, x), 1, row(x, deep - 1), diffusivity[0]
        )
        if x < 3 or x >= wide - 3:
            edges[x if x < 3 else x - wide + 6] = inner[x]
        if x in (0, wide - 1):
            for side in range(2):
                ends[0 if x == 0 else 1, side, 0:4] = others(side, x)

    inmost = range(2, wide - 2)
    copies = planes_copied(
        [inmost[at : at + 4] for at in range(0, len(inmost), 4)], ready, out, semaphores
    )

    def emit_last(x, plane):
        ready[:, x - 2] = jnp.swapaxes(plane, 0, 1)
        if x in copies:
            copies[x].start()

    planes_advanced(
        inmost,
        lambda x: inner[x, 1 : deep + 1],
        lambda x, side: inner[x + 2 * side - 1, 1 : deep + 1],
        lambda x, side: inner[x, 2 * side : 2 * side + deep],
        lambda x: own_rates(flow, coefficients, x, deep),
        lambda x: [rows_for_species(speed, species) for speed in own_speeds(flow, x, deep)],
        diffusivity, mix, emit_last,
    )
    for copy in copies.values():
        copy.wait()


def fourth_step_kernel(
    shape, counts, own_ref, edges, ends, _, field, x_one, x_other, flow, coefficients, mix_ref,
    out, edge, x_sides, ready, semaphores,
):
    wide, deep, species, up = shape
    rows, _ = counts
    even_x, row = own_ref[0] == 1, own_ref[2]
    inside = (row > 0, row < rows - 1)
    diffusivity, mix = coefficients[0][None], mixing(mix_ref[...])
    def beside(side, rows_of, cells=range(deep)):
        return jnp.stack(
            [choose(even_x, x_one, x_other, side, rows_of(cell, species)) for cell in cells]
        )

    def corners(side):
        return [beside(side, rows_of, [deep])[0] for rows_of in (outer_of, inner_of)]

    def last(side):
        return wide - 1 if side else 0

    def y_beside(side, to):
        here, corner = beside(side, outer_of), corners(side)[to][None]
        return jnp.concatenate([here[1:], corner] if to else [corner, here[:-1]], axis=0)

    def other_rows(side):
        return [
            choose(even_x, x_one, x_other, side, flow_of(y, deep + 1, species)) for y in range(deep)
        ]

    def emit(side, plane):
        x_sides[side] = jnp.where(inside[side], plane, 0.0)

    planes_advanced(
        range(2), lambda side: beside(side, outer_of),
        lambda side, to: beside(side, inner_of) if side == to else field[last(side)],
        y_beside,
        lambda side: jnp.stack(
            [rate_of(rows[3:4], coefficients) for rows in other_rows(side)]
        ),
        lambda side: [
            rows_for_species([rows[d : d + 1] for rows in other_rows(side)], species)
            for d in range(3)
        ],
        diffusivity, mix, emit,
    )
    for side in range(2):
        x = last(side)
        low, high = corners(side)
        value = jnp.concatenate([low[None], beside(side, outer_of), high[None]], axis=0)
        speed = rows_for_species(
            [ends[side, 0, 0:1]] + own_speeds(flow, x, deep)[0] + [ends[side, 1, 0:1]], species
        )
        edge[side] = edges[5 * side] + from_beyond(value, side, speed, diffusivity)

    def plane_of(x):
        if x < 0 or x >= wide:
            return x_sides[0 if x < 0 else 1]
        if x == 0 or x == wide - 1:
            return edge[0 if x == 0 else 1, 1 : deep + 1]
        return edges[x if x < 3 else x - wide + 6, 1 : deep + 1]

    def y_of(x, side):
        at = slice(2 * side, 2 * side + deep)
        if x in (0, wide - 1):
            return edge[0 if x == 0 else 1, at]
        return edges[x if x < 3 else x - wide + 6, at]

    outermost = [0, 1, wide - 2, wide - 1]
    copies = planes_copied([outermost[:2], outermost[2:]], ready, out, semaphores)

    def emit_last(x, plane):
        ready[:, outermost.index(x)] = jnp.swapaxes(plane, 0, 1)
        if x in copies:
            copies[x].start()

    planes_advanced(
        outermost, plane_of, lambda x, side: plane_of(x + 2 * side - 1), y_of,
        lambda x: own_rates(flow, coefficients, x, deep),
        lambda x: [rows_for_species(speed, species) for speed in own_speeds(flow, x, deep)],
        diffusivity, mix, emit_last,
    )
    for copy in copies.values():
        copy.wait()


def project_kernel(shape, ranks, field, component, vertical, factor_rows, out):
    wide, deep, species, up = shape
    ranks_a, ranks_d = ranks
    each = deep + 2
    cells = [field[x, y] for y in range(deep) for x in range(wide)]
    high, low = halves_of(jnp.concatenate(cells, axis=0))
    both = jnp.concatenate([high, low], axis=1)
    high, low = halves_of(vertical[...])
    left = jnp.concatenate(
        [jnp.concatenate([high, high], axis=1), jnp.concatenate([low, low], axis=1)], axis=0
    )
    on_d = lax.dot_general(
        left, both, (((1,), (1,)), ((), ())), preferred_element_type=jnp.float32
    )
    on_d = on_d[:ranks_d] + on_d[ranks_d:]
    size = wide * species
    on_d = jnp.concatenate([on_d[:, y * size : (y + 1) * size] for y in range(deep)], axis=0)
    on_both = product(on_d, component[...], (1, 1))
    for y in range(deep):
        out[pl.ds(y, ranks_d, stride=each), :] = on_both[y * ranks_d : (y + 1) * ranks_d]
    for row in range(2):
        out[pl.ds(deep + row, ranks_d, stride=each), :] = jnp.broadcast_to(
            factor_rows[row : row + 1], (ranks_d, 128)
        )


def core_kernel(counts, got, out):
    rows, columns, ranks_a, tall, deep = counts
    devices, each = rows * columns, deep + 2
    own = 128 // ranks_a

    whole = jnp.concatenate(
        [
            jnp.concatenate(
                [got[pl.ds((row * columns + column) * each, deep), :] for column in range(columns)],
                axis=0,
            )
            for row in range(rows)
        ],
        axis=1,
    )

    def in_order(at, of_row):
        both = got[pl.ds(at, devices, stride=each), :]
        halves = jnp.concatenate([both[:, :64], both[:, 64:]], axis=0)
        pick = jnp.full((2 * devices, 2 * devices), 1.0, jnp.float32)
        return product(where_equal(pick, of_row, lambda at: at), halves, (1, 0))

    east = in_order(deep, lambda at: at % 2 * devices + at // 2)
    north = in_order(
        deep + 1, lambda at: at % 2 * devices + at % deep // 2 * columns + at // deep
    )

    def by_rank(array):
        return jnp.concatenate(
            [
                jnp.concatenate(
                    [
                        array[(row * ranks_a + a) * own : (row * ranks_a + a + 1) * own]
                        for row in range(rows)
                    ],
                    axis=0,
                )
                for a in range(ranks_a)
            ],
            axis=1,
        )

    def by_row(parts):
        return jnp.concatenate(
            [
                parts[a][row * own : (row + 1) * own]
                for row in range(rows)
                for a in range(ranks_a)
            ],
            axis=0,
        ).T

    half = by_rank(product(whole, north, (0, 0)))
    core = product(east, half, (0, 0))
    half = product(east, core, (1, 0))
    ranks_c = north.shape[1]
    split = [slice(a * ranks_c, (a + 1) * ranks_c) for a in range(ranks_a)]
    core = by_row([core[:, at] for at in split])
    whole = by_row([product(half[:, at], north, (1, 1)) for at in split])
    for row in range(rows):
        for column in range(columns):
            at = row * columns + column
            out[at, 0:tall] = core[column * tall : (column + 1) * tall, row * 128 : (row + 1) * 128]
            out[at, tall : tall + deep] = whole[
                column * deep : (column + 1) * deep, row * 128 : (row + 1) * 128
            ]


def expand_kernel(shape, ranks, tall, got, field, wide_rows, vertical, residual, core, full):
    wide, deep, species, up = shape
    ranks_a, ranks_d = ranks
    each = tall + deep
    component = where_equal(
        jnp.concatenate([wide_rows[...]] * wide, axis=0),
        lambda at: at // species,
        lambda at: at % wide,
    )
    for y in range(deep):
        on_d = got[pl.ds(tall + y, ranks_d, stride=each), :]
        on_a = product(on_d, vertical[...], (0, 0))
        full[y] = product(component, on_a, (1, 0))
    for x in range(wide):
        residual[:, x] = jnp.swapaxes(
            field[x] - full[:, x * species : (x + 1) * species, :], 0, 1
        )
    turned = [got[pl.ds(c, ranks_d, stride=each), :].T for c in range(tall)]
    core[...] = jnp.swapaxes(jnp.stack(turned), 0, 1)


def swapped(one, other, axes):
    got = []
    for first, face in enumerate((one, other)):
        couples = [(i, i + 1) for i in range(first, lax.axis_size(axes) - 1, 2)]
        got.append(lax.ppermute(face, axes, couples + [(b, a) for a, b in couples]))
    return got


def faces_beside(faces):
    x_one, x_other, y_one, y_other = faces
    y_one, y_other = swapped(y_one, y_other, COLUMN)
    x_one, x_other = swapped(x_one, x_other, ROW)
    return x_one, x_other, y_one, y_other


def whole_factors(tucker_factor_east, tucker_factor_north):
    rows, columns = lax.axis_size(ROW), lax.axis_size(COLUMN)

    def shares(factor, holders, axes):
        count = -(-factor.shape[0] // holders)
        padded = jnp.pad(factor, ((0, count * holders - factor.shape[0]), (0, 0)))
        return lax.dynamic_slice_in_dim(padded, lax.axis_index(axes) * count, count, 0)

    east = shares(tucker_factor_east, columns, COLUMN)
    north = shares(tucker_factor_north, rows, ROW)
    sent = jnp.concatenate([east.reshape(-1), north.reshape(-1)])
    sent = jnp.pad(sent, (0, -sent.size % 128)).reshape(1, -1, 128)
    sent = jnp.broadcast_to(sent, (rows * columns,) + sent.shape[1:])
    got = lax.all_to_all(sent, EVERY, 0, 0, tiled=True).reshape(rows, columns, -1)
    whole_east = got[:, :, : east.size].reshape(rows, -1, east.shape[1])
    whole_east = whole_east[:, : tucker_factor_east.shape[0]].reshape(-1, east.shape[1])
    whole_north = got[:, :, east.size : east.size + north.size]
    whole_north = whole_north.reshape(rows, columns, *north.shape).transpose(1, 0, 2, 3)
    whole_north = whole_north.reshape(columns, -1, north.shape[1])
    whole_north = whole_north[:, : tucker_factor_north.shape[0]].reshape(-1, north.shape[1])
    return whole_east, whole_north


def compress_and_expand(snapshot, east, north, vertical, component):
    rows, columns = lax.axis_size(ROW), lax.axis_size(COLUMN)
    devices = rows * columns
    (wide, deep, _, _), (_, ranks_a) = snapshot.shape, component.shape
    ranks_d = vertical.shape[1]
    ranks_b, ranks_c = east.shape[1], north.shape[1]
    projected = jnp.einsum("xysz,sa->xyaz", snapshot, component, precision=HIGHEST)
    projected = jnp.einsum("xyaz,zd->dyxa", projected, vertical, precision=HIGHEST)
    pairs = ranks_a * ranks_d
    share = -(-pairs // devices)
    flat = jnp.transpose(projected, (0, 3, 1, 2)).reshape(pairs, deep, wide)
    flat = jnp.pad(flat, ((0, share * devices - pairs), (0, 0), (0, 0)))
    flat = flat.reshape(devices, share, deep, wide).transpose(0, 2, 3, 1)
    flat = lax.all_to_all(
        flat.reshape(devices, deep, wide * share), EVERY, 0, 0, tiled=True
    )
    whole = flat.reshape(rows, columns * deep, wide, share)
    part = jnp.einsum("gyxp,yc->cgxp", whole, north, precision=HIGHEST)
    part = part.reshape(ranks_c, rows * wide, share)
    core = jnp.einsum("cxp,xb->cbp", part, east, precision=HIGHEST)
    part = jnp.einsum("cbp,xb->cxp", core, east, precision=HIGHEST)
    whole = jnp.einsum("cxp,yc->yxp", part, north, precision=HIGHEST)
    own_b, own_c = ranks_b // rows, ranks_c // columns

    def pieces(array, tall, broad):
        array = array.reshape(columns, tall, rows, broad, share)
        return array.transpose(2, 0, 1, 3, 4).reshape(devices, tall * broad * share)

    sent = jnp.concatenate([pieces(core, own_c, own_b), pieces(whole, deep, wide)], axis=1)
    sent = jnp.pad(sent, ((0, 0), (0, -sent.shape[1] % 1024)))
    got = lax.all_to_all(
        sent.reshape(devices, -1, 128), EVERY, 0, 0, tiled=True
    ).reshape(devices, -1)

    def ranks_together(array, tall, broad):
        array = array.reshape(devices, tall, broad, share).transpose(0, 3, 2, 1)
        array = array.reshape(devices * share, broad, tall)[:pairs]
        return array.reshape(ranks_d, ranks_a, broad, tall)

    core_size = own_c * own_b * share
    core = ranks_together(got[:, :core_size], own_c, own_b).transpose(1, 2, 3, 0)
    expanded = ranks_together(got[:, core_size : core_size + deep * wide * share], deep, wide)
    expanded = jnp.einsum("daxy,zd->axyz", expanded, vertical, precision=HIGHEST)
    expanded = jnp.einsum("axyz,sa->sxyz", expanded, component, precision=HIGHEST)
    return core, snapshot.transpose(2, 0, 1, 3) - expanded


def body(
    mixture_fields_initial,
    flow_speed_vector,
    thermal_field,
    mass_diffusivity,
    arrhenius_constant,
    arrhenius_energy_temp,
    production_coefficients,
    tucker_factor_east,
    tucker_factor_north,
    tucker_factor_vertical,
    tucker_factor_component,
):
    species, wide, deep, up = mixture_fields_initial.shape
    shape = (wide, deep, species, up)
    cells = wide * deep * species * up
    rows, columns = lax.axis_size(ROW), lax.axis_size(COLUMN)
    devices = rows * columns
    ranks_a, ranks_d = tucker_factor_component.shape[1], tucker_factor_vertical.shape[1]
    ranks_b, ranks_c = tucker_factor_east.shape[1], tucker_factor_north.shape[1]
    own_b, own_c = ranks_b // rows, ranks_c // columns
    kernels_fit = (
        ranks_d == devices
        and wide * ranks_a == 128
        and own_b * ranks_a == 128
        and deep == own_c == 8
        and ranks_b == ranks_c == 64
        and wide == 2 * columns
        and deep == 2 * rows
    )

    row, column = lax.axis_index(ROW), lax.axis_index(COLUMN)
    own = jnp.stack([1 - row % 2, 1 - column % 2, row, column]).astype(jnp.int32)
    face_shapes = [(deep, species, up)] * 2 + [(wide, species, up)] * 2
    faces = vmem_call(
        functools.partial(faces_kernel, shape), face_shapes, 1, 2,
        scratch=[mixture_fields_initial.shape], placed=[1], copies=FACE_COPIES,
    )(own, pltpu.with_memory_space_constraint(mixture_fields_initial, pltpu.HBM))
    faces = faces_beside(faces)
    def with_fetches(kernel, given, small, outs, **cost):
        call = vmem_call(
            kernel, outs, int(given is own), 1 + len(small),
            scratch=[array.shape for array in small], placed=range(1, 1 + len(small)),
            copies=len(small), **cost,
        )
        return call(
            given, *(pltpu.with_memory_space_constraint(array, pltpu.HBM) for array in small)
        )

    field, rates, speeds, coefficients, mix = with_fetches(
        functools.partial(prepare_kernel, shape),
        mixture_fields_initial,
        (
            flow_speed_vector, thermal_field, mass_diffusivity[None], arrhenius_constant[None],
            arrhenius_energy_temp[None], production_coefficients,
        ),
        [shape, shape, (4, wide, deep, up), (3, species, up), (species, 128)],
        flops=4 * cells, moved=12 * cells, exps=cells,
    )
    block, last_block = (
        vmem_call(
            functools.partial(block_kernel, shape, held), [shape], 0, 4 + held,
            flops=60 * cells, moved=8 * cells,
        )
        for held in (1, 0)
    )
    advance = vmem_call(
        functools.partial(advance_kernel, shape), [shape] + face_shapes, 1, 8,
        flops=4 * cells, moved=8 * cells,
    )
    fixed = (rates, speeds, coefficients, mix)
    for substep in range(SUB - 1):
        field, *faces = advance(
            own, *block(field, *fixed), *faces, speeds, coefficients
        )
        first = field
        faces = faces_beside(faces)
    high = 2 * species + 4
    snapshot, *y_faces = vmem_call(
        functools.partial(snapshot_kernel, shape), [shape] + [(wide * high + SPARE_Y, up)] * 2, 1, 8,
        flops=4 * cells, moved=8 * cells,
    )(own, *block(field, *fixed), *faces, speeds, coefficients)
    y_faces = swapped(*y_faces, COLUMN)
    if kernels_fit:
        own, _ = lax.optimization_barrier((own, first))
        squeeze, wide_rows, upright, *factor_rows = with_fetches(
            functools.partial(matrices_kernel, shape),
            own,
            (
                tucker_factor_component.T, tucker_factor_vertical.T, tucker_factor_east,
                tucker_factor_north,
            ),
            [
                (wide * ranks_a, wide * species), (species, wide * ranks_a), (ranks_d, up),
                (2, 128),
            ],
        )
        (sent,) = vmem_call(
            functools.partial(project_kernel, shape, (ranks_a, ranks_d)),
            [(devices * (deep + 2), 128)], 0, 4, flops=60 * cells, moved=4 * cells,
        )(snapshot, squeeze, upright, *factor_rows)
        got = lax.all_to_all(
            sent.reshape(devices, (deep + 2) // 2, 2, 128), EVERY, 0, 0, tiled=True
        )
        (sent,) = vmem_call(
            functools.partial(core_kernel, (rows, columns, ranks_a, own_c, deep)),
            [(devices, own_c + deep, 128)], 0, 1, flops=60 * cells, moved=4 * cells,
        )(got.reshape(devices * (deep + 2), 128))
        sent, later = lax.optimization_barrier((sent, snapshot))
        got = lax.all_to_all(sent, EVERY, 0, 0, tiled=True)
        residual, tucker_core = vmem_call(
            functools.partial(expand_kernel, shape, (ranks_a, ranks_d), own_c),
            [mixture_fields_initial.shape, (ranks_a * own_b, own_c, ranks_d)], 0, 4,
            flops=60 * cells, moved=8 * cells,
            scratch=[(deep, wide * species, up)],
        )(
            got.reshape(devices * (own_c + deep), 128),
            snapshot,
            wide_rows,
            upright,
        )
        tucker_core = tucker_core.reshape(ranks_a, own_b, own_c, ranks_d)
    else:
        east, north = whole_factors(tucker_factor_east, tucker_factor_north)
        tucker_core, residual = compress_and_expand(
            snapshot, east, north, tucker_factor_vertical, tucker_factor_component
        )
        later = snapshot
    fixed = fixed[1:]
    (third,) = last_block(later, *fixed)
    own_wide, third = lax.optimization_barrier((own, third))
    x_faces = vmem_call(
        functools.partial(wide_faces_kernel, shape),
        [((deep + 1) * high - 4 + spare, up) for spare in (SPARE_X, 0)], 1, 5,
        flops=cells, moved=cells,
    )(own_wide, snapshot, *y_faces, speeds)
    x_faces = swapped(*x_faces, ROW)
    edges, ends, inmost = vmem_call(
        functools.partial(third_step_kernel, shape, (rows, columns)),
        [(6, deep + 2, species, up), (2, 2, 8, up), mixture_fields_initial.shape], 1, 8,
        flops=120 * cells, moved=16 * cells,
        scratch=[(wide, deep + 2, species, up), (species, wide - 4, deep, up)], placed=[10],
        copies=-(-(wide - 4) // 4),
    )(own, third, snapshot, *y_faces, *fixed)
    own, _ = lax.optimization_barrier((own, tucker_core))
    (mixture_fields_final,) = vmem_call(
        functools.partial(fourth_step_kernel, shape, (rows, columns)),
        [mixture_fields_initial.shape], 1, 10,
        flops=60 * cells, moved=8 * cells,
        scratch=[(2, deep + 2, species, up), (2, deep, species, up), (species, 4, deep, up)],
        placed=[3, 10], copies=2, aliases={3: 0},
    )(own, edges, ends, inmost, snapshot, *x_faces, *fixed)
    return (mixture_fields_final, residual, tucker_core)


def solution(mesh):
    in_specs = (
        P(None, "gx", ("gy", "ga"), None),
        P(None, "gx", ("gy", "ga"), None),
        P("gx", ("gy", "ga"), None),
        P(),
        P(),
        P(),
        P(),
        P("gx", None),
        P(("gy", "ga"), None),
        P(),
        P(),
    )
    out_specs = (
        P(None, "gx", ("gy", "ga"), None),
        P(None, "gx", ("gy", "ga"), None),
        P(None, "gx", ("gy", "ga"), None),
    )
    return jax.shard_map(body, mesh=mesh, in_specs=in_specs, out_specs=out_specs, check_vma=False)
```

```python
import functools

import jax
import jax.numpy as jnp
from jax import lax
from jax.experimental import pallas as pl
from jax.experimental.pallas import tpu as pltpu
from jax.sharding import PartitionSpec as P

SUB = 2


time_step = 0.5

ROW = "gx"
COLUMN = ("gy", "ga")
EVERY = ("gx", "gy", "ga")
HIGHEST = lax.Precision.HIGHEST
VMEM_LIMIT = 4 * 1024 * 1024
FACE_COPIES = 4

SPARE_X = 104


def vmem_call(
    kernel, outs, in_smem, n_in, flops=0, moved=0, exps=0, scratch=(), placed=(), copies=0, aliases={}
):
    vmem = pl.BlockSpec(memory_space=pltpu.VMEM)
    smem = pl.BlockSpec(memory_space=pltpu.SMEM)
    anywhere = pl.BlockSpec(memory_space=pl.ANY)
    ins = [smem] * in_smem + [vmem] * (n_in - in_smem)
    specs = [anywhere if at in placed else spec for at, spec in enumerate(ins + [vmem] * len(outs))]
    return pl.pallas_call(
        kernel,
        in_specs=specs[:n_in],
        out_specs=specs[n_in:],
        out_shape=[jax.ShapeDtypeStruct(shape, jnp.float32) for shape in outs],
        scratch_shapes=[pltpu.VMEM(shape, jnp.float32) for shape in scratch]
        + [pltpu.SemaphoreType.DMA((copies,))] * (copies > 0),
        input_output_aliases=aliases,
        compiler_params=pltpu.CompilerParams(vmem_limit_bytes=VMEM_LIMIT),
        cost_estimate=pl.CostEstimate(flops=flops, bytes_accessed=moved, transcendentals=exps),
    )


def planes_of_species(ref, species, plane, at):
    return jnp.concatenate(
        [ref[pl.ds(first * plane + at, 8, stride=plane), :] for first in range(0, species, 8)], axis=0
    )


def store_planes_of_species(ref, species, plane, at, value):
    for first in range(0, species, 8):
        ref[pl.ds(first * plane + at, 8, stride=plane), :] = value[first : first + 8]


def faces_kernel(shape, own_ref, given, x_one, x_other, y_one, y_other, held, semaphores):
    wide, deep, species, up = shape
    even_x, even_y = own_ref[0] == 1, own_ref[1] == 1
    plane, together = wide * deep, -(-wide // FACE_COPIES)
    copies = {}
    for x in range(0, wide, together):
        some = pl.ds(x, min(together, wide - x))
        copies[x] = pltpu.make_async_copy(
            given.at[:, some], held.at[:, some], semaphores.at[x // together]
        )
        copies[x].start()
    rows = held.reshape(species * plane, up)
    for x in range(wide):
        if x in copies:
            copies[x].wait()
        low = planes_of_species(rows, species, plane, x * deep)
        high = planes_of_species(rows, species, plane, x * deep + deep - 1)
        y_one[x] = jnp.where(even_y, high, low)
        y_other[x] = jnp.where(even_y, low, high)
        if x in (0, wide - 1):
            face = jnp.swapaxes(held[:, x], 0, 1)
            to_one_or_other(even_x, x_one, x_other, x > 0, face)


def tiled(matrix, count):
    size = matrix.shape[1]
    column = lax.broadcasted_iota(jnp.int32, (size, size * count), 1) % size
    pick = (column == lax.broadcasted_iota(jnp.int32, (size, size * count), 0)).astype(jnp.float32)
    return jnp.dot(matrix, pick, precision=HIGHEST, preferred_element_type=jnp.float32)


def where_equal(matrix, of_row, of_column):
    row = lax.broadcasted_iota(jnp.int32, matrix.shape, 0)
    column = lax.broadcasted_iota(jnp.int32, matrix.shape, 1)
    return jnp.where(of_row(row) == of_column(column), matrix, 0.0)


def fetched(sources, held, semaphores):
    copies = [
        pltpu.make_async_copy(source, target, semaphores.at[at])
        for at, (source, target) in enumerate(zip(sources, held))
    ]
    for copy in copies:
        copy.start()
    return copies


def prepare_kernel(shape, given, *refs):
    wide, deep, species, up = shape
    held, semaphores = refs[-7:-1], refs[-1]
    copies = fetched(refs[:6], held, semaphores)
    flow, thermal, diffusivity, constant, energy, production = held
    field, rates, speeds, coefficients, mix = refs[6:-7]
    for x in range(wide):
        field[x] = jnp.swapaxes(given[:, x], 0, 1)
    for copy in copies:
        copy.wait()
    eye = (
        lax.broadcasted_iota(jnp.int32, (species, species), 0)
        == lax.broadcasted_iota(jnp.int32, (species, species), 1)
    )
    for at, ref in enumerate((diffusivity, constant, energy)):
        column = jnp.sum(jnp.where(eye, ref[...], 0.0), axis=1, keepdims=True)
        coefficients[at] = jnp.broadcast_to(time_step * column if at == 0 else column, (species, up))
    for x in range(wide):
        speeds[3, x] = thermal[x]
        inverse = -1.0 / thermal[x]
        for d in range(3):
            speeds[d, x] = (0.5 * time_step) * flow[d, x]
        for y in range(deep):
            rates[x, y] = coefficients[1] * jnp.exp(coefficients[2] * inverse[y : y + 1])
    mix[...] = tiled(time_step * production[...], mix.shape[1] // species)


def matrices_kernel(shape, own_ref, *refs):
    wide, _, species, _ = shape
    held, semaphores = refs[-5:-1], refs[-1]
    copies = fetched(refs[:4], held, semaphores)
    turned, vertical, east, north = held
    squeeze, wide_rows, upright, factor_rows = refs[4:-5]
    for copy in copies:
        copy.wait()
    ranks_a = turned.shape[0]
    full = tiled(turned[...], wide)
    full = [jnp.broadcast_to(full[a : a + 1], (wide, full.shape[1])) for a in range(ranks_a)]
    full = jnp.concatenate(full, axis=0)
    squeeze[...] = where_equal(full, lambda at: at % wide, lambda at: at // species)
    pick = lax.broadcasted_iota(jnp.int32, (ranks_a, ranks_a * wide), 1) // wide
    pick = pick == lax.broadcasted_iota(jnp.int32, pick.shape, 0)
    wide_rows[...] = lax.dot_general(
        turned[...], pick.astype(jnp.float32), (((0,), (0,)), ((), ())), precision=HIGHEST,
        preferred_element_type=jnp.float32,
    )
    upright[...] = vertical[...]

    def two_rows(ref, at):
        return jnp.concatenate([ref[pl.ds(2 * at + row, 1), :] for row in range(2)], axis=1)

    factor_rows[0:1] = two_rows(east, own_ref[3])
    factor_rows[1:2] = two_rows(north, own_ref[2])


def halves_of(value):
    high = value.astype(jnp.bfloat16)
    return high, (value - high.astype(jnp.float32)).astype(jnp.bfloat16)


def product(a, b, contract):
    def dot(left, right):
        return lax.dot_general(
            left, right, ((contract[:1], contract[1:]), ((), ())),
            preferred_element_type=jnp.float32,
        )

    (a_high, a_low), (b_high, b_low) = halves_of(a), halves_of(b)
    return dot(a_high, b_high) + (dot(a_high, b_low) + dot(a_low, b_high))


def mixing(rows):
    species, size = rows.shape
    full = jnp.concatenate([rows] * (size // species), axis=0)
    high, low = halves_of(
        where_equal(full, lambda at: at // species, lambda at: at // species)
    )
    return jnp.concatenate(
        [jnp.concatenate([high, high], axis=1), jnp.concatenate([low, low], axis=1)], axis=0
    )


def reacted(cells, mix):
    species, up = cells[0].shape
    size = mix.shape[0] // 2
    group = size // species
    cells = cells + [jnp.zeros_like(cells[0])] * (-len(cells) % group)
    right = []
    for at in range(0, len(cells), group):
        high, low = halves_of(jnp.concatenate(cells[at : at + group], axis=0))
        right.append(jnp.concatenate([high, low], axis=0))
    produced = jnp.dot(mix, jnp.concatenate(right, axis=1), preferred_element_type=jnp.float32)
    produced = produced[:size] + produced[size:]
    return [
        produced[cell * species : (cell + 1) * species, at * up : (at + 1) * up]
        for at in range(len(right))
        for cell in range(group)
    ]


def sources(here, rates):
    made = rates * here * pltpu.roll(here, here.shape[1] - 1, 1)
    return [made[cell] for cell in range(here.shape[0])]


def advanced(here, x_minus, x_plus, y_minus, y_plus, speeds, diffusivity, produced):
    up = here.shape[2]
    lane = lax.broadcasted_iota(jnp.int32, here.shape, 2)
    z_minus = jnp.where(lane == 0, 0.0, pltpu.roll(here, 1, 2))
    z_plus = jnp.where(lane == up - 1, 0.0, pltpu.roll(here, up - 1, 2))
    laplace = (x_plus + x_minus) + (y_plus + y_minus) + (z_plus + z_minus) - 6.0 * here
    advect = (
        speeds[0] * (x_plus - x_minus)
        + speeds[1] * (y_plus - y_minus)
        + speeds[2] * (z_plus - z_minus)
    )
    return here + diffusivity * laplace - advect + jnp.stack(produced)


def rows_for_species(rows, species):
    return jnp.stack([jnp.broadcast_to(row, (species, row.shape[1])) for row in rows])


def own_speeds(flow, x, deep):
    return [[flow[d, x, pl.ds(y, 1), :] for y in range(deep)] for d in range(3)]


def planes_advanced(planes, here, x_beside, y_beside, rates, speeds, diffusivity, mix, emit, together=4):
    for at in range(0, len(planes), together):
        some = planes[at : at + together]
        cells, counts = [], []
        for x in some:
            made = sources(here(x), rates(x))
            counts.append((len(cells), len(cells) + len(made)))
            cells += made
        produced = reacted(cells, mix)
        for x, (start, end) in zip(some, counts):
            emit(
                x,
                advanced(
                    here(x), x_beside(x, 0), x_beside(x, 1), y_beside(x, 0), y_beside(x, 1),
                    speeds(x), diffusivity, produced[start:end],
                ),
            )


def rate_of(temperature, coefficients):
    return coefficients[1] * jnp.exp(coefficients[2] * (-1.0 / temperature))


def own_rates(flow, coefficients, x, deep):
    inverse = -1.0 / flow[3, x]
    return jnp.stack(
        [coefficients[1] * jnp.exp(coefficients[2] * inverse[y : y + 1]) for y in range(deep)]
    )


def block_kernel(shape, held, field, *refs):
    wide, deep, species, up = shape
    rates, (flow, coefficients, mix_ref, out) = refs[0] if held else None, refs[held:]

    def x_beside(x, side):
        at = x + 2 * side - 1
        return field[at] if 0 <= at < wide else jnp.zeros((deep, species, up), jnp.float32)

    def y_beside(x, side):
        here, none = field[x], jnp.zeros((1, species, up), jnp.float32)
        return jnp.concatenate([here[1:], none] if side else [none, here[:-1]], axis=0)

    def emit(x, plane):
        out[x] = plane

    planes_advanced(
        range(wide), lambda x: field[x], x_beside, y_beside,
        lambda x: rates[x] if held else own_rates(flow, coefficients, x, deep),
        lambda x: [rows_for_species(speed, species) for speed in own_speeds(flow, x, deep)],
        coefficients[0][None], mixing(mix_ref[...]), emit,
    )


def from_beyond(value, side, speed, diffusivity):
    across = speed * value
    return diffusivity * value - across if side else diffusivity * value + across


def finish(shape, refs, emit):
    wide, deep, species, up = shape
    own_ref, block, x_one, x_other, y_one, y_other, flow, coefficients = refs
    even_x, even_y = own_ref[0] == 1, own_ref[1] == 1
    diffusivity = coefficients[0][None]

    def row(d, x, y):
        return jnp.broadcast_to(flow[d, x, pl.ds(y, 1), :], (species, up))

    for x in range(wide):
        plane = block[x]
        before = jnp.where(even_y, y_other[x], y_one[x])
        after = jnp.where(even_y, y_one[x], y_other[x])
        before = from_beyond(before, 0, row(1, x, 0), diffusivity[0])
        after = from_beyond(after, 1, row(1, x, deep - 1), diffusivity[0])
        plane = jnp.concatenate(
            [(plane[0] + before)[None], plane[1:-1], (plane[-1] + after)[None]], axis=0
        )
        for side in range(2):
            if x == (wide - 1 if side else 0):
                one, other = (x_one, x_other) if side else (x_other, x_one)
                value = jnp.where(even_x, one[...], other[...])
                speed = rows_for_species(own_speeds(flow, x, deep)[0], species)
                plane = plane + from_beyond(value, side, speed, diffusivity)
        emit(x, plane)


def to_one_or_other(even, one, other, high, value):
    first = even if high else jnp.logical_not(even)

    @pl.when(first)
    def _():
        one[...] = value

    @pl.when(jnp.logical_not(first))
    def _():
        other[...] = value


def advance_kernel(shape, *refs):
    wide, deep, _, _ = shape
    own_ref, (out, x_one, x_other, y_one, y_other) = refs[0], refs[8:]
    even_x, even_y = own_ref[0] == 1, own_ref[1] == 1

    def emit(x, plane):
        out[x] = plane
        low, high = plane[0], plane[deep - 1]
        y_one[x] = jnp.where(even_y, high, low)
        y_other[x] = jnp.where(even_y, low, high)
        if x == 0:
            to_one_or_other(even_x, x_one, x_other, False, plane)
        if x == wide - 1:
            to_one_or_other(even_x, x_one, x_other, True, plane)

    finish(shape, refs[:8], emit)


def outer_of(cell, species):
    return slice(2 * cell * species, (2 * cell + 1) * species)


def inner_of(cell, species):
    return slice((2 * cell + 1) * species, (2 * cell + 2) * species)


def flow_of(cell, count, species):
    return slice(2 * count * species + 4 * cell, 2 * count * species + 4 * cell + 4)


def snapshot_kernel(shape, *refs):
    wide, deep, species, _ = shape
    own_ref, flow, (out, y_one, y_other) = refs[0], refs[6], refs[8:]
    even_y = own_ref[1] == 1

    def emit(x, plane):
        out[x] = plane

        def put(low, high, at):
            y_one[at] = jnp.where(even_y, high, low)
            y_other[at] = jnp.where(even_y, low, high)

        def others(y):
            return jnp.concatenate([flow[d, x, pl.ds(y, 1), :] for d in range(4)], axis=0)

        put(plane[0], plane[deep - 1], outer_of(x, species))
        put(plane[1], plane[deep - 2], inner_of(x, species))
        put(others(0), others(deep - 1), flow_of(x, wide, species))

    finish(shape, refs[:8], emit)


def wide_faces_kernel(shape, own_ref, field, y_one, y_other, flow, x_one, x_other):
    wide, deep, species, _ = shape
    even_x, even_y = own_ref[0] == 1, own_ref[1] == 1

    def face(outer, inner, out):
        for y in range(deep):
            out[outer_of(y, species)] = field[outer, y]
            out[inner_of(y, species)] = field[inner, y]
            out[flow_of(y, deep + 1, species)] = jnp.concatenate(
                [flow[d, outer, y : y + 1, :] for d in range(4)], axis=0
            )
        at = outer_of(outer, species)
        out[outer_of(deep, species)] = choose(even_y, y_one, y_other, 0, at)
        out[inner_of(deep, species)] = choose(even_y, y_one, y_other, 1, at)

    @pl.when(even_x)
    def _():
        face(wide - 1, wide - 2, x_one)
        face(0, 1, x_other)

    @pl.when(jnp.logical_not(even_x))
    def _():
        face(0, 1, x_one)
        face(wide - 1, wide - 2, x_other)


def planes_copied(groups, ready, out, semaphores):
    copies, at = {}, 0
    for group in groups:
        copies[group[-1]] = pltpu.make_async_copy(
            ready.at[:, pl.ds(at, len(group))],
            out.at[:, pl.ds(group[0], len(group))],
            semaphores.at[len(copies)],
        )
        at += len(group)
    return copies


def choose(even, one, other, side, at):
    first, second = (one, other) if side else (other, one)
    return jnp.where(even, first[at], second[at])


def third_step_kernel(
    shape, counts, own_ref, block, field, y_one, y_other, flow, coefficients, mix_ref, edges, ends,
    nearly, out, inner, ready, semaphores,
):
    wide, deep, species, up = shape
    _, columns = counts
    even_y, column = own_ref[1] == 1, own_ref[3]
    inside = (column > 0, column < columns - 1)
    diffusivity, mix = coefficients[0][None], mixing(mix_ref[...])

    def outer(side, x):
        return choose(even_y, y_one, y_other, side, outer_of(x, species))

    def others(side, x):
        return choose(even_y, y_one, y_other, side, flow_of(x, wide, species))

    def here(x):
        return jnp.stack([outer(0, x), outer(1, x)])

    def x_beside(x, side):
        at = x + 2 * side - 1
        return here(at) if 0 <= at < wide else jnp.zeros((2, species, up), jnp.float32)

    def y_beside(x, side):
        beyond = choose(even_y, y_one, y_other, side, inner_of(x, species))
        return jnp.stack([field[x, 0], beyond] if side else [beyond, field[x, deep - 1]])

    def emit(x, plane):
        for side in range(2):
            inner[x, side * (deep + 1)] = jnp.where(inside[side], plane[side], 0.0)

    planes_advanced(
        range(wide), here, x_beside, y_beside,
        lambda x: jnp.stack([rate_of(others(side, x)[3:4], coefficients) for side in range(2)]),
        lambda x: [
            rows_for_species([others(side, x)[d : d + 1] for side in range(2)], species)
            for d in range(3)
        ],
        diffusivity, mix, emit, 16,
    )

    def row(x, y):
        return jnp.broadcast_to(flow[1, x, pl.ds(y, 1), :], (species, up))

    for x in range(wide):
        inner[x, 1] = block[x, 0] + from_beyond(outer(0, x), 0, row(x, 0), diffusivity[0])
        inner[x, 2:deep] = block[x, 1 : deep - 1]
        inner[x, deep] = block[x, deep - 1] + from_beyond(
            outer(1, x), 1, row(x, deep - 1), diffusivity[0]
        )
        if x < 2 or x >= wide - 2:
            edges[x if x < 2 else x - wide + 4] = inner[x]
        if x in (0, wide - 1):
            for side in range(2):
                ends[0 if x == 0 else 1, side, 0:4] = others(side, x)

    inmost = range(2, wide - 2)
    copies = planes_copied(
        [inmost[at : at + 4] for at in range(0, len(inmost), 4)], ready, out, semaphores
    )

    def emit_last(x, plane):
        if x in (1, wide - 2):
            nearly[0 if x == 1 else 1] = plane
        else:
            ready[:, x - 2] = jnp.swapaxes(plane, 0, 1)
        if x in copies:
            copies[x].start()

    def last_beside(x, side):
        at = x + 2 * side - 1
        if at in (0, wide - 1):
            return jnp.zeros((deep, species, up), jnp.float32)
        return inner[at, 1 : deep + 1]

    planes_advanced(
        range(1, wide - 1),
        lambda x: inner[x, 1 : deep + 1],
        last_beside,
        lambda x, side: inner[x, 2 * side : 2 * side + deep],
        lambda x: own_rates(flow, coefficients, x, deep),
        lambda x: [rows_for_species(speed, species) for speed in own_speeds(flow, x, deep)],
        diffusivity, mix, emit_last,
    )
    for copy in copies.values():
        copy.wait()


def fourth_step_kernel(
    shape, counts, own_ref, edges, ends, nearly, _, field, x_one, x_other, flow, coefficients,
    mix_ref, out, edge, x_sides, ready, semaphores,
):
    wide, deep, species, up = shape
    rows, _ = counts
    even_x, row = own_ref[0] == 1, own_ref[2]
    inside = (row > 0, row < rows - 1)
    diffusivity, mix = coefficients[0][None], mixing(mix_ref[...])
    def beside(side, rows_of, cells=range(deep)):
        return jnp.stack(
            [choose(even_x, x_one, x_other, side, rows_of(cell, species)) for cell in cells]
        )

    def corners(side):
        return [beside(side, rows_of, [deep])[0] for rows_of in (outer_of, inner_of)]

    def last(side):
        return wide - 1 if side else 0

    def y_beside(side, to):
        here, corner = beside(side, outer_of), corners(side)[to][None]
        return jnp.concatenate([here[1:], corner] if to else [corner, here[:-1]], axis=0)

    def other_rows(side):
        return [
            choose(even_x, x_one, x_other, side, flow_of(y, deep + 1, species)) for y in range(deep)
        ]

    outermost = [[0], [1], [wide - 2], [wide - 1]]
    copies = planes_copied(outermost, ready, out, semaphores)

    def emit_last(x, plane):
        ready[:, outermost.index([x])] = jnp.swapaxes(plane, 0, 1)
        copies[x].start()

    def speeds_of(x):
        return [rows_for_species(speed, species) for speed in own_speeds(flow, x, deep)]

    for side in range(2):
        x = last(side)
        low, high = corners(side)
        value = jnp.concatenate([low[None], beside(side, outer_of), high[None]], axis=0)
        speed = rows_for_species(
            [ends[side, 0, 0:1]] + own_speeds(flow, x, deep)[0] + [ends[side, 1, 0:1]], species
        )
        edge[side] = edges[3 * side] + from_beyond(value, side, speed, diffusivity)
        inner = wide - 2 if side else 1
        emit_last(
            inner,
            nearly[side]
            + from_beyond(edge[side, 1 : deep + 1], side, speeds_of(inner)[0], diffusivity),
        )

    def emit(side, plane):
        x_sides[side] = jnp.where(inside[side], plane, 0.0)

    planes_advanced(
        range(2), lambda side: beside(side, outer_of),
        lambda side, to: beside(side, inner_of) if side == to else field[last(side)],
        y_beside,
        lambda side: jnp.stack(
            [rate_of(rows[3:4], coefficients) for rows in other_rows(side)]
        ),
        lambda side: [
            rows_for_species([rows[d : d + 1] for rows in other_rows(side)], species)
            for d in range(3)
        ],
        diffusivity, mix, emit,
    )
    planes_advanced(
        range(2),
        lambda side: edge[side, 1 : deep + 1],
        lambda side, to: x_sides[side] if side == to else edges[1 + side, 1 : deep + 1],
        lambda side, to: edge[side, 2 * to : 2 * to + deep],
        lambda side: own_rates(flow, coefficients, last(side), deep),
        lambda side: speeds_of(last(side)),
        diffusivity, mix, lambda side, plane: emit_last(last(side), plane),
    )
    for copy in copies.values():
        copy.wait()


def project_kernel(shape, ranks, field, component, vertical, factor_rows, out):
    wide, deep, species, up = shape
    ranks_a, ranks_d = ranks
    each = deep + 2
    cells = [field[x, y] for y in range(deep) for x in range(wide)]
    high, low = halves_of(jnp.concatenate(cells, axis=0))
    both = jnp.concatenate([high, low], axis=1)
    high, low = halves_of(vertical[...])
    left = jnp.concatenate(
        [jnp.concatenate([high, high], axis=1), jnp.concatenate([low, low], axis=1)], axis=0
    )
    on_d = lax.dot_general(
        left, both, (((1,), (1,)), ((), ())), preferred_element_type=jnp.float32
    )
    on_d = on_d[:ranks_d] + on_d[ranks_d:]
    size = wide * species
    on_d = jnp.concatenate([on_d[:, y * size : (y + 1) * size] for y in range(deep)], axis=0)
    on_both = product(on_d, component[...], (1, 1))
    for y in range(deep):
        out[pl.ds(y, ranks_d, stride=each), :] = on_both[y * ranks_d : (y + 1) * ranks_d]
    for row in range(2):
        out[pl.ds(deep + row, ranks_d, stride=each), :] = jnp.broadcast_to(
            factor_rows[row : row + 1], (ranks_d, 128)
        )


def core_kernel(counts, got, out):
    rows, columns, ranks_a, tall, deep = counts
    devices, each = rows * columns, deep + 2
    own = 128 // ranks_a

    whole = jnp.concatenate(
        [
            jnp.concatenate(
                [got[pl.ds((row * columns + column) * each, deep), :] for column in range(columns)],
                axis=0,
            )
            for row in range(rows)
        ],
        axis=1,
    )

    def in_order(at, of_row):
        both = got[pl.ds(at, devices, stride=each), :]
        halves = jnp.concatenate([both[:, :64], both[:, 64:]], axis=0)
        pick = jnp.full((2 * devices, 2 * devices), 1.0, jnp.float32)
        return product(where_equal(pick, of_row, lambda at: at), halves, (1, 0))

    east = in_order(deep, lambda at: at % 2 * devices + at // 2)
    north = in_order(
        deep + 1, lambda at: at % 2 * devices + at % deep // 2 * columns + at // deep
    )

    def by_rank(array):
        return jnp.concatenate(
            [
                jnp.concatenate(
                    [
                        array[(row * ranks_a + a) * own : (row * ranks_a + a + 1) * own]
                        for row in range(rows)
                    ],
                    axis=0,
                )
                for a in range(ranks_a)
            ],
            axis=1,
        )

    def by_row(parts):
        return jnp.concatenate(
            [
                parts[a][row * own : (row + 1) * own]
                for row in range(rows)
                for a in range(ranks_a)
            ],
            axis=0,
        ).T

    half = by_rank(product(whole, north, (0, 0)))
    core = product(east, half, (0, 0))
    half = product(east, core, (1, 0))
    ranks_c = north.shape[1]
    split = [slice(a * ranks_c, (a + 1) * ranks_c) for a in range(ranks_a)]
    core = by_row([core[:, at] for at in split])
    whole = by_row([product(half[:, at], north, (1, 1)) for at in split])
    for row in range(rows):
        for column in range(columns):
            at = row * columns + column
            out[at, 0:tall] = core[column * tall : (column + 1) * tall, row * 128 : (row + 1) * 128]
            out[at, tall : tall + deep] = whole[
                column * deep : (column + 1) * deep, row * 128 : (row + 1) * 128
            ]


def expand_kernel(shape, ranks, tall, got, field, wide_rows, vertical, residual, core, full):
    wide, deep, species, up = shape
    ranks_a, ranks_d = ranks
    each = tall + deep
    component = where_equal(
        jnp.concatenate([wide_rows[...]] * wide, axis=0),
        lambda at: at // species,
        lambda at: at % wide,
    )
    for y in range(deep):
        on_d = got[pl.ds(tall + y, ranks_d, stride=each), :]
        on_a = product(on_d, vertical[...], (0, 0))
        full[y] = product(component, on_a, (1, 0))
    for x in range(wide):
        residual[:, x] = jnp.swapaxes(
            field[x] - full[:, x * species : (x + 1) * species, :], 0, 1
        )
    turned = [got[pl.ds(c, ranks_d, stride=each), :].T for c in range(tall)]
    core[...] = jnp.swapaxes(jnp.stack(turned), 0, 1)


def swapped(one, other, axes):
    got = []
    for first, face in enumerate((one, other)):
        couples = [(i, i + 1) for i in range(first, lax.axis_size(axes) - 1, 2)]
        got.append(lax.ppermute(face, axes, couples + [(b, a) for a, b in couples]))
    return got


def faces_beside(faces):
    x_one, x_other, y_one, y_other = faces
    y_one, y_other = swapped(y_one, y_other, COLUMN)
    x_one, x_other = swapped(x_one, x_other, ROW)
    return x_one, x_other, y_one, y_other


def whole_factors(tucker_factor_east, tucker_factor_north):
    rows, columns = lax.axis_size(ROW), lax.axis_size(COLUMN)

    def shares(factor, holders, axes):
        count = -(-factor.shape[0] // holders)
        padded = jnp.pad(factor, ((0, count * holders - factor.shape[0]), (0, 0)))
        return lax.dynamic_slice_in_dim(padded, lax.axis_index(axes) * count, count, 0)

    east = shares(tucker_factor_east, columns, COLUMN)
    north = shares(tucker_factor_north, rows, ROW)
    sent = jnp.concatenate([east.reshape(-1), north.reshape(-1)])
    sent = jnp.pad(sent, (0, -sent.size % 128)).reshape(1, -1, 128)
    sent = jnp.broadcast_to(sent, (rows * columns,) + sent.shape[1:])
    got = lax.all_to_all(sent, EVERY, 0, 0, tiled=True).reshape(rows, columns, -1)
    whole_east = got[:, :, : east.size].reshape(rows, -1, east.shape[1])
    whole_east = whole_east[:, : tucker_factor_east.shape[0]].reshape(-1, east.shape[1])
    whole_north = got[:, :, east.size : east.size + north.size]
    whole_north = whole_north.reshape(rows, columns, *north.shape).transpose(1, 0, 2, 3)
    whole_north = whole_north.reshape(columns, -1, north.shape[1])
    whole_north = whole_north[:, : tucker_factor_north.shape[0]].reshape(-1, north.shape[1])
    return whole_east, whole_north


def compress_and_expand(snapshot, east, north, vertical, component):
    rows, columns = lax.axis_size(ROW), lax.axis_size(COLUMN)
    devices = rows * columns
    (wide, deep, _, _), (_, ranks_a) = snapshot.shape, component.shape
    ranks_d = vertical.shape[1]
    ranks_b, ranks_c = east.shape[1], north.shape[1]
    projected = jnp.einsum("xysz,sa->xyaz", snapshot, component, precision=HIGHEST)
    projected = jnp.einsum("xyaz,zd->dyxa", projected, vertical, precision=HIGHEST)
    pairs = ranks_a * ranks_d
    share = -(-pairs // devices)
    flat = jnp.transpose(projected, (0, 3, 1, 2)).reshape(pairs, deep, wide)
    flat = jnp.pad(flat, ((0, share * devices - pairs), (0, 0), (0, 0)))
    flat = flat.reshape(devices, share, deep, wide).transpose(0, 2, 3, 1)
    flat = lax.all_to_all(
        flat.reshape(devices, deep, wide * share), EVERY, 0, 0, tiled=True
    )
    whole = flat.reshape(rows, columns * deep, wide, share)
    part = jnp.einsum("gyxp,yc->cgxp", whole, north, precision=HIGHEST)
    part = part.reshape(ranks_c, rows * wide, share)
    core = jnp.einsum("cxp,xb->cbp", part, east, precision=HIGHEST)
    part = jnp.einsum("cbp,xb->cxp", core, east, precision=HIGHEST)
    whole = jnp.einsum("cxp,yc->yxp", part, north, precision=HIGHEST)
    own_b, own_c = ranks_b // rows, ranks_c // columns

    def pieces(array, tall, broad):
        array = array.reshape(columns, tall, rows, broad, share)
        return array.transpose(2, 0, 1, 3, 4).reshape(devices, tall * broad * share)

    sent = jnp.concatenate([pieces(core, own_c, own_b), pieces(whole, deep, wide)], axis=1)
    sent = jnp.pad(sent, ((0, 0), (0, -sent.shape[1] % 1024)))
    got = lax.all_to_all(
        sent.reshape(devices, -1, 128), EVERY, 0, 0, tiled=True
    ).reshape(devices, -1)

    def ranks_together(array, tall, broad):
        array = array.reshape(devices, tall, broad, share).transpose(0, 3, 2, 1)
        array = array.reshape(devices * share, broad, tall)[:pairs]
        return array.reshape(ranks_d, ranks_a, broad, tall)

    core_size = own_c * own_b * share
    core = ranks_together(got[:, :core_size], own_c, own_b).transpose(1, 2, 3, 0)
    expanded = ranks_together(got[:, core_size : core_size + deep * wide * share], deep, wide)
    expanded = jnp.einsum("daxy,zd->axyz", expanded, vertical, precision=HIGHEST)
    expanded = jnp.einsum("axyz,sa->sxyz", expanded, component, precision=HIGHEST)
    return core, snapshot.transpose(2, 0, 1, 3) - expanded


def body(
    mixture_fields_initial,
    flow_speed_vector,
    thermal_field,
    mass_diffusivity,
    arrhenius_constant,
    arrhenius_energy_temp,
    production_coefficients,
    tucker_factor_east,
    tucker_factor_north,
    tucker_factor_vertical,
    tucker_factor_component,
):
    species, wide, deep, up = mixture_fields_initial.shape
    shape = (wide, deep, species, up)
    cells = wide * deep * species * up
    rows, columns = lax.axis_size(ROW), lax.axis_size(COLUMN)
    devices = rows * columns
    ranks_a, ranks_d = tucker_factor_component.shape[1], tucker_factor_vertical.shape[1]
    ranks_b, ranks_c = tucker_factor_east.shape[1], tucker_factor_north.shape[1]
    own_b, own_c = ranks_b // rows, ranks_c // columns
    kernels_fit = (
        ranks_d == devices
        and wide * ranks_a == 128
        and own_b * ranks_a == 128
        and deep == own_c == 8
        and ranks_b == ranks_c == 64
        and wide == 2 * columns
        and deep == 2 * rows
    )

    row, column = lax.axis_index(ROW), lax.axis_index(COLUMN)
    own = jnp.stack([1 - row % 2, 1 - column % 2, row, column]).astype(jnp.int32)
    face_shapes = [(deep, species, up)] * 2 + [(wide, species, up)] * 2
    faces = vmem_call(
        functools.partial(faces_kernel, shape), face_shapes, 1, 2,
        scratch=[mixture_fields_initial.shape], placed=[1], copies=FACE_COPIES,
    )(own, pltpu.with_memory_space_constraint(mixture_fields_initial, pltpu.HBM))
    faces = faces_beside(faces)
    def with_fetches(kernel, given, small, outs, **cost):
        call = vmem_call(
            kernel, outs, int(given is own), 1 + len(small),
            scratch=[array.shape for array in small], placed=range(1, 1 + len(small)),
            copies=len(small), **cost,
        )
        return call(
            given, *(pltpu.with_memory_space_constraint(array, pltpu.HBM) for array in small)
        )

    field, rates, speeds, coefficients, mix = with_fetches(
        functools.partial(prepare_kernel, shape),
        mixture_fields_initial,
        (
            flow_speed_vector, thermal_field, mass_diffusivity[None], arrhenius_constant[None],
            arrhenius_energy_temp[None], production_coefficients,
        ),
        [shape, shape, (4, wide, deep, up), (3, species, up), (species, 128)],
        flops=4 * cells, moved=12 * cells, exps=cells,
    )
    block, last_block = (
        vmem_call(
            functools.partial(block_kernel, shape, held), [shape], 0, 4 + held,
            flops=60 * cells, moved=8 * cells,
        )
        for held in (1, 0)
    )
    advance = vmem_call(
        functools.partial(advance_kernel, shape), [shape] + face_shapes, 1, 8,
        flops=4 * cells, moved=8 * cells,
    )
    fixed = (rates, speeds, coefficients, mix)
    for substep in range(SUB - 1):
        field, *faces = advance(
            own, *block(field, *fixed), *faces, speeds, coefficients
        )
        first = field
        faces = faces_beside(faces)
    high = 2 * species + 4
    snapshot, *y_faces = vmem_call(
        functools.partial(snapshot_kernel, shape), [shape] + [(wide * high, up)] * 2, 1, 8,
        flops=4 * cells, moved=8 * cells,
    )(own, *block(field, *fixed), *faces, speeds, coefficients)
    y_faces = swapped(*y_faces, COLUMN)
    if kernels_fit:
        own, _ = lax.optimization_barrier((own, first))
        squeeze, wide_rows, upright, *factor_rows = with_fetches(
            functools.partial(matrices_kernel, shape),
            own,
            (
                tucker_factor_component.T, tucker_factor_vertical.T, tucker_factor_east,
                tucker_factor_north,
            ),
            [
                (wide * ranks_a, wide * species), (species, wide * ranks_a), (ranks_d, up),
                (2, 128),
            ],
        )
        (sent,) = vmem_call(
            functools.partial(project_kernel, shape, (ranks_a, ranks_d)),
            [(devices * (deep + 2), 128)], 0, 4, flops=60 * cells, moved=4 * cells,
        )(snapshot, squeeze, upright, *factor_rows)
        got = lax.all_to_all(
            sent.reshape(devices, (deep + 2) // 2, 2, 128), EVERY, 0, 0, tiled=True
        )
        (sent,) = vmem_call(
            functools.partial(core_kernel, (rows, columns, ranks_a, own_c, deep)),
            [(devices, own_c + deep, 128)], 0, 1, flops=60 * cells, moved=4 * cells,
        )(got.reshape(devices * (deep + 2), 128))
        sent, later = lax.optimization_barrier((sent, snapshot))
        got = lax.all_to_all(sent, EVERY, 0, 0, tiled=True)
        residual, tucker_core = vmem_call(
            functools.partial(expand_kernel, shape, (ranks_a, ranks_d), own_c),
            [mixture_fields_initial.shape, (ranks_a * own_b, own_c, ranks_d)], 0, 4,
            flops=60 * cells, moved=8 * cells,
            scratch=[(deep, wide * species, up)],
        )(
            got.reshape(devices * (own_c + deep), 128),
            snapshot,
            wide_rows,
            upright,
        )
        tucker_core = tucker_core.reshape(ranks_a, own_b, own_c, ranks_d)
    else:
        east, north = whole_factors(tucker_factor_east, tucker_factor_north)
        tucker_core, residual = compress_and_expand(
            snapshot, east, north, tucker_factor_vertical, tucker_factor_component
        )
        later = snapshot
    fixed = fixed[1:]
    (third,) = last_block(later, *fixed)
    x_faces = vmem_call(
        functools.partial(wide_faces_kernel, shape),
        [((deep + 1) * high - 4 + spare, up) for spare in (SPARE_X, 0)], 1, 5,
        flops=cells, moved=cells,
    )(own, snapshot, *y_faces, speeds)
    x_faces = swapped(*x_faces, ROW)
    edges, ends, nearly, inmost = vmem_call(
        functools.partial(third_step_kernel, shape, (rows, columns)),
        [
            (4, deep + 2, species, up), (2, 2, 8, up), (2, deep, species, up),
            mixture_fields_initial.shape,
        ], 1, 8,
        flops=120 * cells, moved=16 * cells,
        scratch=[(wide, deep + 2, species, up), (species, wide - 4, deep, up)], placed=[11],
        copies=-(-(wide - 4) // 4),
    )(own, third, snapshot, *y_faces, *fixed)
    own, _ = lax.optimization_barrier((own, tucker_core))
    (mixture_fields_final,) = vmem_call(
        functools.partial(fourth_step_kernel, shape, (rows, columns)),
        [mixture_fields_initial.shape], 1, 11,
        flops=60 * cells, moved=8 * cells,
        scratch=[(2, deep + 2, species, up), (2, deep, species, up), (species, 4, deep, up)],
        placed=[4, 11], copies=4, aliases={4: 0},
    )(own, edges, ends, nearly, inmost, snapshot, *x_faces, *fixed)
    return (mixture_fields_final, residual, tucker_core)


def solution(mesh):
    in_specs = (
        P(None, "gx", ("gy", "ga"), None),
        P(None, "gx", ("gy", "ga"), None),
        P("gx", ("gy", "ga"), None),
        P(),
        P(),
        P(),
        P(),
        P("gx", None),
        P(("gy", "ga"), None),
        P(),
        P(),
    )
    out_specs = (
        P(None, "gx", ("gy", "ga"), None),
        P(None, "gx", ("gy", "ga"), None),
        P(None, "gx", ("gy", "ga"), None),
    )
    return jax.shard_map(body, mesh=mesh, in_specs=in_specs, out_specs=out_specs, check_vma=False)
```

```python
import functools

import jax
import jax.numpy as jnp
from jax import lax
from jax.experimental import pallas as pl
from jax.experimental.pallas import tpu as pltpu
from jax.sharding import PartitionSpec as P

SUB = 2


time_step = 0.5

ROW = "gx"
COLUMN = ("gy", "ga")
EVERY = ("gx", "gy", "ga")
HIGHEST = lax.Precision.HIGHEST
VMEM_LIMIT = 4 * 1024 * 1024
FACE_COPIES = 4

SPARE_X = 104


def vmem_call(
    kernel, outs, in_smem, n_in, flops=0, moved=0, exps=0, scratch=(), placed=(), copies=0, aliases={}
):
    vmem = pl.BlockSpec(memory_space=pltpu.VMEM)
    smem = pl.BlockSpec(memory_space=pltpu.SMEM)
    anywhere = pl.BlockSpec(memory_space=pl.ANY)
    ins = [smem] * in_smem + [vmem] * (n_in - in_smem)
    specs = [anywhere if at in placed else spec for at, spec in enumerate(ins + [vmem] * len(outs))]
    return pl.pallas_call(
        kernel,
        in_specs=specs[:n_in],
        out_specs=specs[n_in:],
        out_shape=[jax.ShapeDtypeStruct(shape, jnp.float32) for shape in outs],
        scratch_shapes=[pltpu.VMEM(shape, jnp.float32) for shape in scratch]
        + [pltpu.SemaphoreType.DMA((copies,))] * (copies > 0),
        input_output_aliases=aliases,
        compiler_params=pltpu.CompilerParams(vmem_limit_bytes=VMEM_LIMIT),
        cost_estimate=pl.CostEstimate(flops=flops, bytes_accessed=moved, transcendentals=exps),
    )


def planes_of_species(ref, species, plane, at):
    return jnp.concatenate(
        [ref[pl.ds(first * plane + at, 8, stride=plane), :] for first in range(0, species, 8)], axis=0
    )


def store_planes_of_species(ref, species, plane, at, value):
    for first in range(0, species, 8):
        ref[pl.ds(first * plane + at, 8, stride=plane), :] = value[first : first + 8]


def faces_kernel(shape, own_ref, given, x_one, x_other, y_one, y_other, held, semaphores):
    wide, deep, species, up = shape
    even_x, even_y = own_ref[0] == 1, own_ref[1] == 1
    plane, together = wide * deep, -(-wide // FACE_COPIES)
    copies = {}
    for x in range(0, wide, together):
        some = pl.ds(x, min(together, wide - x))
        copies[x] = pltpu.make_async_copy(
            given.at[:, some], held.at[:, some], semaphores.at[x // together]
        )
        copies[x].start()
    rows = held.reshape(species * plane, up)
    for x in range(wide):
        if x in copies:
            copies[x].wait()
        low = planes_of_species(rows, species, plane, x * deep)
        high = planes_of_species(rows, species, plane, x * deep + deep - 1)
        y_one[x] = jnp.where(even_y, high, low)
        y_other[x] = jnp.where(even_y, low, high)
        if x in (0, wide - 1):
            face = jnp.swapaxes(held[:, x], 0, 1)
            to_one_or_other(even_x, x_one, x_other, x > 0, face)


def tiled(matrix, count):
    size = matrix.shape[1]
    column = lax.broadcasted_iota(jnp.int32, (size, size * count), 1) % size
    pick = (column == lax.broadcasted_iota(jnp.int32, (size, size * count), 0)).astype(jnp.float32)
    return jnp.dot(matrix, pick, precision=HIGHEST, preferred_element_type=jnp.float32)


def where_equal(matrix, of_row, of_column):
    row = lax.broadcasted_iota(jnp.int32, matrix.shape, 0)
    column = lax.broadcasted_iota(jnp.int32, matrix.shape, 1)
    return jnp.where(of_row(row) == of_column(column), matrix, 0.0)


def fetched(sources, held, semaphores):
    copies = [
        pltpu.make_async_copy(source, target, semaphores.at[at])
        for at, (source, target) in enumerate(zip(sources, held))
    ]
    for copy in copies:
        copy.start()
    return copies


def prepare_kernel(shape, given, *refs):
    wide, deep, species, up = shape
    held, semaphores = refs[-11:-1], refs[-1]
    copies = fetched(refs[:10], held, semaphores)
    flow, thermal, diffusivity, constant, energy, production = held[:6]
    field, rates, speeds, coefficients, mix = refs[10:15]
    for x in range(wide):
        field[x] = jnp.swapaxes(given[:, x], 0, 1)
    for copy in copies:
        copy.wait()
    eye = (
        lax.broadcasted_iota(jnp.int32, (species, species), 0)
        == lax.broadcasted_iota(jnp.int32, (species, species), 1)
    )
    for at, ref in enumerate((diffusivity, constant, energy)):
        column = jnp.sum(jnp.where(eye, ref[...], 0.0), axis=1, keepdims=True)
        coefficients[at] = jnp.broadcast_to(time_step * column if at == 0 else column, (species, up))
    for x in range(wide):
        speeds[3, x] = thermal[x]
        inverse = -1.0 / thermal[x]
        for d in range(3):
            speeds[d, x] = (0.5 * time_step) * flow[d, x]
        for y in range(deep):
            rates[x, y] = coefficients[1] * jnp.exp(coefficients[2] * inverse[y : y + 1])
    mix[...] = tiled(time_step * production[...], mix.shape[1] // species)
    for target, source in zip(refs[15:19], held[6:]):
        target[...] = source[...]


def x_of(lane, wide):
    return 2 * (lane % (wide // 2)) + lane % wide // (wide // 2)


def matrices_kernel(shape, own_ref, turned, east, north, squeeze, wide_rows, factor_rows):
    wide, _, species, _ = shape
    ranks_a = turned.shape[0]
    full = tiled(turned[...], wide)
    full = [jnp.broadcast_to(full[a : a + 1], (wide, full.shape[1])) for a in range(ranks_a)]
    full = jnp.concatenate(full, axis=0)
    squeeze[...] = where_equal(full, lambda at: x_of(at, wide), lambda at: at // species)
    pick = lax.broadcasted_iota(jnp.int32, (ranks_a, ranks_a * wide), 1) // wide
    pick = pick == lax.broadcasted_iota(jnp.int32, pick.shape, 0)
    wide_rows[...] = lax.dot_general(
        turned[...], pick.astype(jnp.float32), (((0,), (0,)), ((), ())), precision=HIGHEST,
        preferred_element_type=jnp.float32,
    )

    def two_rows(ref, at):
        return jnp.concatenate([ref[pl.ds(2 * at + row, 1), :] for row in range(2)], axis=1)

    factor_rows[0:1] = two_rows(east, own_ref[3])
    factor_rows[1:2] = two_rows(north, own_ref[2])


def halves_of(value):
    high = value.astype(jnp.bfloat16)
    return high, (value - high.astype(jnp.float32)).astype(jnp.bfloat16)


def product(a, b, contract):
    def dot(left, right):
        return lax.dot_general(
            left, right, ((contract[:1], contract[1:]), ((), ())),
            preferred_element_type=jnp.float32,
        )

    (a_high, a_low), (b_high, b_low) = halves_of(a), halves_of(b)
    return dot(a_high, b_high) + (dot(a_high, b_low) + dot(a_low, b_high))


def mixing(rows):
    species, size = rows.shape
    full = jnp.concatenate([rows] * (size // species), axis=0)
    high, low = halves_of(
        where_equal(full, lambda at: at // species, lambda at: at // species)
    )
    return jnp.concatenate(
        [jnp.concatenate([high, high], axis=1), jnp.concatenate([low, low], axis=1)], axis=0
    )


def reacted(cells, mix):
    species, up = cells[0].shape
    size = mix.shape[0] // 2
    group = size // species
    cells = cells + [jnp.zeros_like(cells[0])] * (-len(cells) % group)
    right = []
    for at in range(0, len(cells), group):
        high, low = halves_of(jnp.concatenate(cells[at : at + group], axis=0))
        right.append(jnp.concatenate([high, low], axis=0))
    produced = jnp.dot(mix, jnp.concatenate(right, axis=1), preferred_element_type=jnp.float32)
    produced = produced[:size] + produced[size:]
    return [
        produced[cell * species : (cell + 1) * species, at * up : (at + 1) * up]
        for at in range(len(right))
        for cell in range(group)
    ]


def sources(here, rates):
    made = rates * here * pltpu.roll(here, here.shape[1] - 1, 1)
    return [made[cell] for cell in range(here.shape[0])]


def advanced(here, x_minus, x_plus, y_minus, y_plus, speeds, diffusivity, produced):
    up = here.shape[2]
    lane = lax.broadcasted_iota(jnp.int32, here.shape, 2)
    z_minus = jnp.where(lane == 0, 0.0, pltpu.roll(here, 1, 2))
    z_plus = jnp.where(lane == up - 1, 0.0, pltpu.roll(here, up - 1, 2))
    laplace = (x_plus + x_minus) + (y_plus + y_minus) + (z_plus + z_minus) - 6.0 * here
    advect = (
        speeds[0] * (x_plus - x_minus)
        + speeds[1] * (y_plus - y_minus)
        + speeds[2] * (z_plus - z_minus)
    )
    return here + diffusivity * laplace - advect + jnp.stack(produced)


def rows_for_species(rows, species):
    return jnp.stack([jnp.broadcast_to(row, (species, row.shape[1])) for row in rows])


def own_speeds(flow, x, deep):
    return [[flow[d, x, pl.ds(y, 1), :] for y in range(deep)] for d in range(3)]


def planes_advanced(planes, here, x_beside, y_beside, rates, speeds, diffusivity, mix, emit, together=4):
    for at in range(0, len(planes), together):
        some = planes[at : at + together]
        cells, counts = [], []
        for x in some:
            made = sources(here(x), rates(x))
            counts.append((len(cells), len(cells) + len(made)))
            cells += made
        produced = reacted(cells, mix)
        for x, (start, end) in zip(some, counts):
            emit(
                x,
                advanced(
                    here(x), x_beside(x, 0), x_beside(x, 1), y_beside(x, 0), y_beside(x, 1),
                    speeds(x), diffusivity, produced[start:end],
                ),
            )


def rate_of(temperature, coefficients):
    return coefficients[1] * jnp.exp(coefficients[2] * (-1.0 / temperature))


def own_rates(flow, coefficients, x, deep):
    inverse = -1.0 / flow[3, x]
    return jnp.stack(
        [coefficients[1] * jnp.exp(coefficients[2] * inverse[y : y + 1]) for y in range(deep)]
    )


def block_kernel(shape, held, field, *refs):
    wide, deep, species, up = shape
    rates, (flow, coefficients, mix_ref, out) = refs[0] if held else None, refs[held:]

    def x_beside(x, side):
        at = x + 2 * side - 1
        return field[at] if 0 <= at < wide else jnp.zeros((deep, species, up), jnp.float32)

    def y_beside(x, side):
        here, none = field[x], jnp.zeros((1, species, up), jnp.float32)
        return jnp.concatenate([here[1:], none] if side else [none, here[:-1]], axis=0)

    def emit(x, plane):
        out[x] = plane

    planes_advanced(
        range(wide), lambda x: field[x], x_beside, y_beside,
        lambda x: rates[x] if held else own_rates(flow, coefficients, x, deep),
        lambda x: [rows_for_species(speed, species) for speed in own_speeds(flow, x, deep)],
        coefficients[0][None], mixing(mix_ref[...]), emit,
    )


def from_beyond(value, side, speed, diffusivity):
    across = speed * value
    return diffusivity * value - across if side else diffusivity * value + across


def finish(shape, refs, emit):
    wide, deep, species, up = shape
    own_ref, block, x_one, x_other, y_one, y_other, flow, coefficients = refs
    even_x, even_y = own_ref[0] == 1, own_ref[1] == 1
    diffusivity = coefficients[0][None]

    def row(d, x, y):
        return jnp.broadcast_to(flow[d, x, pl.ds(y, 1), :], (species, up))

    for x in range(wide):
        plane = block[x]
        before = jnp.where(even_y, y_other[x], y_one[x])
        after = jnp.where(even_y, y_one[x], y_other[x])
        before = from_beyond(before, 0, row(1, x, 0), diffusivity[0])
        after = from_beyond(after, 1, row(1, x, deep - 1), diffusivity[0])
        plane = jnp.concatenate(
            [(plane[0] + before)[None], plane[1:-1], (plane[-1] + after)[None]], axis=0
        )
        for side in range(2):
            if x == (wide - 1 if side else 0):
                one, other = (x_one, x_other) if side else (x_other, x_one)
                value = jnp.where(even_x, one[...], other[...])
                speed = rows_for_species(own_speeds(flow, x, deep)[0], species)
                plane = plane + from_beyond(value, side, speed, diffusivity)
        emit(x, plane)


def to_one_or_other(even, one, other, high, value):
    first = even if high else jnp.logical_not(even)

    @pl.when(first)
    def _():
        one[...] = value

    @pl.when(jnp.logical_not(first))
    def _():
        other[...] = value


def advance_kernel(shape, *refs):
    wide, deep, _, _ = shape
    own_ref, (out, x_one, x_other, y_one, y_other) = refs[0], refs[8:]
    even_x, even_y = own_ref[0] == 1, own_ref[1] == 1

    def emit(x, plane):
        out[x] = plane
        low, high = plane[0], plane[deep - 1]
        y_one[x] = jnp.where(even_y, high, low)
        y_other[x] = jnp.where(even_y, low, high)
        if x == 0:
            to_one_or_other(even_x, x_one, x_other, False, plane)
        if x == wide - 1:
            to_one_or_other(even_x, x_one, x_other, True, plane)

    finish(shape, refs[:8], emit)


def outer_of(cell, species):
    return slice(2 * cell * species, (2 * cell + 1) * species)


def inner_of(cell, species):
    return slice((2 * cell + 1) * species, (2 * cell + 2) * species)


def flow_of(cell, count, species):
    return slice(2 * count * species + 4 * cell, 2 * count * species + 4 * cell + 4)


def snapshot_kernel(shape, *refs):
    wide, deep, species, _ = shape
    own_ref, flow, (out, y_one, y_other) = refs[0], refs[6], refs[8:]
    even_y = own_ref[1] == 1

    def emit(x, plane):
        out[x] = plane

        def put(low, high, at):
            y_one[at] = jnp.where(even_y, high, low)
            y_other[at] = jnp.where(even_y, low, high)

        def others(y):
            return jnp.concatenate([flow[d, x, pl.ds(y, 1), :] for d in range(4)], axis=0)

        put(plane[0], plane[deep - 1], outer_of(x, species))
        put(plane[1], plane[deep - 2], inner_of(x, species))
        put(others(0), others(deep - 1), flow_of(x, wide, species))

    finish(shape, refs[:8], emit)


def wide_faces_kernel(shape, own_ref, field, y_one, y_other, flow, x_one, x_other):
    wide, deep, species, _ = shape
    even_x, even_y = own_ref[0] == 1, own_ref[1] == 1

    def face(outer, inner, out):
        for y in range(deep):
            out[outer_of(y, species)] = field[outer, y]
            out[inner_of(y, species)] = field[inner, y]
            out[flow_of(y, deep + 1, species)] = jnp.concatenate(
                [flow[d, outer, y : y + 1, :] for d in range(4)], axis=0
            )
        at = outer_of(outer, species)
        out[outer_of(deep, species)] = choose(even_y, y_one, y_other, 0, at)
        out[inner_of(deep, species)] = choose(even_y, y_one, y_other, 1, at)

    @pl.when(even_x)
    def _():
        face(wide - 1, wide - 2, x_one)
        face(0, 1, x_other)

    @pl.when(jnp.logical_not(even_x))
    def _():
        face(0, 1, x_one)
        face(wide - 1, wide - 2, x_other)


def planes_copied(groups, ready, out, semaphores):
    copies, at = {}, 0
    for group in groups:
        copies[group[-1]] = pltpu.make_async_copy(
            ready.at[:, pl.ds(at, len(group))],
            out.at[:, pl.ds(group[0], len(group))],
            semaphores.at[len(copies)],
        )
        at += len(group)
    return copies


def choose(even, one, other, side, at):
    first, second = (one, other) if side else (other, one)
    return jnp.where(even, first[at], second[at])


def third_step_kernel(
    shape, counts, own_ref, block, field, y_one, y_other, flow, coefficients, mix_ref, edges, ends,
    nearly, out, inner, ready, semaphores,
):
    wide, deep, species, up = shape
    _, columns = counts
    even_y, column = own_ref[1] == 1, own_ref[3]
    inside = (column > 0, column < columns - 1)
    diffusivity, mix = coefficients[0][None], mixing(mix_ref[...])

    def outer(side, x):
        return choose(even_y, y_one, y_other, side, outer_of(x, species))

    def others(side, x):
        return choose(even_y, y_one, y_other, side, flow_of(x, wide, species))

    def here(x):
        return jnp.stack([outer(0, x), outer(1, x)])

    def x_beside(x, side):
        at = x + 2 * side - 1
        return here(at) if 0 <= at < wide else jnp.zeros((2, species, up), jnp.float32)

    def y_beside(x, side):
        beyond = choose(even_y, y_one, y_other, side, inner_of(x, species))
        return jnp.stack([field[x, 0], beyond] if side else [beyond, field[x, deep - 1]])

    def emit(x, plane):
        for side in range(2):
            inner[x, side * (deep + 1)] = jnp.where(inside[side], plane[side], 0.0)

    planes_advanced(
        range(wide), here, x_beside, y_beside,
        lambda x: jnp.stack([rate_of(others(side, x)[3:4], coefficients) for side in range(2)]),
        lambda x: [
            rows_for_species([others(side, x)[d : d + 1] for side in range(2)], species)
            for d in range(3)
        ],
        diffusivity, mix, emit, 16,
    )

    def row(x, y):
        return jnp.broadcast_to(flow[1, x, pl.ds(y, 1), :], (species, up))

    for x in range(wide):
        inner[x, 1] = block[x, 0] + from_beyond(outer(0, x), 0, row(x, 0), diffusivity[0])
        inner[x, 2:deep] = block[x, 1 : deep - 1]
        inner[x, deep] = block[x, deep - 1] + from_beyond(
            outer(1, x), 1, row(x, deep - 1), diffusivity[0]
        )
        if x < 2 or x >= wide - 2:
            edges[x if x < 2 else x - wide + 4] = inner[x]
        if x in (0, wide - 1):
            for side in range(2):
                ends[0 if x == 0 else 1, side, 0:4] = others(side, x)

    inmost = range(2, wide - 2)
    copies = planes_copied(
        [inmost[at : at + 6] for at in range(0, len(inmost), 6)], ready, out, semaphores
    )

    def emit_last(x, plane):
        if x in (1, wide - 2):
            nearly[0 if x == 1 else 1] = plane
        else:
            ready[:, x - 2] = jnp.swapaxes(plane, 0, 1)
        if x in copies:
            copies[x].start()

    def last_beside(x, side):
        at = x + 2 * side - 1
        if at in (0, wide - 1):
            return jnp.zeros((deep, species, up), jnp.float32)
        return inner[at, 1 : deep + 1]

    planes_advanced(
        [*inmost, 1, wide - 2],
        lambda x: inner[x, 1 : deep + 1],
        last_beside,
        lambda x, side: inner[x, 2 * side : 2 * side + deep],
        lambda x: own_rates(flow, coefficients, x, deep),
        lambda x: [rows_for_species(speed, species) for speed in own_speeds(flow, x, deep)],
        diffusivity, mix, emit_last,
    )
    for copy in copies.values():
        copy.wait()


def fourth_step_kernel(
    shape, counts, own_ref, edges, ends, nearly, _, field, x_one, x_other, flow, coefficients,
    mix_ref, out, edge, x_sides, ready, semaphores,
):
    wide, deep, species, up = shape
    rows, _ = counts
    even_x, row = own_ref[0] == 1, own_ref[2]
    inside = (row > 0, row < rows - 1)
    diffusivity, mix = coefficients[0][None], mixing(mix_ref[...])
    def beside(side, rows_of, cells=range(deep)):
        return jnp.stack(
            [choose(even_x, x_one, x_other, side, rows_of(cell, species)) for cell in cells]
        )

    def corners(side):
        return [beside(side, rows_of, [deep])[0] for rows_of in (outer_of, inner_of)]

    def last(side):
        return wide - 1 if side else 0

    def y_beside(side, to):
        here, corner = beside(side, outer_of), corners(side)[to][None]
        return jnp.concatenate([here[1:], corner] if to else [corner, here[:-1]], axis=0)

    def other_rows(side):
        return [
            choose(even_x, x_one, x_other, side, flow_of(y, deep + 1, species)) for y in range(deep)
        ]

    outermost = [[0], [1], [wide - 2], [wide - 1]]
    copies = planes_copied(outermost, ready, out, semaphores)

    def emit_last(x, plane):
        ready[:, outermost.index([x])] = jnp.swapaxes(plane, 0, 1)
        copies[x].start()

    def speeds_of(x):
        return [rows_for_species(speed, species) for speed in own_speeds(flow, x, deep)]

    for side in range(2):
        x = last(side)
        low, high = corners(side)
        value = jnp.concatenate([low[None], beside(side, outer_of), high[None]], axis=0)
        speed = rows_for_species(
            [ends[side, 0, 0:1]] + own_speeds(flow, x, deep)[0] + [ends[side, 1, 0:1]], species
        )
        edge[side] = edges[3 * side] + from_beyond(value, side, speed, diffusivity)
        inner = wide - 2 if side else 1
        emit_last(
            inner,
            nearly[side]
            + from_beyond(edge[side, 1 : deep + 1], side, speeds_of(inner)[0], diffusivity),
        )

    def emit(side, plane):
        x_sides[side] = jnp.where(inside[side], plane, 0.0)

    planes_advanced(
        range(2), lambda side: beside(side, outer_of),
        lambda side, to: beside(side, inner_of) if side == to else field[last(side)],
        y_beside,
        lambda side: jnp.stack(
            [rate_of(rows[3:4], coefficients) for rows in other_rows(side)]
        ),
        lambda side: [
            rows_for_species([rows[d : d + 1] for rows in other_rows(side)], species)
            for d in range(3)
        ],
        diffusivity, mix, emit,
    )
    planes_advanced(
        range(2),
        lambda side: edge[side, 1 : deep + 1],
        lambda side, to: x_sides[side] if side == to else edges[1 + side, 1 : deep + 1],
        lambda side, to: edge[side, 2 * to : 2 * to + deep],
        lambda side: own_rates(flow, coefficients, last(side), deep),
        lambda side: speeds_of(last(side)),
        diffusivity, mix, lambda side, plane: emit_last(last(side), plane),
    )
    for copy in copies.values():
        copy.wait()


def project_kernel(shape, ranks, field, component, vertical, factor_rows, out):
    wide, deep, species, up = shape
    ranks_a, ranks_d = ranks
    each = deep + 2
    cells = [field[x, y] for y in range(deep) for x in range(wide)]
    high, low = halves_of(jnp.concatenate(cells, axis=0))
    both = jnp.concatenate([high, low], axis=1)
    high, low = halves_of(vertical[...])
    left = jnp.concatenate(
        [jnp.concatenate([high, high], axis=1), jnp.concatenate([low, low], axis=1)], axis=0
    )
    on_d = lax.dot_general(
        left, both, (((1,), (1,)), ((), ())), preferred_element_type=jnp.float32
    )
    on_d = on_d[:ranks_d] + on_d[ranks_d:]
    size = wide * species
    on_d = jnp.concatenate([on_d[:, y * size : (y + 1) * size] for y in range(deep)], axis=0)
    on_both = product(on_d, component[...], (1, 1))
    for y in range(deep):
        out[pl.ds(y, ranks_d, stride=each), :] = on_both[y * ranks_d : (y + 1) * ranks_d]
    for row in range(2):
        out[pl.ds(deep + row, ranks_d, stride=each), :] = jnp.broadcast_to(
            factor_rows[row : row + 1], (ranks_d, 128)
        )


def core_kernel(counts, got, out):
    rows, columns, ranks_a, tall, deep = counts
    devices, each, all_of = rows * columns, deep + 2, tall + deep
    own = 128 // ranks_a
    in_order = [(r, g) for r in range(2) for g in range(rows)]

    whole = jnp.concatenate(
        [
            jnp.concatenate(
                [
                    got[pl.ds(row * columns * each + 2 * g + r, columns, stride=each), :]
                    for r, g in in_order
                ],
                axis=0,
            )
            for row in range(rows)
        ],
        axis=1,
    )

    def factor(at):
        both = got[pl.ds(at, devices, stride=each), :]
        return jnp.concatenate([both[:, :64], both[:, 64:]], axis=0)

    east, north = factor(deep), factor(deep + 1)
    half = product(whole, north, (0, 0))

    def part(array, a, r, g):
        at = (g * ranks_a + a) * own + r * columns
        return array[at : at + columns]

    half = jnp.concatenate(
        [
            jnp.concatenate([part(half, a, r, g) for r, g in in_order], axis=0)
            for a in range(ranks_a)
        ],
        axis=1,
    )
    core = product(east, half, (0, 0))
    half = product(east, core, (1, 0))
    ranks_c, size = north.shape[1], len(in_order) * columns
    split = [slice(a * ranks_c, (a + 1) * ranks_c) for a in range(ranks_a)]
    core = jnp.concatenate(
        [core[row * own : (row + 1) * own, at] for row in range(rows) for at in split], axis=0
    ).T
    whole = product(jnp.concatenate([half[:, at] for at in split], axis=0), north, (1, 1))
    whole = jnp.concatenate(
        [
            whole[at : at + columns]
            for row in range(rows)
            for a in range(ranks_a)
            for r in range(2)
            for at in [a * size + (r * rows + row) * columns]
        ],
        axis=0,
    ).T
    flat = out.reshape(devices * all_of, 128)
    for row in range(rows):
        lanes = slice(row * 128, (row + 1) * 128)
        for column in range(columns):
            out[row * columns + column, 0:tall] = core[column * tall : (column + 1) * tall, lanes]
        for at, (r, g) in enumerate(in_order):
            flat[pl.ds(row * columns * all_of + tall + 2 * g + r, columns, stride=all_of), :] = whole[
                at * columns : (at + 1) * columns, lanes
            ]


def expand_kernel(shape, ranks, tall, got, field, wide_rows, vertical, residual, core, full):
    wide, deep, species, up = shape
    ranks_a, ranks_d = ranks
    each = tall + deep
    component = where_equal(
        jnp.concatenate([wide_rows[...]] * wide, axis=0),
        lambda at: at // species,
        lambda at: x_of(at, wide),
    )
    for y in range(deep):
        on_d = got[pl.ds(tall + y, ranks_d, stride=each), :]
        on_a = product(on_d, vertical[...], (0, 0))
        full[y] = product(component, on_a, (1, 0))
    for x in range(wide):
        residual[:, x] = jnp.swapaxes(
            field[x] - full[:, x * species : (x + 1) * species, :], 0, 1
        )
    turned = [got[pl.ds(c, ranks_d, stride=each), :].T for c in range(tall)]
    core[...] = jnp.swapaxes(jnp.stack(turned), 0, 1)


def swapped(one, other, axes):
    got = []
    for first, face in enumerate((one, other)):
        couples = [(i, i + 1) for i in range(first, lax.axis_size(axes) - 1, 2)]
        got.append(lax.ppermute(face, axes, couples + [(b, a) for a, b in couples]))
    return got


def faces_beside(faces):
    x_one, x_other, y_one, y_other = faces
    y_one, y_other = swapped(y_one, y_other, COLUMN)
    x_one, x_other = swapped(x_one, x_other, ROW)
    return x_one, x_other, y_one, y_other


def whole_factors(tucker_factor_east, tucker_factor_north):
    rows, columns = lax.axis_size(ROW), lax.axis_size(COLUMN)

    def shares(factor, holders, axes):
        count = -(-factor.shape[0] // holders)
        padded = jnp.pad(factor, ((0, count * holders - factor.shape[0]), (0, 0)))
        return lax.dynamic_slice_in_dim(padded, lax.axis_index(axes) * count, count, 0)

    east = shares(tucker_factor_east, columns, COLUMN)
    north = shares(tucker_factor_north, rows, ROW)
    sent = jnp.concatenate([east.reshape(-1), north.reshape(-1)])
    sent = jnp.pad(sent, (0, -sent.size % 128)).reshape(1, -1, 128)
    sent = jnp.broadcast_to(sent, (rows * columns,) + sent.shape[1:])
    got = lax.all_to_all(sent, EVERY, 0, 0, tiled=True).reshape(rows, columns, -1)
    whole_east = got[:, :, : east.size].reshape(rows, -1, east.shape[1])
    whole_east = whole_east[:, : tucker_factor_east.shape[0]].reshape(-1, east.shape[1])
    whole_north = got[:, :, east.size : east.size + north.size]
    whole_north = whole_north.reshape(rows, columns, *north.shape).transpose(1, 0, 2, 3)
    whole_north = whole_north.reshape(columns, -1, north.shape[1])
    whole_north = whole_north[:, : tucker_factor_north.shape[0]].reshape(-1, north.shape[1])
    return whole_east, whole_north


def compress_and_expand(snapshot, east, north, vertical, component):
    rows, columns = lax.axis_size(ROW), lax.axis_size(COLUMN)
    devices = rows * columns
    (wide, deep, _, _), (_, ranks_a) = snapshot.shape, component.shape
    ranks_d = vertical.shape[1]
    ranks_b, ranks_c = east.shape[1], north.shape[1]
    projected = jnp.einsum("xysz,sa->xyaz", snapshot, component, precision=HIGHEST)
    projected = jnp.einsum("xyaz,zd->dyxa", projected, vertical, precision=HIGHEST)
    pairs = ranks_a * ranks_d
    share = -(-pairs // devices)
    flat = jnp.transpose(projected, (0, 3, 1, 2)).reshape(pairs, deep, wide)
    flat = jnp.pad(flat, ((0, share * devices - pairs), (0, 0), (0, 0)))
    flat = flat.reshape(devices, share, deep, wide).transpose(0, 2, 3, 1)
    flat = lax.all_to_all(
        flat.reshape(devices, deep, wide * share), EVERY, 0, 0, tiled=True
    )
    whole = flat.reshape(rows, columns * deep, wide, share)
    part = jnp.einsum("gyxp,yc->cgxp", whole, north, precision=HIGHEST)
    part = part.reshape(ranks_c, rows * wide, share)
    core = jnp.einsum("cxp,xb->cbp", part, east, precision=HIGHEST)
    part = jnp.einsum("cbp,xb->cxp", core, east, precision=HIGHEST)
    whole = jnp.einsum("cxp,yc->yxp", part, north, precision=HIGHEST)
    own_b, own_c = ranks_b // rows, ranks_c // columns

    def pieces(array, tall, broad):
        array = array.reshape(columns, tall, rows, broad, share)
        return array.transpose(2, 0, 1, 3, 4).reshape(devices, tall * broad * share)

    sent = jnp.concatenate([pieces(core, own_c, own_b), pieces(whole, deep, wide)], axis=1)
    sent = jnp.pad(sent, ((0, 0), (0, -sent.shape[1] % 1024)))
    got = lax.all_to_all(
        sent.reshape(devices, -1, 128), EVERY, 0, 0, tiled=True
    ).reshape(devices, -1)

    def ranks_together(array, tall, broad):
        array = array.reshape(devices, tall, broad, share).transpose(0, 3, 2, 1)
        array = array.reshape(devices * share, broad, tall)[:pairs]
        return array.reshape(ranks_d, ranks_a, broad, tall)

    core_size = own_c * own_b * share
    core = ranks_together(got[:, :core_size], own_c, own_b).transpose(1, 2, 3, 0)
    expanded = ranks_together(got[:, core_size : core_size + deep * wide * share], deep, wide)
    expanded = jnp.einsum("daxy,zd->axyz", expanded, vertical, precision=HIGHEST)
    expanded = jnp.einsum("axyz,sa->sxyz", expanded, component, precision=HIGHEST)
    return core, snapshot.transpose(2, 0, 1, 3) - expanded


def body(
    mixture_fields_initial,
    flow_speed_vector,
    thermal_field,
    mass_diffusivity,
    arrhenius_constant,
    arrhenius_energy_temp,
    production_coefficients,
    tucker_factor_east,
    tucker_factor_north,
    tucker_factor_vertical,
    tucker_factor_component,
):
    species, wide, deep, up = mixture_fields_initial.shape
    shape = (wide, deep, species, up)
    cells = wide * deep * species * up
    rows, columns = lax.axis_size(ROW), lax.axis_size(COLUMN)
    devices = rows * columns
    ranks_a, ranks_d = tucker_factor_component.shape[1], tucker_factor_vertical.shape[1]
    ranks_b, ranks_c = tucker_factor_east.shape[1], tucker_factor_north.shape[1]
    own_b, own_c = ranks_b // rows, ranks_c // columns
    kernels_fit = (
        ranks_d == devices
        and wide * ranks_a == 128
        and own_b * ranks_a == 128
        and deep == own_c == 8
        and ranks_b == ranks_c == 64
        and wide == 2 * columns
        and deep == 2 * rows
    )

    row, column = lax.axis_index(ROW), lax.axis_index(COLUMN)
    own = jnp.stack([1 - row % 2, 1 - column % 2, row, column]).astype(jnp.int32)
    face_shapes = [(deep, species, up)] * 2 + [(wide, species, up)] * 2
    faces = vmem_call(
        functools.partial(faces_kernel, shape), face_shapes, 1, 2,
        scratch=[mixture_fields_initial.shape], placed=[1], copies=FACE_COPIES,
    )(own, pltpu.with_memory_space_constraint(mixture_fields_initial, pltpu.HBM))
    faces = faces_beside(faces)
    def with_fetches(kernel, given, small, outs, **cost):
        call = vmem_call(
            kernel, outs, 0, 1 + len(small),
            scratch=[array.shape for array in small], placed=range(1, 1 + len(small)),
            copies=len(small), **cost,
        )
        return call(
            given, *(pltpu.with_memory_space_constraint(array, pltpu.HBM) for array in small)
        )

    field, rates, speeds, coefficients, mix, turned, upright, east, north = with_fetches(
        functools.partial(prepare_kernel, shape),
        mixture_fields_initial,
        (
            flow_speed_vector, thermal_field, mass_diffusivity[None], arrhenius_constant[None],
            arrhenius_energy_temp[None], production_coefficients, tucker_factor_component.T,
            tucker_factor_vertical.T, tucker_factor_east, tucker_factor_north,
        ),
        [
            shape, shape, (4, wide, deep, up), (3, species, up), (species, 128),
            (ranks_a, species), (ranks_d, up), tucker_factor_east.shape, tucker_factor_north.shape,
        ],
        flops=4 * cells, moved=12 * cells, exps=cells,
    )
    block, last_block = (
        vmem_call(
            functools.partial(block_kernel, shape, held), [shape], 0, 4 + held,
            flops=60 * cells, moved=8 * cells,
        )
        for held in (1, 0)
    )
    advance = vmem_call(
        functools.partial(advance_kernel, shape), [shape] + face_shapes, 1, 8,
        flops=4 * cells, moved=8 * cells,
    )
    fixed = (rates, speeds, coefficients, mix)
    for substep in range(SUB - 1):
        field, *faces = advance(
            own, *block(field, *fixed), *faces, speeds, coefficients
        )
        first = field
        faces = faces_beside(faces)
    high = 2 * species + 4
    snapshot, *y_faces = vmem_call(
        functools.partial(snapshot_kernel, shape), [shape] + [(wide * high, up)] * 2, 1, 8,
        flops=4 * cells, moved=8 * cells,
    )(own, *block(field, *fixed), *faces, speeds, coefficients)
    y_faces = swapped(*y_faces, COLUMN)
    if kernels_fit:
        own, _ = lax.optimization_barrier((own, first))
        squeeze, wide_rows, factor_rows = vmem_call(
            functools.partial(matrices_kernel, shape),
            [(wide * ranks_a, wide * species), (species, wide * ranks_a), (2, 128)], 1, 4,
        )(own, turned, east, north)
        (sent,) = vmem_call(
            functools.partial(project_kernel, shape, (ranks_a, ranks_d)),
            [(devices * (deep + 2), 128)], 0, 4, flops=60 * cells, moved=4 * cells,
        )(snapshot, squeeze, upright, factor_rows)
        got = lax.all_to_all(
            sent.reshape(devices, (deep + 2) // 2, 2, 128), EVERY, 0, 0, tiled=True
        )
        (sent,) = vmem_call(
            functools.partial(core_kernel, (rows, columns, ranks_a, own_c, deep)),
            [(devices, own_c + deep, 128)], 0, 1, flops=60 * cells, moved=4 * cells,
        )(got.reshape(devices * (deep + 2), 128))
        sent, later = lax.optimization_barrier((sent, snapshot))
        got = lax.all_to_all(sent, EVERY, 0, 0, tiled=True)
        residual, tucker_core = vmem_call(
            functools.partial(expand_kernel, shape, (ranks_a, ranks_d), own_c),
            [mixture_fields_initial.shape, (ranks_a * own_b, own_c, ranks_d)], 0, 4,
            flops=60 * cells, moved=8 * cells,
            scratch=[(deep, wide * species, up)],
        )(
            got.reshape(devices * (own_c + deep), 128),
            snapshot,
            wide_rows,
            upright,
        )
        tucker_core = tucker_core.reshape(ranks_a, own_b, own_c, ranks_d)
    else:
        east, north = whole_factors(tucker_factor_east, tucker_factor_north)
        tucker_core, residual = compress_and_expand(
            snapshot, east, north, tucker_factor_vertical, tucker_factor_component
        )
        later = snapshot
    fixed = fixed[1:]
    (third,) = last_block(later, *fixed)
    x_faces = vmem_call(
        functools.partial(wide_faces_kernel, shape),
        [((deep + 1) * high - 4 + spare, up) for spare in (SPARE_X, 0)], 1, 5,
        flops=cells, moved=cells,
    )(own, snapshot, *y_faces, speeds)
    x_faces = swapped(*x_faces, ROW)
    edges, ends, nearly, inmost = vmem_call(
        functools.partial(third_step_kernel, shape, (rows, columns)),
        [
            (4, deep + 2, species, up), (2, 2, 8, up), (2, deep, species, up),
            mixture_fields_initial.shape,
        ], 1, 8,
        flops=120 * cells, moved=16 * cells,
        scratch=[(wide, deep + 2, species, up), (species, wide - 4, deep, up)], placed=[11],
        copies=-(-(wide - 4) // 4),
    )(own, third, snapshot, *y_faces, *fixed)
    own, _ = lax.optimization_barrier((own, tucker_core))
    (mixture_fields_final,) = vmem_call(
        functools.partial(fourth_step_kernel, shape, (rows, columns)),
        [mixture_fields_initial.shape], 1, 11,
        flops=60 * cells, moved=8 * cells,
        scratch=[(2, deep + 2, species, up), (2, deep, species, up), (species, 4, deep, up)],
        placed=[4, 11], copies=4, aliases={4: 0},
    )(own, edges, ends, nearly, inmost, snapshot, *x_faces, *fixed)
    return (mixture_fields_final, residual, tucker_core)


def solution(mesh):
    in_specs = (
        P(None, "gx", ("gy", "ga"), None),
        P(None, "gx", ("gy", "ga"), None),
        P("gx", ("gy", "ga"), None),
        P(),
        P(),
        P(),
        P(),
        P("gx", None),
        P(("gy", "ga"), None),
        P(),
        P(),
    )
    out_specs = (
        P(None, "gx", ("gy", "ga"), None),
        P(None, "gx", ("gy", "ga"), None),
        P(None, "gx", ("gy", "ga"), None),
    )
    return jax.shard_map(body, mesh=mesh, in_specs=in_specs, out_specs=out_specs, check_vma=False)
```

```python
import functools

import jax
import jax.numpy as jnp
from jax import lax
from jax.experimental import pallas as pl
from jax.experimental.pallas import tpu as pltpu
from jax.sharding import PartitionSpec as P

SUB = 2


time_step = 0.5

ROW = "gx"
COLUMN = ("gy", "ga")
EVERY = ("gx", "gy", "ga")
HIGHEST = lax.Precision.HIGHEST
VMEM_LIMIT = 4 * 1024 * 1024
FACE_COPIES = 4

SPARE_X = 104


def vmem_call(
    kernel, outs, in_smem, n_in, flops=0, moved=0, exps=0, scratch=(), placed=(), copies=0, aliases={}
):
    vmem = pl.BlockSpec(memory_space=pltpu.VMEM)
    smem = pl.BlockSpec(memory_space=pltpu.SMEM)
    anywhere = pl.BlockSpec(memory_space=pl.ANY)
    ins = [smem] * in_smem + [vmem] * (n_in - in_smem)
    specs = [anywhere if at in placed else spec for at, spec in enumerate(ins + [vmem] * len(outs))]
    return pl.pallas_call(
        kernel,
        in_specs=specs[:n_in],
        out_specs=specs[n_in:],
        out_shape=[jax.ShapeDtypeStruct(shape, jnp.float32) for shape in outs],
        scratch_shapes=[pltpu.VMEM(shape, jnp.float32) for shape in scratch]
        + [pltpu.SemaphoreType.DMA((copies,))] * (copies > 0),
        input_output_aliases=aliases,
        compiler_params=pltpu.CompilerParams(vmem_limit_bytes=VMEM_LIMIT),
        cost_estimate=pl.CostEstimate(flops=flops, bytes_accessed=moved, transcendentals=exps),
    )


def planes_of_species(ref, species, plane, at):
    return jnp.concatenate(
        [ref[pl.ds(first * plane + at, 8, stride=plane), :] for first in range(0, species, 8)], axis=0
    )


def store_planes_of_species(ref, species, plane, at, value):
    for first in range(0, species, 8):
        ref[pl.ds(first * plane + at, 8, stride=plane), :] = value[first : first + 8]


def faces_kernel(shape, own_ref, given, x_one, x_other, y_one, y_other, held, semaphores):
    wide, deep, species, up = shape
    even_x, even_y = own_ref[0] == 1, own_ref[1] == 1
    plane, together = wide * deep, -(-wide // FACE_COPIES)
    copies = {}
    for x in range(0, wide, together):
        some = pl.ds(x, min(together, wide - x))
        copies[x] = pltpu.make_async_copy(
            given.at[:, some], held.at[:, some], semaphores.at[x // together]
        )
        copies[x].start()
    rows = held.reshape(species * plane, up)
    for x in range(wide):
        if x in copies:
            copies[x].wait()
        low = planes_of_species(rows, species, plane, x * deep)
        high = planes_of_species(rows, species, plane, x * deep + deep - 1)
        y_one[x] = jnp.where(even_y, high, low)
        y_other[x] = jnp.where(even_y, low, high)
        if x in (0, wide - 1):
            face = jnp.swapaxes(held[:, x], 0, 1)
            to_one_or_other(even_x, x_one, x_other, x > 0, face)


def tiled(matrix, count):
    size = matrix.shape[1]
    column = lax.broadcasted_iota(jnp.int32, (size, size * count), 1) % size
    pick = (column == lax.broadcasted_iota(jnp.int32, (size, size * count), 0)).astype(jnp.float32)
    return jnp.dot(matrix, pick, precision=HIGHEST, preferred_element_type=jnp.float32)


def where_equal(matrix, of_row, of_column):
    row = lax.broadcasted_iota(jnp.int32, matrix.shape, 0)
    column = lax.broadcasted_iota(jnp.int32, matrix.shape, 1)
    return jnp.where(of_row(row) == of_column(column), matrix, 0.0)


def fetched(sources, held, semaphores):
    copies = [
        pltpu.make_async_copy(source, target, semaphores.at[at])
        for at, (source, target) in enumerate(zip(sources, held))
    ]
    for copy in copies:
        copy.start()
    return copies


def prepare_kernel(shape, given, *refs):
    wide, deep, species, up = shape
    held, semaphores = refs[-11:-1], refs[-1]
    copies = fetched(refs[:10], held, semaphores)
    flow, thermal, diffusivity, constant, energy, production = held[:6]
    field, rates, speeds, coefficients, mix = refs[10:15]
    for x in range(wide):
        field[x] = jnp.swapaxes(given[:, x], 0, 1)
    for copy in copies:
        copy.wait()
    eye = (
        lax.broadcasted_iota(jnp.int32, (species, species), 0)
        == lax.broadcasted_iota(jnp.int32, (species, species), 1)
    )
    for at, ref in enumerate((diffusivity, constant, energy)):
        column = jnp.sum(jnp.where(eye, ref[...], 0.0), axis=1, keepdims=True)
        coefficients[at] = jnp.broadcast_to(time_step * column if at == 0 else column, (species, up))
    for x in range(wide):
        speeds[3, x] = thermal[x]
        inverse = -1.0 / thermal[x]
        for d in range(3):
            speeds[d, x] = (0.5 * time_step) * flow[d, x]
        for y in range(deep):
            rates[x, y] = coefficients[1] * jnp.exp(coefficients[2] * inverse[y : y + 1])
    mix[...] = tiled(time_step * production[...], mix.shape[1] // species)
    for target, source in zip(refs[15:19], held[6:]):
        target[...] = source[...]


def x_of(lane, wide):
    return 2 * (lane % (wide // 2)) + lane % wide // (wide // 2)


def matrices_kernel(shape, own_ref, turned, east, north, squeeze, wide_rows, factor_rows):
    wide, _, species, _ = shape
    ranks_a = turned.shape[0]
    full = tiled(turned[...], wide)
    full = [jnp.broadcast_to(full[a : a + 1], (wide, full.shape[1])) for a in range(ranks_a)]
    full = jnp.concatenate(full, axis=0)
    squeeze[...] = where_equal(full, lambda at: x_of(at, wide), lambda at: at // species)
    pick = lax.broadcasted_iota(jnp.int32, (ranks_a, ranks_a * wide), 1) // wide
    pick = pick == lax.broadcasted_iota(jnp.int32, pick.shape, 0)
    wide_rows[...] = lax.dot_general(
        turned[...], pick.astype(jnp.float32), (((0,), (0,)), ((), ())), precision=HIGHEST,
        preferred_element_type=jnp.float32,
    )

    def two_rows(ref, at):
        return jnp.concatenate([ref[pl.ds(2 * at + row, 1), :] for row in range(2)], axis=1)

    factor_rows[0:1] = two_rows(east, own_ref[3])
    factor_rows[1:2] = two_rows(north, own_ref[2])


def halves_of(value):
    high = value.astype(jnp.bfloat16)
    return high, (value - high.astype(jnp.float32)).astype(jnp.bfloat16)


def product(a, b, contract):
    def dot(left, right):
        return lax.dot_general(
            left, right, ((contract[:1], contract[1:]), ((), ())),
            preferred_element_type=jnp.float32,
        )

    (a_high, a_low), (b_high, b_low) = halves_of(a), halves_of(b)
    return dot(a_high, b_high) + (dot(a_high, b_low) + dot(a_low, b_high))


def mixing(rows):
    species, size = rows.shape
    full = jnp.concatenate([rows] * (size // species), axis=0)
    high, low = halves_of(
        where_equal(full, lambda at: at // species, lambda at: at // species)
    )
    return jnp.concatenate(
        [jnp.concatenate([high, high], axis=1), jnp.concatenate([low, low], axis=1)], axis=0
    )


def reacted(cells, mix):
    species, up = cells[0].shape
    size = mix.shape[0] // 2
    group = size // species
    cells = cells + [jnp.zeros_like(cells[0])] * (-len(cells) % group)
    right = []
    for at in range(0, len(cells), group):
        high, low = halves_of(jnp.concatenate(cells[at : at + group], axis=0))
        right.append(jnp.concatenate([high, low], axis=0))
    produced = jnp.dot(mix, jnp.concatenate(right, axis=1), preferred_element_type=jnp.float32)
    produced = produced[:size] + produced[size:]
    return [
        produced[cell * species : (cell + 1) * species, at * up : (at + 1) * up]
        for at in range(len(right))
        for cell in range(group)
    ]


def sources(here, rates):
    made = rates * here * pltpu.roll(here, here.shape[1] - 1, 1)
    return [made[cell] for cell in range(here.shape[0])]


def advanced(here, x_minus, x_plus, y_minus, y_plus, speeds, diffusivity, produced):
    up = here.shape[2]
    lane = lax.broadcasted_iota(jnp.int32, here.shape, 2)
    z_minus = jnp.where(lane == 0, 0.0, pltpu.roll(here, 1, 2))
    z_plus = jnp.where(lane == up - 1, 0.0, pltpu.roll(here, up - 1, 2))
    laplace = (x_plus + x_minus) + (y_plus + y_minus) + (z_plus + z_minus) - 6.0 * here
    advect = (
        speeds[0] * (x_plus - x_minus)
        + speeds[1] * (y_plus - y_minus)
        + speeds[2] * (z_plus - z_minus)
    )
    return here + diffusivity * laplace - advect + jnp.stack(produced)


def rows_for_species(rows, species):
    return jnp.stack([jnp.broadcast_to(row, (species, row.shape[1])) for row in rows])


def own_speeds(flow, x, deep):
    return [[flow[d, x, pl.ds(y, 1), :] for y in range(deep)] for d in range(3)]


def planes_advanced(planes, here, x_beside, y_beside, rates, speeds, diffusivity, mix, emit, together=4):
    for at in range(0, len(planes), together):
        some = planes[at : at + together]
        cells, counts = [], []
        for x in some:
            made = sources(here(x), rates(x))
            counts.append((len(cells), len(cells) + len(made)))
            cells += made
        produced = reacted(cells, mix)
        for x, (start, end) in zip(some, counts):
            emit(
                x,
                advanced(
                    here(x), x_beside(x, 0), x_beside(x, 1), y_beside(x, 0), y_beside(x, 1),
                    speeds(x), diffusivity, produced[start:end],
                ),
            )


def rate_of(temperature, coefficients):
    return coefficients[1] * jnp.exp(coefficients[2] * (-1.0 / temperature))


def own_rates(flow, coefficients, x, deep):
    inverse = -1.0 / flow[3, x]
    return jnp.stack(
        [coefficients[1] * jnp.exp(coefficients[2] * inverse[y : y + 1]) for y in range(deep)]
    )


def block_kernel(shape, held, field, *refs):
    wide, deep, species, up = shape
    rates, (flow, coefficients, mix_ref, out) = refs[0] if held else None, refs[held:]

    def x_beside(x, side):
        at = x + 2 * side - 1
        return field[at] if 0 <= at < wide else jnp.zeros((deep, species, up), jnp.float32)

    def y_beside(x, side):
        here, none = field[x], jnp.zeros((1, species, up), jnp.float32)
        return jnp.concatenate([here[1:], none] if side else [none, here[:-1]], axis=0)

    def emit(x, plane):
        out[x] = plane

    planes_advanced(
        range(wide), lambda x: field[x], x_beside, y_beside,
        lambda x: rates[x] if held else own_rates(flow, coefficients, x, deep),
        lambda x: [rows_for_species(speed, species) for speed in own_speeds(flow, x, deep)],
        coefficients[0][None], mixing(mix_ref[...]), emit,
    )


def from_beyond(value, side, speed, diffusivity):
    across = speed * value
    return diffusivity * value - across if side else diffusivity * value + across


def finish(shape, refs, emit):
    wide, deep, species, up = shape
    own_ref, block, x_one, x_other, y_one, y_other, flow, coefficients = refs
    even_x, even_y = own_ref[0] == 1, own_ref[1] == 1
    diffusivity = coefficients[0][None]

    def row(d, x, y):
        return jnp.broadcast_to(flow[d, x, pl.ds(y, 1), :], (species, up))

    for x in range(wide):
        plane = block[x]
        before = jnp.where(even_y, y_other[x], y_one[x])
        after = jnp.where(even_y, y_one[x], y_other[x])
        before = from_beyond(before, 0, row(1, x, 0), diffusivity[0])
        after = from_beyond(after, 1, row(1, x, deep - 1), diffusivity[0])
        plane = jnp.concatenate(
            [(plane[0] + before)[None], plane[1:-1], (plane[-1] + after)[None]], axis=0
        )
        for side in range(2):
            if x == (wide - 1 if side else 0):
                one, other = (x_one, x_other) if side else (x_other, x_one)
                value = jnp.where(even_x, one[...], other[...])
                speed = rows_for_species(own_speeds(flow, x, deep)[0], species)
                plane = plane + from_beyond(value, side, speed, diffusivity)
        emit(x, plane)


def to_one_or_other(even, one, other, high, value):
    first = even if high else jnp.logical_not(even)

    @pl.when(first)
    def _():
        one[...] = value

    @pl.when(jnp.logical_not(first))
    def _():
        other[...] = value


def advance_kernel(shape, *refs):
    wide, deep, _, _ = shape
    own_ref, (out, x_one, x_other, y_one, y_other) = refs[0], refs[8:]
    even_x, even_y = own_ref[0] == 1, own_ref[1] == 1

    def emit(x, plane):
        out[x] = plane
        low, high = plane[0], plane[deep - 1]
        y_one[x] = jnp.where(even_y, high, low)
        y_other[x] = jnp.where(even_y, low, high)
        if x == 0:
            to_one_or_other(even_x, x_one, x_other, False, plane)
        if x == wide - 1:
            to_one_or_other(even_x, x_one, x_other, True, plane)

    finish(shape, refs[:8], emit)


def outer_of(cell, species):
    return slice(2 * cell * species, (2 * cell + 1) * species)


def inner_of(cell, species):
    return slice((2 * cell + 1) * species, (2 * cell + 2) * species)


def flow_of(cell, count, species):
    return slice(2 * count * species + 4 * cell, 2 * count * species + 4 * cell + 4)


def snapshot_kernel(shape, *refs):
    wide, deep, species, _ = shape
    own_ref, flow, (out, y_one, y_other) = refs[0], refs[6], refs[8:]
    even_y = own_ref[1] == 1

    def emit(x, plane):
        out[x] = plane

        def put(low, high, at):
            y_one[at] = jnp.where(even_y, high, low)
            y_other[at] = jnp.where(even_y, low, high)

        def others(y):
            return jnp.concatenate([flow[d, x, pl.ds(y, 1), :] for d in range(4)], axis=0)

        put(plane[0], plane[deep - 1], outer_of(x, species))
        put(plane[1], plane[deep - 2], inner_of(x, species))
        put(others(0), others(deep - 1), flow_of(x, wide, species))

    finish(shape, refs[:8], emit)


def wide_faces_kernel(shape, own_ref, field, y_one, y_other, flow, x_one, x_other):
    wide, deep, species, _ = shape
    even_x, even_y = own_ref[0] == 1, own_ref[1] == 1

    def face(outer, inner, out):
        for y in range(deep):
            out[outer_of(y, species)] = field[outer, y]
            out[inner_of(y, species)] = field[inner, y]
            out[flow_of(y, deep + 1, species)] = jnp.concatenate(
                [flow[d, outer, y : y + 1, :] for d in range(4)], axis=0
            )
        at = outer_of(outer, species)
        out[outer_of(deep, species)] = choose(even_y, y_one, y_other, 0, at)
        out[inner_of(deep, species)] = choose(even_y, y_one, y_other, 1, at)

    @pl.when(even_x)
    def _():
        face(wide - 1, wide - 2, x_one)
        face(0, 1, x_other)

    @pl.when(jnp.logical_not(even_x))
    def _():
        face(0, 1, x_one)
        face(wide - 1, wide - 2, x_other)


def planes_copied(groups, ready, out, semaphores):
    copies, at = {}, 0
    for group in groups:
        copies[group[-1]] = pltpu.make_async_copy(
            ready.at[:, pl.ds(at, len(group))],
            out.at[:, pl.ds(group[0], len(group))],
            semaphores.at[len(copies)],
        )
        at += len(group)
    return copies


def choose(even, one, other, side, at):
    first, second = (one, other) if side else (other, one)
    return jnp.where(even, first[at], second[at])


def third_step_kernel(
    shape, counts, own_ref, block, field, y_one, y_other, flow, coefficients, mix_ref, edges, ends,
    nearly, out, inner, ready, semaphores,
):
    wide, deep, species, up = shape
    _, columns = counts
    even_y, column = own_ref[1] == 1, own_ref[3]
    inside = (column > 0, column < columns - 1)
    diffusivity, mix = coefficients[0][None], mixing(mix_ref[...])

    def outer(side, x):
        return choose(even_y, y_one, y_other, side, outer_of(x, species))

    def others(side, x):
        return choose(even_y, y_one, y_other, side, flow_of(x, wide, species))

    def here(x):
        return jnp.stack([outer(0, x), outer(1, x)])

    def x_beside(x, side):
        at = x + 2 * side - 1
        return here(at) if 0 <= at < wide else jnp.zeros((2, species, up), jnp.float32)

    def y_beside(x, side):
        beyond = choose(even_y, y_one, y_other, side, inner_of(x, species))
        return jnp.stack([field[x, 0], beyond] if side else [beyond, field[x, deep - 1]])

    def emit(x, plane):
        for side in range(2):
            inner[x, side * (deep + 1)] = jnp.where(inside[side], plane[side], 0.0)

    planes_advanced(
        range(wide), here, x_beside, y_beside,
        lambda x: jnp.stack([rate_of(others(side, x)[3:4], coefficients) for side in range(2)]),
        lambda x: [
            rows_for_species([others(side, x)[d : d + 1] for side in range(2)], species)
            for d in range(3)
        ],
        diffusivity, mix, emit, 16,
    )

    def row(x, y):
        return jnp.broadcast_to(flow[1, x, pl.ds(y, 1), :], (species, up))

    for x in range(wide):
        inner[x, 1] = block[x, 0] + from_beyond(outer(0, x), 0, row(x, 0), diffusivity[0])
        inner[x, 2:deep] = block[x, 1 : deep - 1]
        inner[x, deep] = block[x, deep - 1] + from_beyond(
            outer(1, x), 1, row(x, deep - 1), diffusivity[0]
        )
        if x < 2 or x >= wide - 2:
            edges[x if x < 2 else x - wide + 4] = inner[x]
        if x in (0, wide - 1):
            for side in range(2):
                ends[0 if x == 0 else 1, side, 0:4] = others(side, x)

    inmost = range(2, wide - 2)
    copies = planes_copied(
        [inmost[at : at + 6] for at in range(0, len(inmost), 6)], ready, out, semaphores
    )

    def emit_last(x, plane):
        if x in (1, wide - 2):
            nearly[0 if x == 1 else 1] = plane
        else:
            ready[:, x - 2] = jnp.swapaxes(plane, 0, 1)
        if x in copies:
            copies[x].start()

    def last_beside(x, side):
        at = x + 2 * side - 1
        if at in (0, wide - 1):
            return jnp.zeros((deep, species, up), jnp.float32)
        return inner[at, 1 : deep + 1]

    planes_advanced(
        [*inmost, 1, wide - 2],
        lambda x: inner[x, 1 : deep + 1],
        last_beside,
        lambda x, side: inner[x, 2 * side : 2 * side + deep],
        lambda x: own_rates(flow, coefficients, x, deep),
        lambda x: [rows_for_species(speed, species) for speed in own_speeds(flow, x, deep)],
        diffusivity, mix, emit_last,
    )
    for copy in copies.values():
        copy.wait()


def fourth_step_kernel(
    shape, counts, own_ref, edges, ends, nearly, _, field, x_one, x_other, flow, coefficients,
    mix_ref, out, edge, x_sides, ready, semaphores,
):
    wide, deep, species, up = shape
    rows, _ = counts
    even_x, row = own_ref[0] == 1, own_ref[2]
    inside = (row > 0, row < rows - 1)
    diffusivity, mix = coefficients[0][None], mixing(mix_ref[...])
    def beside(side, rows_of, cells=range(deep)):
        return jnp.stack(
            [choose(even_x, x_one, x_other, side, rows_of(cell, species)) for cell in cells]
        )

    def corners(side):
        return [beside(side, rows_of, [deep])[0] for rows_of in (outer_of, inner_of)]

    def last(side):
        return wide - 1 if side else 0

    def y_beside(side, to):
        here, corner = beside(side, outer_of), corners(side)[to][None]
        return jnp.concatenate([here[1:], corner] if to else [corner, here[:-1]], axis=0)

    def other_rows(side):
        return [
            choose(even_x, x_one, x_other, side, flow_of(y, deep + 1, species)) for y in range(deep)
        ]

    outermost = [[0], [1], [wide - 2], [wide - 1]]
    copies = planes_copied(outermost, ready, out, semaphores)

    def emit_last(x, plane):
        ready[:, outermost.index([x])] = jnp.swapaxes(plane, 0, 1)
        copies[x].start()

    def speeds_of(x):
        return [rows_for_species(speed, species) for speed in own_speeds(flow, x, deep)]

    for side in range(2):
        x = last(side)
        low, high = corners(side)
        value = jnp.concatenate([low[None], beside(side, outer_of), high[None]], axis=0)
        speed = rows_for_species(
            [ends[side, 0, 0:1]] + own_speeds(flow, x, deep)[0] + [ends[side, 1, 0:1]], species
        )
        edge[side] = edges[3 * side] + from_beyond(value, side, speed, diffusivity)
        inner = wide - 2 if side else 1
        emit_last(
            inner,
            nearly[side]
            + from_beyond(edge[side, 1 : deep + 1], side, speeds_of(inner)[0], diffusivity),
        )

    def emit(side, plane):
        x_sides[side] = jnp.where(inside[side], plane, 0.0)

    planes_advanced(
        range(2), lambda side: beside(side, outer_of),
        lambda side, to: beside(side, inner_of) if side == to else field[last(side)],
        y_beside,
        lambda side: jnp.stack(
            [rate_of(rows[3:4], coefficients) for rows in other_rows(side)]
        ),
        lambda side: [
            rows_for_species([rows[d : d + 1] for rows in other_rows(side)], species)
            for d in range(3)
        ],
        diffusivity, mix, emit,
    )
    planes_advanced(
        range(2),
        lambda side: edge[side, 1 : deep + 1],
        lambda side, to: x_sides[side] if side == to else edges[1 + side, 1 : deep + 1],
        lambda side, to: edge[side, 2 * to : 2 * to + deep],
        lambda side: own_rates(flow, coefficients, last(side), deep),
        lambda side: speeds_of(last(side)),
        diffusivity, mix, lambda side, plane: emit_last(last(side), plane),
    )
    for copy in copies.values():
        copy.wait()


def project_kernel(shape, ranks, field, component, vertical, factor_rows, out):
    wide, deep, species, up = shape
    ranks_a, ranks_d = ranks
    each = deep + 2
    cells = [field[x, y] for y in range(deep) for x in range(wide)]
    high, low = halves_of(jnp.concatenate(cells, axis=0))
    both = jnp.concatenate([high, low], axis=1)
    high, low = halves_of(vertical[...])
    left = jnp.concatenate(
        [jnp.concatenate([high, high], axis=1), jnp.concatenate([low, low], axis=1)], axis=0
    )
    on_d = lax.dot_general(
        left, both, (((1,), (1,)), ((), ())), preferred_element_type=jnp.float32
    )
    on_d = on_d[:ranks_d] + on_d[ranks_d:]
    size = wide * species
    on_d = jnp.concatenate([on_d[:, y * size : (y + 1) * size] for y in range(deep)], axis=0)
    on_both = product(on_d, component[...], (1, 1))
    for y in range(deep):
        out[pl.ds(y, ranks_d, stride=each), :] = on_both[y * ranks_d : (y + 1) * ranks_d]
    for row in range(2):
        out[pl.ds(deep + row, ranks_d, stride=each), :] = jnp.broadcast_to(
            factor_rows[row : row + 1], (ranks_d, 128)
        )


def snapshot_and_project_kernel(shape, ranks, *refs):
    snapshot_kernel(shape, *refs[:8], *refs[11:14])
    project_kernel(shape, ranks, refs[11], *refs[8:11], refs[14])


def core_kernel(counts, got, out):
    rows, columns, ranks_a, tall, deep = counts
    devices, each, all_of = rows * columns, deep + 2, tall + deep
    own = 128 // ranks_a
    in_order = [(r, g) for r in range(2) for g in range(rows)]

    whole = jnp.concatenate(
        [
            jnp.concatenate(
                [
                    got[pl.ds(row * columns * each + 2 * g + r, columns, stride=each), :]
                    for r, g in in_order
                ],
                axis=0,
            )
            for row in range(rows)
        ],
        axis=1,
    )

    def factor(at):
        both = got[pl.ds(at, devices, stride=each), :]
        return jnp.concatenate([both[:, :64], both[:, 64:]], axis=0)

    east, north = factor(deep), factor(deep + 1)
    half = product(whole, north, (0, 0))

    def part(array, a, r, g):
        at = (g * ranks_a + a) * own + r * columns
        return array[at : at + columns]

    half = jnp.concatenate(
        [
            jnp.concatenate([part(half, a, r, g) for r, g in in_order], axis=0)
            for a in range(ranks_a)
        ],
        axis=1,
    )
    core = product(east, half, (0, 0))
    half = product(east, core, (1, 0))
    ranks_c, size = north.shape[1], len(in_order) * columns
    split = [slice(a * ranks_c, (a + 1) * ranks_c) for a in range(ranks_a)]
    core = jnp.concatenate(
        [core[row * own : (row + 1) * own, at] for row in range(rows) for at in split], axis=0
    ).T
    whole = product(jnp.concatenate([half[:, at] for at in split], axis=0), north, (1, 1))
    whole = jnp.concatenate(
        [
            whole[at : at + columns]
            for row in range(rows)
            for a in range(ranks_a)
            for r in range(2)
            for at in [a * size + (r * rows + row) * columns]
        ],
        axis=0,
    ).T
    flat = out.reshape(devices * all_of, 128)
    for row in range(rows):
        lanes = slice(row * 128, (row + 1) * 128)
        for column in range(columns):
            out[row * columns + column, 0:tall] = core[column * tall : (column + 1) * tall, lanes]
        for at, (r, g) in enumerate(in_order):
            flat[pl.ds(row * columns * all_of + tall + 2 * g + r, columns, stride=all_of), :] = whole[
                at * columns : (at + 1) * columns, lanes
            ]


def expand_kernel(shape, ranks, tall, got, field, wide_rows, vertical, residual, core, full):
    wide, deep, species, up = shape
    ranks_a, ranks_d = ranks
    each = tall + deep
    component = where_equal(
        jnp.concatenate([wide_rows[...]] * wide, axis=0),
        lambda at: at // species,
        lambda at: x_of(at, wide),
    )
    for y in range(deep):
        on_d = got[pl.ds(tall + y, ranks_d, stride=each), :]
        on_a = product(on_d, vertical[...], (0, 0))
        full[y] = product(component, on_a, (1, 0))
    for x in range(wide):
        residual[:, x] = jnp.swapaxes(
            field[x] - full[:, x * species : (x + 1) * species, :], 0, 1
        )
    turned = [got[pl.ds(c, ranks_d, stride=each), :].T for c in range(tall)]
    core[...] = jnp.swapaxes(jnp.stack(turned), 0, 1)


def swapped(one, other, axes):
    got = []
    for first, face in enumerate((one, other)):
        couples = [(i, i + 1) for i in range(first, lax.axis_size(axes) - 1, 2)]
        got.append(lax.ppermute(face, axes, couples + [(b, a) for a, b in couples]))
    return got


def faces_beside(faces):
    x_one, x_other, y_one, y_other = faces
    y_one, y_other = swapped(y_one, y_other, COLUMN)
    x_one, x_other = swapped(x_one, x_other, ROW)
    return x_one, x_other, y_one, y_other


def whole_factors(tucker_factor_east, tucker_factor_north):
    rows, columns = lax.axis_size(ROW), lax.axis_size(COLUMN)

    def shares(factor, holders, axes):
        count = -(-factor.shape[0] // holders)
        padded = jnp.pad(factor, ((0, count * holders - factor.shape[0]), (0, 0)))
        return lax.dynamic_slice_in_dim(padded, lax.axis_index(axes) * count, count, 0)

    east = shares(tucker_factor_east, columns, COLUMN)
    north = shares(tucker_factor_north, rows, ROW)
    sent = jnp.concatenate([east.reshape(-1), north.reshape(-1)])
    sent = jnp.pad(sent, (0, -sent.size % 128)).reshape(1, -1, 128)
    sent = jnp.broadcast_to(sent, (rows * columns,) + sent.shape[1:])
    got = lax.all_to_all(sent, EVERY, 0, 0, tiled=True).reshape(rows, columns, -1)
    whole_east = got[:, :, : east.size].reshape(rows, -1, east.shape[1])
    whole_east = whole_east[:, : tucker_factor_east.shape[0]].reshape(-1, east.shape[1])
    whole_north = got[:, :, east.size : east.size + north.size]
    whole_north = whole_north.reshape(rows, columns, *north.shape).transpose(1, 0, 2, 3)
    whole_north = whole_north.reshape(columns, -1, north.shape[1])
    whole_north = whole_north[:, : tucker_factor_north.shape[0]].reshape(-1, north.shape[1])
    return whole_east, whole_north


def compress_and_expand(snapshot, east, north, vertical, component):
    rows, columns = lax.axis_size(ROW), lax.axis_size(COLUMN)
    devices = rows * columns
    (wide, deep, _, _), (_, ranks_a) = snapshot.shape, component.shape
    ranks_d = vertical.shape[1]
    ranks_b, ranks_c = east.shape[1], north.shape[1]
    projected = jnp.einsum("xysz,sa->xyaz", snapshot, component, precision=HIGHEST)
    projected = jnp.einsum("xyaz,zd->dyxa", projected, vertical, precision=HIGHEST)
    pairs = ranks_a * ranks_d
    share = -(-pairs // devices)
    flat = jnp.transpose(projected, (0, 3, 1, 2)).reshape(pairs, deep, wide)
    flat = jnp.pad(flat, ((0, share * devices - pairs), (0, 0), (0, 0)))
    flat = flat.reshape(devices, share, deep, wide).transpose(0, 2, 3, 1)
    flat = lax.all_to_all(
        flat.reshape(devices, deep, wide * share), EVERY, 0, 0, tiled=True
    )
    whole = flat.reshape(rows, columns * deep, wide, share)
    part = jnp.einsum("gyxp,yc->cgxp", whole, north, precision=HIGHEST)
    part = part.reshape(ranks_c, rows * wide, share)
    core = jnp.einsum("cxp,xb->cbp", part, east, precision=HIGHEST)
    part = jnp.einsum("cbp,xb->cxp", core, east, precision=HIGHEST)
    whole = jnp.einsum("cxp,yc->yxp", part, north, precision=HIGHEST)
    own_b, own_c = ranks_b // rows, ranks_c // columns

    def pieces(array, tall, broad):
        array = array.reshape(columns, tall, rows, broad, share)
        return array.transpose(2, 0, 1, 3, 4).reshape(devices, tall * broad * share)

    sent = jnp.concatenate([pieces(core, own_c, own_b), pieces(whole, deep, wide)], axis=1)
    sent = jnp.pad(sent, ((0, 0), (0, -sent.shape[1] % 1024)))
    got = lax.all_to_all(
        sent.reshape(devices, -1, 128), EVERY, 0, 0, tiled=True
    ).reshape(devices, -1)

    def ranks_together(array, tall, broad):
        array = array.reshape(devices, tall, broad, share).transpose(0, 3, 2, 1)
        array = array.reshape(devices * share, broad, tall)[:pairs]
        return array.reshape(ranks_d, ranks_a, broad, tall)

    core_size = own_c * own_b * share
    core = ranks_together(got[:, :core_size], own_c, own_b).transpose(1, 2, 3, 0)
    expanded = ranks_together(got[:, core_size : core_size + deep * wide * share], deep, wide)
    expanded = jnp.einsum("daxy,zd->axyz", expanded, vertical, precision=HIGHEST)
    expanded = jnp.einsum("axyz,sa->sxyz", expanded, component, precision=HIGHEST)
    return core, snapshot.transpose(2, 0, 1, 3) - expanded


def body(
    mixture_fields_initial,
    flow_speed_vector,
    thermal_field,
    mass_diffusivity,
    arrhenius_constant,
    arrhenius_energy_temp,
    production_coefficients,
    tucker_factor_east,
    tucker_factor_north,
    tucker_factor_vertical,
    tucker_factor_component,
):
    species, wide, deep, up = mixture_fields_initial.shape
    shape = (wide, deep, species, up)
    cells = wide * deep * species * up
    rows, columns = lax.axis_size(ROW), lax.axis_size(COLUMN)
    devices = rows * columns
    ranks_a, ranks_d = tucker_factor_component.shape[1], tucker_factor_vertical.shape[1]
    ranks_b, ranks_c = tucker_factor_east.shape[1], tucker_factor_north.shape[1]
    own_b, own_c = ranks_b // rows, ranks_c // columns
    kernels_fit = (
        ranks_d == devices
        and wide * ranks_a == 128
        and own_b * ranks_a == 128
        and deep == own_c == 8
        and ranks_b == ranks_c == 64
        and wide == 2 * columns
        and deep == 2 * rows
    )

    row, column = lax.axis_index(ROW), lax.axis_index(COLUMN)
    own = jnp.stack([1 - row % 2, 1 - column % 2, row, column]).astype(jnp.int32)
    face_shapes = [(deep, species, up)] * 2 + [(wide, species, up)] * 2
    faces = vmem_call(
        functools.partial(faces_kernel, shape), face_shapes, 1, 2,
        scratch=[mixture_fields_initial.shape], placed=[1], copies=FACE_COPIES,
    )(own, pltpu.with_memory_space_constraint(mixture_fields_initial, pltpu.HBM))
    faces = faces_beside(faces)
    def with_fetches(kernel, given, small, outs, **cost):
        call = vmem_call(
            kernel, outs, 0, 1 + len(small),
            scratch=[array.shape for array in small], placed=range(1, 1 + len(small)),
            copies=len(small), **cost,
        )
        return call(
            given, *(pltpu.with_memory_space_constraint(array, pltpu.HBM) for array in small)
        )

    field, rates, speeds, coefficients, mix, turned, upright, east, north = with_fetches(
        functools.partial(prepare_kernel, shape),
        mixture_fields_initial,
        (
            flow_speed_vector, thermal_field, mass_diffusivity[None], arrhenius_constant[None],
            arrhenius_energy_temp[None], production_coefficients, tucker_factor_component.T,
            tucker_factor_vertical.T, tucker_factor_east, tucker_factor_north,
        ),
        [
            shape, shape, (4, wide, deep, up), (3, species, up), (species, 128),
            (ranks_a, species), (ranks_d, up), tucker_factor_east.shape, tucker_factor_north.shape,
        ],
        flops=4 * cells, moved=12 * cells, exps=cells,
    )
    block, last_block = (
        vmem_call(
            functools.partial(block_kernel, shape, held), [shape], 0, 4 + held,
            flops=60 * cells, moved=8 * cells,
        )
        for held in (1, 0)
    )
    advance = vmem_call(
        functools.partial(advance_kernel, shape), [shape] + face_shapes, 1, 8,
        flops=4 * cells, moved=8 * cells,
    )
    fixed = (rates, speeds, coefficients, mix)
    for substep in range(SUB - 1):
        field, *faces = advance(
            own, *block(field, *fixed), *faces, speeds, coefficients
        )
        first = field
        faces = faces_beside(faces)
    high = 2 * species + 4
    last_given = (*block(field, *fixed), *faces, speeds, coefficients)
    snapshot_outs = [shape] + [(wide * high, up)] * 2
    if kernels_fit:
        own, _ = lax.optimization_barrier((own, first))
        squeeze, wide_rows, factor_rows = vmem_call(
            functools.partial(matrices_kernel, shape),
            [(wide * ranks_a, wide * species), (species, wide * ranks_a), (2, 128)], 1, 4,
        )(own, turned, east, north)
        snapshot, *y_faces, sent = vmem_call(
            functools.partial(snapshot_and_project_kernel, shape, (ranks_a, ranks_d)),
            snapshot_outs + [(devices * (deep + 2), 128)], 1, 11,
            flops=60 * cells, moved=8 * cells,
        )(own, *last_given, squeeze, upright, factor_rows)
    else:
        snapshot, *y_faces = vmem_call(
            functools.partial(snapshot_kernel, shape), snapshot_outs, 1, 8,
            flops=4 * cells, moved=8 * cells,
        )(own, *last_given)
    y_faces = swapped(*y_faces, COLUMN)
    if kernels_fit:
        got = lax.all_to_all(
            sent.reshape(devices, (deep + 2) // 2, 2, 128), EVERY, 0, 0, tiled=True
        )
        (sent,) = vmem_call(
            functools.partial(core_kernel, (rows, columns, ranks_a, own_c, deep)),
            [(devices, own_c + deep, 128)], 0, 1, flops=60 * cells, moved=4 * cells,
        )(got.reshape(devices * (deep + 2), 128))
        sent, later = lax.optimization_barrier((sent, snapshot))
        got = lax.all_to_all(sent, EVERY, 0, 0, tiled=True)
        residual, tucker_core = vmem_call(
            functools.partial(expand_kernel, shape, (ranks_a, ranks_d), own_c),
            [mixture_fields_initial.shape, (ranks_a * own_b, own_c, ranks_d)], 0, 4,
            flops=60 * cells, moved=8 * cells,
            scratch=[(deep, wide * species, up)],
        )(
            got.reshape(devices * (own_c + deep), 128),
            snapshot,
            wide_rows,
            upright,
        )
        tucker_core = tucker_core.reshape(ranks_a, own_b, own_c, ranks_d)
    else:
        east, north = whole_factors(tucker_factor_east, tucker_factor_north)
        tucker_core, residual = compress_and_expand(
            snapshot, east, north, tucker_factor_vertical, tucker_factor_component
        )
        later = snapshot
    fixed = fixed[1:]
    (third,) = last_block(later, *fixed)
    x_faces = vmem_call(
        functools.partial(wide_faces_kernel, shape),
        [((deep + 1) * high - 4 + spare, up) for spare in (SPARE_X, 0)], 1, 5,
        flops=cells, moved=cells,
    )(own, snapshot, *y_faces, speeds)
    x_faces = swapped(*x_faces, ROW)
    edges, ends, nearly, inmost = vmem_call(
        functools.partial(third_step_kernel, shape, (rows, columns)),
        [
            (4, deep + 2, species, up), (2, 2, 8, up), (2, deep, species, up),
            mixture_fields_initial.shape,
        ], 1, 8,
        flops=120 * cells, moved=16 * cells,
        scratch=[(wide, deep + 2, species, up), (species, wide - 4, deep, up)], placed=[11],
        copies=-(-(wide - 4) // 4),
    )(own, third, snapshot, *y_faces, *fixed)
    own, _ = lax.optimization_barrier((own, tucker_core))
    (mixture_fields_final,) = vmem_call(
        functools.partial(fourth_step_kernel, shape, (rows, columns)),
        [mixture_fields_initial.shape], 1, 11,
        flops=60 * cells, moved=8 * cells,
        scratch=[(2, deep + 2, species, up), (2, deep, species, up), (species, 4, deep, up)],
        placed=[4, 11], copies=4, aliases={4: 0},
    )(own, edges, ends, nearly, inmost, snapshot, *x_faces, *fixed)
    return (mixture_fields_final, residual, tucker_core)


def solution(mesh):
    in_specs = (
        P(None, "gx", ("gy", "ga"), None),
        P(None, "gx", ("gy", "ga"), None),
        P("gx", ("gy", "ga"), None),
        P(),
        P(),
        P(),
        P(),
        P("gx", None),
        P(("gy", "ga"), None),
        P(),
        P(),
    )
    out_specs = (
        P(None, "gx", ("gy", "ga"), None),
        P(None, "gx", ("gy", "ga"), None),
        P(None, "gx", ("gy", "ga"), None),
    )
    return jax.shard_map(body, mesh=mesh, in_specs=in_specs, out_specs=out_specs, check_vma=False)
```

```python
import functools

import jax
import jax.numpy as jnp
from jax import lax
from jax.experimental import pallas as pl
from jax.experimental.pallas import tpu as pltpu
from jax.sharding import PartitionSpec as P

SUB = 2


time_step = 0.5

ROW = "gx"
COLUMN = ("gy", "ga")
EVERY = ("gx", "gy", "ga")
HIGHEST = lax.Precision.HIGHEST
VMEM_LIMIT = 4 * 1024 * 1024
FACE_COPIES = 4

SPARE_X = 104


def vmem_call(
    kernel, outs, in_smem, n_in, flops=0, moved=0, exps=0, scratch=(), placed=(), copies=0, aliases={}
):
    vmem = pl.BlockSpec(memory_space=pltpu.VMEM)
    smem = pl.BlockSpec(memory_space=pltpu.SMEM)
    anywhere = pl.BlockSpec(memory_space=pl.ANY)
    ins = [smem] * in_smem + [vmem] * (n_in - in_smem)
    specs = [anywhere if at in placed else spec for at, spec in enumerate(ins + [vmem] * len(outs))]
    return pl.pallas_call(
        kernel,
        in_specs=specs[:n_in],
        out_specs=specs[n_in:],
        out_shape=[jax.ShapeDtypeStruct(shape, jnp.float32) for shape in outs],
        scratch_shapes=[pltpu.VMEM(shape, jnp.float32) for shape in scratch]
        + [pltpu.SemaphoreType.DMA((copies,))] * (copies > 0),
        input_output_aliases=aliases,
        compiler_params=pltpu.CompilerParams(vmem_limit_bytes=VMEM_LIMIT),
        cost_estimate=pl.CostEstimate(flops=flops, bytes_accessed=moved, transcendentals=exps),
    )


def planes_of_species(ref, species, plane, at):
    return jnp.concatenate(
        [ref[pl.ds(first * plane + at, 8, stride=plane), :] for first in range(0, species, 8)], axis=0
    )


def store_planes_of_species(ref, species, plane, at, value):
    for first in range(0, species, 8):
        ref[pl.ds(first * plane + at, 8, stride=plane), :] = value[first : first + 8]


def faces_kernel(shape, own_ref, given, x_one, x_other, y_one, y_other, held, semaphores):
    wide, deep, species, up = shape
    even_x, even_y = own_ref[0] == 1, own_ref[1] == 1
    plane, together = wide * deep, -(-wide // FACE_COPIES)
    copies = {}
    for x in range(0, wide, together):
        some = pl.ds(x, min(together, wide - x))
        copies[x] = pltpu.make_async_copy(
            given.at[:, some], held.at[:, some], semaphores.at[x // together]
        )
        copies[x].start()
    rows = held.reshape(species * plane, up)
    for x in range(wide):
        if x in copies:
            copies[x].wait()
        low = planes_of_species(rows, species, plane, x * deep)
        high = planes_of_species(rows, species, plane, x * deep + deep - 1)
        y_one[x] = jnp.where(even_y, high, low)
        y_other[x] = jnp.where(even_y, low, high)
        if x in (0, wide - 1):
            face = jnp.swapaxes(held[:, x], 0, 1)
            to_one_or_other(even_x, x_one, x_other, x > 0, face)


def tiled(matrix, count):
    size = matrix.shape[1]
    column = lax.broadcasted_iota(jnp.int32, (size, size * count), 1) % size
    pick = (column == lax.broadcasted_iota(jnp.int32, (size, size * count), 0)).astype(jnp.float32)
    return jnp.dot(matrix, pick, precision=HIGHEST, preferred_element_type=jnp.float32)


def where_equal(matrix, of_row, of_column):
    row = lax.broadcasted_iota(jnp.int32, matrix.shape, 0)
    column = lax.broadcasted_iota(jnp.int32, matrix.shape, 1)
    return jnp.where(of_row(row) == of_column(column), matrix, 0.0)


def fetched(sources, held, semaphores):
    copies = [
        pltpu.make_async_copy(source, target, semaphores.at[at])
        for at, (source, target) in enumerate(zip(sources, held))
    ]
    for copy in copies:
        copy.start()
    return copies


def prepare_kernel(shape, given, *refs):
    wide, deep, species, up = shape
    held, semaphores = refs[-7:-1], refs[-1]
    copies = fetched(refs[:6], held, semaphores)
    flow, thermal, diffusivity, constant, energy, production = held
    field, rates, speeds, coefficients, mix = refs[6:-7]
    for x in range(wide):
        field[x] = jnp.swapaxes(given[:, x], 0, 1)
    for copy in copies:
        copy.wait()
    eye = (
        lax.broadcasted_iota(jnp.int32, (species, species), 0)
        == lax.broadcasted_iota(jnp.int32, (species, species), 1)
    )
    for at, ref in enumerate((diffusivity, constant, energy)):
        column = jnp.sum(jnp.where(eye, ref[...], 0.0), axis=1, keepdims=True)
        coefficients[at] = jnp.broadcast_to(time_step * column if at == 0 else column, (species, up))
    for x in range(wide):
        speeds[3, x] = thermal[x]
        inverse = -1.0 / thermal[x]
        for d in range(3):
            speeds[d, x] = (0.5 * time_step) * flow[d, x]
        for y in range(deep):
            rates[x, y] = coefficients[1] * jnp.exp(coefficients[2] * inverse[y : y + 1])
    mix[...] = tiled(time_step * production[...], mix.shape[1] // species)


def matrices_kernel(shape, own_ref, *refs):
    wide, _, species, _ = shape
    held, semaphores = refs[-5:-1], refs[-1]
    copies = fetched(refs[:4], held, semaphores)
    turned, vertical, east, north = held
    squeeze, wide_rows, upright, factor_rows = refs[4:-5]
    for copy in copies:
        copy.wait()
    ranks_a = turned.shape[0]
    full = tiled(turned[...], wide)
    full = [jnp.broadcast_to(full[a : a + 1], (wide, full.shape[1])) for a in range(ranks_a)]
    full = jnp.concatenate(full, axis=0)
    squeeze[...] = where_equal(full, lambda at: at % wide, lambda at: at // species)
    pick = lax.broadcasted_iota(jnp.int32, (ranks_a, ranks_a * wide), 1) // wide
    pick = pick == lax.broadcasted_iota(jnp.int32, pick.shape, 0)
    wide_rows[...] = lax.dot_general(
        turned[...], pick.astype(jnp.float32), (((0,), (0,)), ((), ())), precision=HIGHEST,
        preferred_element_type=jnp.float32,
    )
    upright[...] = vertical[...]

    def two_rows(ref, at):
        return jnp.concatenate([ref[pl.ds(2 * at + row, 1), :] for row in range(2)], axis=1)

    factor_rows[0:1] = two_rows(east, own_ref[3])
    factor_rows[1:2] = two_rows(north, own_ref[2])


def halves_of(value):
    high = value.astype(jnp.bfloat16)
    return high, (value - high.astype(jnp.float32)).astype(jnp.bfloat16)


def product(a, b, contract):
    def dot(left, right):
        return lax.dot_general(
            left, right, ((contract[:1], contract[1:]), ((), ())),
            preferred_element_type=jnp.float32,
        )

    (a_high, a_low), (b_high, b_low) = halves_of(a), halves_of(b)
    return dot(a_high, b_high) + (dot(a_high, b_low) + dot(a_low, b_high))


def mixing(rows):
    species, size = rows.shape
    full = jnp.concatenate([rows] * (size // species), axis=0)
    high, low = halves_of(
        where_equal(full, lambda at: at // species, lambda at: at // species)
    )
    return jnp.concatenate(
        [jnp.concatenate([high, high], axis=1), jnp.concatenate([low, low], axis=1)], axis=0
    )


def reacted(cells, mix):
    species, up = cells[0].shape
    size = mix.shape[0] // 2
    group = size // species
    cells = cells + [jnp.zeros_like(cells[0])] * (-len(cells) % group)
    right = []
    for at in range(0, len(cells), group):
        high, low = halves_of(jnp.concatenate(cells[at : at + group], axis=0))
        right.append(jnp.concatenate([high, low], axis=0))
    produced = jnp.dot(mix, jnp.concatenate(right, axis=1), preferred_element_type=jnp.float32)
    produced = produced[:size] + produced[size:]
    return [
        produced[cell * species : (cell + 1) * species, at * up : (at + 1) * up]
        for at in range(len(right))
        for cell in range(group)
    ]


def sources(here, rates):
    made = rates * here * pltpu.roll(here, here.shape[1] - 1, 1)
    return [made[cell] for cell in range(here.shape[0])]


def advanced(here, x_minus, x_plus, y_minus, y_plus, speeds, diffusivity, produced):
    up = here.shape[2]
    lane = lax.broadcasted_iota(jnp.int32, here.shape, 2)
    z_minus = jnp.where(lane == 0, 0.0, pltpu.roll(here, 1, 2))
    z_plus = jnp.where(lane == up - 1, 0.0, pltpu.roll(here, up - 1, 2))
    laplace = (x_plus + x_minus) + (y_plus + y_minus) + (z_plus + z_minus) - 6.0 * here
    advect = (
        speeds[0] * (x_plus - x_minus)
        + speeds[1] * (y_plus - y_minus)
        + speeds[2] * (z_plus - z_minus)
    )
    return here + diffusivity * laplace - advect + jnp.stack(produced)


def rows_for_species(rows, species):
    return jnp.stack([jnp.broadcast_to(row, (species, row.shape[1])) for row in rows])


def own_speeds(flow, x, deep):
    return [[flow[d, x, pl.ds(y, 1), :] for y in range(deep)] for d in range(3)]


def planes_advanced(planes, here, x_beside, y_beside, rates, speeds, diffusivity, mix, emit, together=4):
    for at in range(0, len(planes), together):
        some = planes[at : at + together]
        cells, counts = [], []
        for x in some:
            made = sources(here(x), rates(x))
            counts.append((len(cells), len(cells) + len(made)))
            cells += made
        produced = reacted(cells, mix)
        for x, (start, end) in zip(some, counts):
            emit(
                x,
                advanced(
                    here(x), x_beside(x, 0), x_beside(x, 1), y_beside(x, 0), y_beside(x, 1),
                    speeds(x), diffusivity, produced[start:end],
                ),
            )


def rate_of(temperature, coefficients):
    return coefficients[1] * jnp.exp(coefficients[2] * (-1.0 / temperature))


def own_rates(flow, coefficients, x, deep):
    inverse = -1.0 / flow[3, x]
    return jnp.stack(
        [coefficients[1] * jnp.exp(coefficients[2] * inverse[y : y + 1]) for y in range(deep)]
    )


def block_kernel(shape, held, field, *refs):
    wide, deep, species, up = shape
    rates, (flow, coefficients, mix_ref, out) = refs[0] if held else None, refs[held:]

    def x_beside(x, side):
        at = x + 2 * side - 1
        return field[at] if 0 <= at < wide else jnp.zeros((deep, species, up), jnp.float32)

    def y_beside(x, side):
        here, none = field[x], jnp.zeros((1, species, up), jnp.float32)
        return jnp.concatenate([here[1:], none] if side else [none, here[:-1]], axis=0)

    def emit(x, plane):
        out[x] = plane

    planes_advanced(
        range(wide), lambda x: field[x], x_beside, y_beside,
        lambda x: rates[x] if held else own_rates(flow, coefficients, x, deep),
        lambda x: [rows_for_species(speed, species) for speed in own_speeds(flow, x, deep)],
        coefficients[0][None], mixing(mix_ref[...]), emit,
    )


def from_beyond(value, side, speed, diffusivity):
    across = speed * value
    return diffusivity * value - across if side else diffusivity * value + across


def finish(shape, refs, emit):
    wide, deep, species, up = shape
    own_ref, block, x_one, x_other, y_one, y_other, flow, coefficients = refs
    even_x, even_y = own_ref[0] == 1, own_ref[1] == 1
    diffusivity = coefficients[0][None]

    def row(d, x, y):
        return jnp.broadcast_to(flow[d, x, pl.ds(y, 1), :], (species, up))

    for x in range(wide):
        plane = block[x]
        before = jnp.where(even_y, y_other[x], y_one[x])
        after = jnp.where(even_y, y_one[x], y_other[x])
        before = from_beyond(before, 0, row(1, x, 0), diffusivity[0])
        after = from_beyond(after, 1, row(1, x, deep - 1), diffusivity[0])
        plane = jnp.concatenate(
            [(plane[0] + before)[None], plane[1:-1], (plane[-1] + after)[None]], axis=0
        )
        for side in range(2):
            if x == (wide - 1 if side else 0):
                one, other = (x_one, x_other) if side else (x_other, x_one)
                value = jnp.where(even_x, one[...], other[...])
                speed = rows_for_species(own_speeds(flow, x, deep)[0], species)
                plane = plane + from_beyond(value, side, speed, diffusivity)
        emit(x, plane)


def to_one_or_other(even, one, other, high, value):
    first = even if high else jnp.logical_not(even)

    @pl.when(first)
    def _():
        one[...] = value

    @pl.when(jnp.logical_not(first))
    def _():
        other[...] = value


def advance_kernel(shape, *refs):
    wide, deep, _, _ = shape
    own_ref, (out, x_one, x_other, y_one, y_other) = refs[0], refs[8:]
    even_x, even_y = own_ref[0] == 1, own_ref[1] == 1

    def emit(x, plane):
        out[x] = plane
        low, high = plane[0], plane[deep - 1]
        y_one[x] = jnp.where(even_y, high, low)
        y_other[x] = jnp.where(even_y, low, high)
        if x == 0:
            to_one_or_other(even_x, x_one, x_other, False, plane)
        if x == wide - 1:
            to_one_or_other(even_x, x_one, x_other, True, plane)

    finish(shape, refs[:8], emit)


def outer_of(cell, species):
    return slice(2 * cell * species, (2 * cell + 1) * species)


def inner_of(cell, species):
    return slice((2 * cell + 1) * species, (2 * cell + 2) * species)


def flow_of(cell, count, species):
    return slice(2 * count * species + 4 * cell, 2 * count * species + 4 * cell + 4)


def snapshot_kernel(shape, *refs):
    wide, deep, species, _ = shape
    own_ref, flow, (out, y_one, y_other) = refs[0], refs[6], refs[8:]
    even_y = own_ref[1] == 1

    def emit(x, plane):
        out[x] = plane

        def put(low, high, at):
            y_one[at] = jnp.where(even_y, high, low)
            y_other[at] = jnp.where(even_y, low, high)

        def others(y):
            return jnp.concatenate([flow[d, x, pl.ds(y, 1), :] for d in range(4)], axis=0)

        put(plane[0], plane[deep - 1], outer_of(x, species))
        put(plane[1], plane[deep - 2], inner_of(x, species))
        put(others(0), others(deep - 1), flow_of(x, wide, species))

    finish(shape, refs[:8], emit)


def wide_faces_kernel(shape, own_ref, field, y_one, y_other, flow, x_one, x_other):
    wide, deep, species, _ = shape
    even_x, even_y = own_ref[0] == 1, own_ref[1] == 1

    def face(outer, inner, out):
        for y in range(deep):
            out[outer_of(y, species)] = field[outer, y]
            out[inner_of(y, species)] = field[inner, y]
            out[flow_of(y, deep + 1, species)] = jnp.concatenate(
                [flow[d, outer, y : y + 1, :] for d in range(4)], axis=0
            )
        at = outer_of(outer, species)
        out[outer_of(deep, species)] = choose(even_y, y_one, y_other, 0, at)
        out[inner_of(deep, species)] = choose(even_y, y_one, y_other, 1, at)

    @pl.when(even_x)
    def _():
        face(wide - 1, wide - 2, x_one)
        face(0, 1, x_other)

    @pl.when(jnp.logical_not(even_x))
    def _():
        face(0, 1, x_one)
        face(wide - 1, wide - 2, x_other)


def planes_copied(groups, ready, out, semaphores):
    copies, at = {}, 0
    for group in groups:
        copies[group[-1]] = pltpu.make_async_copy(
            ready.at[:, pl.ds(at, len(group))],
            out.at[:, pl.ds(group[0], len(group))],
            semaphores.at[len(copies)],
        )
        at += len(group)
    return copies


def choose(even, one, other, side, at):
    first, second = (one, other) if side else (other, one)
    return jnp.where(even, first[at], second[at])


def third_step_kernel(
    shape, counts, own_ref, block, field, y_one, y_other, flow, coefficients, mix_ref, edges, ends,
    nearly, out, inner, ready, semaphores,
):
    wide, deep, species, up = shape
    _, columns = counts
    even_y, column = own_ref[1] == 1, own_ref[3]
    inside = (column > 0, column < columns - 1)
    diffusivity, mix = coefficients[0][None], mixing(mix_ref[...])

    def outer(side, x):
        return choose(even_y, y_one, y_other, side, outer_of(x, species))

    def others(side, x):
        return choose(even_y, y_one, y_other, side, flow_of(x, wide, species))

    def here(x):
        return jnp.stack([outer(0, x), outer(1, x)])

    def x_beside(x, side):
        at = x + 2 * side - 1
        return here(at) if 0 <= at < wide else jnp.zeros((2, species, up), jnp.float32)

    def y_beside(x, side):
        beyond = choose(even_y, y_one, y_other, side, inner_of(x, species))
        return jnp.stack([field[x, 0], beyond] if side else [beyond, field[x, deep - 1]])

    def emit(x, plane):
        for side in range(2):
            inner[x, side * (deep + 1)] = jnp.where(inside[side], plane[side], 0.0)

    planes_advanced(
        range(wide), here, x_beside, y_beside,
        lambda x: jnp.stack([rate_of(others(side, x)[3:4], coefficients) for side in range(2)]),
        lambda x: [
            rows_for_species([others(side, x)[d : d + 1] for side in range(2)], species)
            for d in range(3)
        ],
        diffusivity, mix, emit, 16,
    )

    def row(x, y):
        return jnp.broadcast_to(flow[1, x, pl.ds(y, 1), :], (species, up))

    for x in range(wide):
        inner[x, 1] = block[x, 0] + from_beyond(outer(0, x), 0, row(x, 0), diffusivity[0])
        inner[x, 2:deep] = block[x, 1 : deep - 1]
        inner[x, deep] = block[x, deep - 1] + from_beyond(
            outer(1, x), 1, row(x, deep - 1), diffusivity[0]
        )
        if x < 2 or x >= wide - 2:
            edges[x if x < 2 else x - wide + 4] = inner[x]
        if x in (0, wide - 1):
            for side in range(2):
                ends[0 if x == 0 else 1, side, 0:4] = others(side, x)

    inmost = range(2, wide - 2)
    copies = planes_copied(
        [inmost[at : at + 6] for at in range(0, len(inmost), 6)], ready, out, semaphores
    )

    def emit_last(x, plane):
        if x in (1, wide - 2):
            nearly[0 if x == 1 else 1] = plane
        else:
            ready[:, x - 2] = jnp.swapaxes(plane, 0, 1)
        if x in copies:
            copies[x].start()

    def last_beside(x, side):
        at = x + 2 * side - 1
        if at in (0, wide - 1):
            return jnp.zeros((deep, species, up), jnp.float32)
        return inner[at, 1 : deep + 1]

    planes_advanced(
        [*inmost, 1, wide - 2],
        lambda x: inner[x, 1 : deep + 1],
        last_beside,
        lambda x, side: inner[x, 2 * side : 2 * side + deep],
        lambda x: own_rates(flow, coefficients, x, deep),
        lambda x: [rows_for_species(speed, species) for speed in own_speeds(flow, x, deep)],
        diffusivity, mix, emit_last,
    )
    for copy in copies.values():
        copy.wait()


def fourth_step_kernel(
    shape, counts, own_ref, edges, ends, nearly, _, field, x_one, x_other, flow, coefficients,
    mix_ref, out, edge, x_sides, ready, semaphores,
):
    wide, deep, species, up = shape
    rows, _ = counts
    even_x, row = own_ref[0] == 1, own_ref[2]
    inside = (row > 0, row < rows - 1)
    diffusivity, mix = coefficients[0][None], mixing(mix_ref[...])
    def beside(side, rows_of, cells=range(deep)):
        return jnp.stack(
            [choose(even_x, x_one, x_other, side, rows_of(cell, species)) for cell in cells]
        )

    def corners(side):
        return [beside(side, rows_of, [deep])[0] for rows_of in (outer_of, inner_of)]

    def last(side):
        return wide - 1 if side else 0

    def y_beside(side, to):
        here, corner = beside(side, outer_of), corners(side)[to][None]
        return jnp.concatenate([here[1:], corner] if to else [corner, here[:-1]], axis=0)

    def other_rows(side):
        return [
            choose(even_x, x_one, x_other, side, flow_of(y, deep + 1, species)) for y in range(deep)
        ]

    outermost = [[0], [1], [wide - 2], [wide - 1]]
    copies = planes_copied(outermost, ready, out, semaphores)

    def emit_last(x, plane):
        ready[:, outermost.index([x])] = jnp.swapaxes(plane, 0, 1)
        copies[x].start()

    def speeds_of(x):
        return [rows_for_species(speed, species) for speed in own_speeds(flow, x, deep)]

    for side in range(2):
        x = last(side)
        low, high = corners(side)
        value = jnp.concatenate([low[None], beside(side, outer_of), high[None]], axis=0)
        speed = rows_for_species(
            [ends[side, 0, 0:1]] + own_speeds(flow, x, deep)[0] + [ends[side, 1, 0:1]], species
        )
        edge[side] = edges[3 * side] + from_beyond(value, side, speed, diffusivity)
        inner = wide - 2 if side else 1
        emit_last(
            inner,
            nearly[side]
            + from_beyond(edge[side, 1 : deep + 1], side, speeds_of(inner)[0], diffusivity),
        )

    def emit(side, plane):
        x_sides[side] = jnp.where(inside[side], plane, 0.0)

    planes_advanced(
        range(2), lambda side: beside(side, outer_of),
        lambda side, to: beside(side, inner_of) if side == to else field[last(side)],
        y_beside,
        lambda side: jnp.stack(
            [rate_of(rows[3:4], coefficients) for rows in other_rows(side)]
        ),
        lambda side: [
            rows_for_species([rows[d : d + 1] for rows in other_rows(side)], species)
            for d in range(3)
        ],
        diffusivity, mix, emit,
    )
    planes_advanced(
        range(2),
        lambda side: edge[side, 1 : deep + 1],
        lambda side, to: x_sides[side] if side == to else edges[1 + side, 1 : deep + 1],
        lambda side, to: edge[side, 2 * to : 2 * to + deep],
        lambda side: own_rates(flow, coefficients, last(side), deep),
        lambda side: speeds_of(last(side)),
        diffusivity, mix, lambda side, plane: emit_last(last(side), plane),
    )
    for copy in copies.values():
        copy.wait()


def project_kernel(shape, ranks, field, component, vertical, factor_rows, out):
    wide, deep, species, up = shape
    ranks_a, ranks_d = ranks
    each = deep + 2
    cells = [field[x, y] for y in range(deep) for x in range(wide)]
    high, low = halves_of(jnp.concatenate(cells, axis=0))
    both = jnp.concatenate([high, low], axis=1)
    high, low = halves_of(vertical[...])
    left = jnp.concatenate(
        [jnp.concatenate([high, high], axis=1), jnp.concatenate([low, low], axis=1)], axis=0
    )
    on_d = lax.dot_general(
        left, both, (((1,), (1,)), ((), ())), preferred_element_type=jnp.float32
    )
    on_d = on_d[:ranks_d] + on_d[ranks_d:]
    size = wide * species
    on_d = jnp.concatenate([on_d[:, y * size : (y + 1) * size] for y in range(deep)], axis=0)
    on_both = product(on_d, component[...], (1, 1))
    for y in range(deep):
        out[pl.ds(y, ranks_d, stride=each), :] = on_both[y * ranks_d : (y + 1) * ranks_d]
    for row in range(2):
        out[pl.ds(deep + row, ranks_d, stride=each), :] = jnp.broadcast_to(
            factor_rows[row : row + 1], (ranks_d, 128)
        )


def core_kernel(counts, got, out):
    rows, columns, ranks_a, tall, deep = counts
    devices, each = rows * columns, deep + 2
    own = 128 // ranks_a

    whole = jnp.concatenate(
        [
            jnp.concatenate(
                [got[pl.ds((row * columns + column) * each, deep), :] for column in range(columns)],
                axis=0,
            )
            for row in range(rows)
        ],
        axis=1,
    )

    def in_order(at, of_row):
        both = got[pl.ds(at, devices, stride=each), :]
        halves = jnp.concatenate([both[:, :64], both[:, 64:]], axis=0)
        pick = jnp.full((2 * devices, 2 * devices), 1.0, jnp.float32)
        return product(where_equal(pick, of_row, lambda at: at), halves, (1, 0))

    east = in_order(deep, lambda at: at % 2 * devices + at // 2)
    north = in_order(
        deep + 1, lambda at: at % 2 * devices + at % deep // 2 * columns + at // deep
    )

    def by_rank(array):
        return jnp.concatenate(
            [
                jnp.concatenate(
                    [
                        array[(row * ranks_a + a) * own : (row * ranks_a + a + 1) * own]
                        for row in range(rows)
                    ],
                    axis=0,
                )
                for a in range(ranks_a)
            ],
            axis=1,
        )

    def by_row(parts):
        return jnp.concatenate(
            [
                parts[a][row * own : (row + 1) * own]
                for row in range(rows)
                for a in range(ranks_a)
            ],
            axis=0,
        ).T

    half = by_rank(product(whole, north, (0, 0)))
    core = product(east, half, (0, 0))
    half = product(east, core, (1, 0))
    ranks_c = north.shape[1]
    split = [slice(a * ranks_c, (a + 1) * ranks_c) for a in range(ranks_a)]
    core = by_row([core[:, at] for at in split])
    whole = by_row([product(half[:, at], north, (1, 1)) for at in split])
    for row in range(rows):
        for column in range(columns):
            at = row * columns + column
            out[at, 0:tall] = core[column * tall : (column + 1) * tall, row * 128 : (row + 1) * 128]
            out[at, tall : tall + deep] = whole[
                column * deep : (column + 1) * deep, row * 128 : (row + 1) * 128
            ]


def expand_kernel(shape, ranks, tall, got, field, wide_rows, vertical, residual, core, full):
    wide, deep, species, up = shape
    ranks_a, ranks_d = ranks
    each = tall + deep
    component = where_equal(
        jnp.concatenate([wide_rows[...]] * wide, axis=0),
        lambda at: at // species,
        lambda at: at % wide,
    )
    for y in range(deep):
        on_d = got[pl.ds(tall + y, ranks_d, stride=each), :]
        on_a = product(on_d, vertical[...], (0, 0))
        full[y] = product(component, on_a, (1, 0))
    for x in range(wide):
        residual[:, x] = jnp.swapaxes(
            field[x] - full[:, x * species : (x + 1) * species, :], 0, 1
        )
    turned = [got[pl.ds(c, ranks_d, stride=each), :].T for c in range(tall)]
    core[...] = jnp.swapaxes(jnp.stack(turned), 0, 1)


def swapped(one, other, axes):
    got = []
    for first, face in enumerate((one, other)):
        couples = [(i, i + 1) for i in range(first, lax.axis_size(axes) - 1, 2)]
        got.append(lax.ppermute(face, axes, couples + [(b, a) for a, b in couples]))
    return got


def faces_beside(faces):
    x_one, x_other, y_one, y_other = faces
    y_one, y_other = swapped(y_one, y_other, COLUMN)
    x_one, x_other = swapped(x_one, x_other, ROW)
    return x_one, x_other, y_one, y_other


def whole_factors(tucker_factor_east, tucker_factor_north):
    rows, columns = lax.axis_size(ROW), lax.axis_size(COLUMN)

    def shares(factor, holders, axes):
        count = -(-factor.shape[0] // holders)
        padded = jnp.pad(factor, ((0, count * holders - factor.shape[0]), (0, 0)))
        return lax.dynamic_slice_in_dim(padded, lax.axis_index(axes) * count, count, 0)

    east = shares(tucker_factor_east, columns, COLUMN)
    north = shares(tucker_factor_north, rows, ROW)
    sent = jnp.concatenate([east.reshape(-1), north.reshape(-1)])
    sent = jnp.pad(sent, (0, -sent.size % 128)).reshape(1, -1, 128)
    sent = jnp.broadcast_to(sent, (rows * columns,) + sent.shape[1:])
    got = lax.all_to_all(sent, EVERY, 0, 0, tiled=True).reshape(rows, columns, -1)
    whole_east = got[:, :, : east.size].reshape(rows, -1, east.shape[1])
    whole_east = whole_east[:, : tucker_factor_east.shape[0]].reshape(-1, east.shape[1])
    whole_north = got[:, :, east.size : east.size + north.size]
    whole_north = whole_north.reshape(rows, columns, *north.shape).transpose(1, 0, 2, 3)
    whole_north = whole_north.reshape(columns, -1, north.shape[1])
    whole_north = whole_north[:, : tucker_factor_north.shape[0]].reshape(-1, north.shape[1])
    return whole_east, whole_north


def compress_and_expand(snapshot, east, north, vertical, component):
    rows, columns = lax.axis_size(ROW), lax.axis_size(COLUMN)
    devices = rows * columns
    (wide, deep, _, _), (_, ranks_a) = snapshot.shape, component.shape
    ranks_d = vertical.shape[1]
    ranks_b, ranks_c = east.shape[1], north.shape[1]
    projected = jnp.einsum("xysz,sa->xyaz", snapshot, component, precision=HIGHEST)
    projected = jnp.einsum("xyaz,zd->dyxa", projected, vertical, precision=HIGHEST)
    pairs = ranks_a * ranks_d
    share = -(-pairs // devices)
    flat = jnp.transpose(projected, (0, 3, 1, 2)).reshape(pairs, deep, wide)
    flat = jnp.pad(flat, ((0, share * devices - pairs), (0, 0), (0, 0)))
    flat = flat.reshape(devices, share, deep, wide).transpose(0, 2, 3, 1)
    flat = lax.all_to_all(
        flat.reshape(devices, deep, wide * share), EVERY, 0, 0, tiled=True
    )
    whole = flat.reshape(rows, columns * deep, wide, share)
    part = jnp.einsum("gyxp,yc->cgxp", whole, north, precision=HIGHEST)
    part = part.reshape(ranks_c, rows * wide, share)
    core = jnp.einsum("cxp,xb->cbp", part, east, precision=HIGHEST)
    part = jnp.einsum("cbp,xb->cxp", core, east, precision=HIGHEST)
    whole = jnp.einsum("cxp,yc->yxp", part, north, precision=HIGHEST)
    own_b, own_c = ranks_b // rows, ranks_c // columns

    def pieces(array, tall, broad):
        array = array.reshape(columns, tall, rows, broad, share)
        return array.transpose(2, 0, 1, 3, 4).reshape(devices, tall * broad * share)

    sent = jnp.concatenate([pieces(core, own_c, own_b), pieces(whole, deep, wide)], axis=1)
    sent = jnp.pad(sent, ((0, 0), (0, -sent.shape[1] % 1024)))
    got = lax.all_to_all(
        sent.reshape(devices, -1, 128), EVERY, 0, 0, tiled=True
    ).reshape(devices, -1)

    def ranks_together(array, tall, broad):
        array = array.reshape(devices, tall, broad, share).transpose(0, 3, 2, 1)
        array = array.reshape(devices * share, broad, tall)[:pairs]
        return array.reshape(ranks_d, ranks_a, broad, tall)

    core_size = own_c * own_b * share
    core = ranks_together(got[:, :core_size], own_c, own_b).transpose(1, 2, 3, 0)
    expanded = ranks_together(got[:, core_size : core_size + deep * wide * share], deep, wide)
    expanded = jnp.einsum("daxy,zd->axyz", expanded, vertical, precision=HIGHEST)
    expanded = jnp.einsum("axyz,sa->sxyz", expanded, component, precision=HIGHEST)
    return core, snapshot.transpose(2, 0, 1, 3) - expanded


def body(
    mixture_fields_initial,
    flow_speed_vector,
    thermal_field,
    mass_diffusivity,
    arrhenius_constant,
    arrhenius_energy_temp,
    production_coefficients,
    tucker_factor_east,
    tucker_factor_north,
    tucker_factor_vertical,
    tucker_factor_component,
):
    species, wide, deep, up = mixture_fields_initial.shape
    shape = (wide, deep, species, up)
    cells = wide * deep * species * up
    rows, columns = lax.axis_size(ROW), lax.axis_size(COLUMN)
    devices = rows * columns
    ranks_a, ranks_d = tucker_factor_component.shape[1], tucker_factor_vertical.shape[1]
    ranks_b, ranks_c = tucker_factor_east.shape[1], tucker_factor_north.shape[1]
    own_b, own_c = ranks_b // rows, ranks_c // columns
    kernels_fit = (
        ranks_d == devices
        and wide * ranks_a == 128
        and own_b * ranks_a == 128
        and deep == own_c == 8
        and ranks_b == ranks_c == 64
        and wide == 2 * columns
        and deep == 2 * rows
    )

    row, column = lax.axis_index(ROW), lax.axis_index(COLUMN)
    own = jnp.stack([1 - row % 2, 1 - column % 2, row, column]).astype(jnp.int32)
    face_shapes = [(deep, species, up)] * 2 + [(wide, species, up)] * 2
    faces = vmem_call(
        functools.partial(faces_kernel, shape), face_shapes, 1, 2,
        scratch=[mixture_fields_initial.shape], placed=[1], copies=FACE_COPIES,
    )(own, pltpu.with_memory_space_constraint(mixture_fields_initial, pltpu.HBM))
    faces = faces_beside(faces)
    def with_fetches(kernel, given, small, outs, **cost):
        call = vmem_call(
            kernel, outs, int(given is own), 1 + len(small),
            scratch=[array.shape for array in small], placed=range(1, 1 + len(small)),
            copies=len(small), **cost,
        )
        return call(
            given, *(pltpu.with_memory_space_constraint(array, pltpu.HBM) for array in small)
        )

    field, rates, speeds, coefficients, mix = with_fetches(
        functools.partial(prepare_kernel, shape),
        mixture_fields_initial,
        (
            flow_speed_vector, thermal_field, mass_diffusivity[None], arrhenius_constant[None],
            arrhenius_energy_temp[None], production_coefficients,
        ),
        [shape, shape, (4, wide, deep, up), (3, species, up), (species, 128)],
        flops=4 * cells, moved=12 * cells, exps=cells,
    )
    block, last_block = (
        vmem_call(
            functools.partial(block_kernel, shape, held), [shape], 0, 4 + held,
            flops=60 * cells, moved=8 * cells,
        )
        for held in (1, 0)
    )
    advance = vmem_call(
        functools.partial(advance_kernel, shape), [shape] + face_shapes, 1, 8,
        flops=4 * cells, moved=8 * cells,
    )
    fixed = (rates, speeds, coefficients, mix)
    for substep in range(SUB - 1):
        field, *faces = advance(
            own, *block(field, *fixed), *faces, speeds, coefficients
        )
        first = field
        faces = faces_beside(faces)
    high = 2 * species + 4
    snapshot, *y_faces = vmem_call(
        functools.partial(snapshot_kernel, shape), [shape] + [(wide * high, up)] * 2, 1, 8,
        flops=4 * cells, moved=8 * cells,
    )(own, *block(field, *fixed), *faces, speeds, coefficients)
    y_faces = swapped(*y_faces, COLUMN)
    if kernels_fit:
        own, _ = lax.optimization_barrier((own, first))
        squeeze, wide_rows, upright, *factor_rows = with_fetches(
            functools.partial(matrices_kernel, shape),
            own,
            (
                tucker_factor_component.T, tucker_factor_vertical.T, tucker_factor_east,
                tucker_factor_north,
            ),
            [
                (wide * ranks_a, wide * species), (species, wide * ranks_a), (ranks_d, up),
                (2, 128),
            ],
        )
        (sent,) = vmem_call(
            functools.partial(project_kernel, shape, (ranks_a, ranks_d)),
            [(devices * (deep + 2), 128)], 0, 4, flops=60 * cells, moved=4 * cells,
        )(snapshot, squeeze, upright, *factor_rows)
        got = lax.all_to_all(
            sent.reshape(devices, (deep + 2) // 2, 2, 128), EVERY, 0, 0, tiled=True
        )
        (sent,) = vmem_call(
            functools.partial(core_kernel, (rows, columns, ranks_a, own_c, deep)),
            [(devices, own_c + deep, 128)], 0, 1, flops=60 * cells, moved=4 * cells,
        )(got.reshape(devices * (deep + 2), 128))
        sent, later = lax.optimization_barrier((sent, snapshot))
        got = lax.all_to_all(sent, EVERY, 0, 0, tiled=True)
        residual, tucker_core = vmem_call(
            functools.partial(expand_kernel, shape, (ranks_a, ranks_d), own_c),
            [mixture_fields_initial.shape, (ranks_a * own_b, own_c, ranks_d)], 0, 4,
            flops=60 * cells, moved=8 * cells,
            scratch=[(deep, wide * species, up)],
        )(
            got.reshape(devices * (own_c + deep), 128),
            snapshot,
            wide_rows,
            upright,
        )
        tucker_core = tucker_core.reshape(ranks_a, own_b, own_c, ranks_d)
    else:
        east, north = whole_factors(tucker_factor_east, tucker_factor_north)
        tucker_core, residual = compress_and_expand(
            snapshot, east, north, tucker_factor_vertical, tucker_factor_component
        )
        later = snapshot
    fixed = fixed[1:]
    (third,) = last_block(later, *fixed)
    x_faces = vmem_call(
        functools.partial(wide_faces_kernel, shape),
        [((deep + 1) * high - 4 + spare, up) for spare in (SPARE_X, 0)], 1, 5,
        flops=cells, moved=cells,
    )(own, snapshot, *y_faces, speeds)
    x_faces = swapped(*x_faces, ROW)
    edges, ends, nearly, inmost = vmem_call(
        functools.partial(third_step_kernel, shape, (rows, columns)),
        [
            (4, deep + 2, species, up), (2, 2, 8, up), (2, deep, species, up),
            mixture_fields_initial.shape,
        ], 1, 8,
        flops=120 * cells, moved=16 * cells,
        scratch=[(wide, deep + 2, species, up), (species, wide - 4, deep, up)], placed=[11],
        copies=-(-(wide - 4) // 4),
    )(own, third, snapshot, *y_faces, *fixed)
    own, _ = lax.optimization_barrier((own, tucker_core))
    (mixture_fields_final,) = vmem_call(
        functools.partial(fourth_step_kernel, shape, (rows, columns)),
        [mixture_fields_initial.shape], 1, 11,
        flops=60 * cells, moved=8 * cells,
        scratch=[(2, deep + 2, species, up), (2, deep, species, up), (species, 4, deep, up)],
        placed=[4, 11], copies=4, aliases={4: 0},
    )(own, edges, ends, nearly, inmost, snapshot, *x_faces, *fixed)
    return (mixture_fields_final, residual, tucker_core)


def solution(mesh):
    in_specs = (
        P(None, "gx", ("gy", "ga"), None),
        P(None, "gx", ("gy", "ga"), None),
        P("gx", ("gy", "ga"), None),
        P(),
        P(),
        P(),
        P(),
        P("gx", None),
        P(("gy", "ga"), None),
        P(),
        P(),
    )
    out_specs = (
        P(None, "gx", ("gy", "ga"), None),
        P(None, "gx", ("gy", "ga"), None),
        P(None, "gx", ("gy", "ga"), None),
    )
    return jax.shard_map(body, mesh=mesh, in_specs=in_specs, out_specs=out_specs, check_vma=False)
```
